128 devices in a mesh: grp: 8 (over x, z_hi), unit: 16 (over z_lo, y, core).
Axes of the slice: x: 4, y: 4, z: 4 (z_hi: 2, z_lo: 2; z = z_hi * 2 + z_lo), core: 2. Of those that a mesh axis runs over, the one named last changes fastest.
Arguments:
- x_fp: bfloat16 [768, 4096], P(('grp', 'unit')), may hold values from -6 to 6
- x_q: bfloat16 [768, 4096], P(('grp', 'unit')), may hold values from -6 to 6
- expert_ids: int32 [768, 8], P(('grp', 'unit')), may hold values from 0 to 15, all different within a row; in each aligned block of 6 rows (0 to 5, 6 to 11, ...) at most 4 rows name the same one
- route_weight: float32 [768, 8], P(('grp', 'unit')), may hold values from 0.05 to 0.4
- gate_weight: bfloat16 [16, 1536, 4096], P('grp', 'unit'), may hold values from -0.09375 to 0.09375
- up_weight: bfloat16 [16, 1536, 4096], P('grp', 'unit'), may hold values from -0.09375 to 0.09375
- down_weight: bfloat16 [16, 1536, 4096], P('grp', 'unit'), may hold values from -0.15625 to 0.15625
- gate_clip: float32 [2, 16, 1536], P(None, 'grp', 'unit'), may hold values from 0 to 4
- up_clip: float32 [2, 16, 1536], P(None, 'grp', 'unit'), may hold values from 0 to 4
- down_clip: float32 [2, 16, 4096], P(None, 'grp'), may hold values from 0 to 4
Outputs:
- gate_clip_grad: float32 [2, 16, 1536], P(None, 'grp', 'unit')
- up_clip_grad: float32 [2, 16, 1536], P(None, 'grp', 'unit')
- down_clip_grad: float32 [2, 16, 4096], P(None, 'grp', 'unit')
The draws below stay inside these ranges and needn't reach their ends.
Inputs may be any that keep to these rules, and one draw needn't show every extreme that they name: `expert_ids`: in each aligned block of 6 rows (the tokens of one device) no expert is named by more than 4 rows; a row names 8 different experts.
All inputs are finite; a program needn't handle non-finite values.
Results may differ from the reference program's by a relative error of at most 0.03.
Values may be sent and summed in bfloat16 or wider, within the bound.
A program may use at most 128 MiB of HBM per device.

```python
import math
import jax
import jax.numpy as jnp
import numpy as np
from jax import lax

D = 4096
FF = 1536
TOP = 8
TOK_DEV = 6
EXPERTS = 16
TOKENS = 768
CAP = 4
N_GRP = 8
N_UNIT = 16


def block_scale(stream_key, dims, split, smallest, largest):
    factor_of, own = 1.0, jax.random.fold_in(stream_key, 6)
    for position, shards_of in split:
        heights = jnp.exp(jax.random.uniform(jax.random.fold_in(own, position), (shards_of,), jnp.float32, smallest / len(split), largest / len(split)))
        factor_of = factor_of * jnp.repeat(heights, dims[position] // shards_of).reshape([-1 if axis == position else 1 for axis in range(len(dims))])
    return factor_of


def deal_out(rng, own, number, rows, amount, top, limit, slope):
    order = jax.random.permutation(rng, amount)
    heavy_load, common = portions_of(amount, rows * top, limit, slope, True), portions_of(amount, rows * top, limit, slope, False)
    places = jnp.arange(amount)

    def named(tallies, offset_by):
        used = int((tallies > 0).sum())
        fixed = max(1, used // 4)
        passed = fixed + (places - fixed + offset_by * (used - fixed)) % max(1, amount - fixed)
        return jnp.zeros((amount,), jnp.int32).at[order[jnp.where(places < fixed, places, passed)]].set(jnp.asarray(tallies, jnp.int32))

    tallies = jnp.where(number % 4 == 0, named(heavy_load, number // 4), named(common, number - number // 4 - 1))
    mixed = jax.random.permutation(jax.random.fold_in(own, 3), amount)
    source_of, taker = mixed[0:amount // 2 * 2:2], mixed[1:amount // 2 * 2:2]
    slack = jnp.minimum(tallies[source_of] - 1, limit - tallies[taker]) // 2
    slack = jnp.where((source_of == order[0]) | (taker == order[0]) | (tallies[taker] == 0), 0, jnp.maximum(slack, 0))
    passed = jax.random.randint(jax.random.fold_in(own, 4), (amount // 2,), 0, 1 << 20) % (slack + 1)
    tallies = tallies.at[source_of].add(-passed).at[taker].add(passed)
    items = jnp.searchsorted(jnp.cumsum(tallies), jnp.arange(rows * top), side="right").astype(jnp.int32)
    table = items.reshape(top, rows).T
    table = table[jax.random.permutation(jax.random.fold_in(own, 1), rows)]
    offset_by = jax.random.randint(jax.random.fold_in(own, 2), (rows, 1), 0, top)
    return jnp.take_along_axis(table, (jnp.arange(top)[None, :] + offset_by) % top, axis=1)


def portions_of(amount, total, reach, slope, full):
    weights = [(1 << 20) // math.isqrt(standing ** slope) + 1 for standing in range(1, amount + 1)]
    largest = reach if full else min(reach, max(-(-total // amount), total * weights[0] // sum(weights)))
    least = 1 if total - largest >= amount - 1 else 0
    given, spare = [largest] + [least] * (amount - 1), total - largest - least * (amount - 1)
    while spare > 0:
        free = [i for i in range(1, amount) if given[i] < largest] or [i for i in range(1, amount) if given[i] < reach]
        whole, budget = sum([weights[i] for i in free]), spare
        for i in free:
            addition = min(reach - given[i], max(1, budget * weights[i] // whole), spare)
            given[i] = given[i] + addition
            spare = spare - addition
    return np.array(given)


def noise(stream_key, extent, deviation, limit, shards=(), kind=jnp.bfloat16):
    array = deviation * jax.random.normal(stream_key, extent, jnp.float32)
    if shards:
        array = array * block_scale(stream_key, extent, shards, -0.22, 0.18)
    return jnp.clip(array, -limit, limit).astype(kind)


def setup_inputs(seed: int = 0) -> dict:
    splits = jax.random.split(jax.random.key(seed), 11)
    x_fp = noise(splits[0], (TOKENS, D), 1.0, 6.0, ((0, 128),))
    x_q = noise(splits[1], (TOKENS, D), 1.0, 6.0, ((0, 128),))
    expert_ids_keys = jax.random.split(jax.random.fold_in(splits[2], 1), TOKENS // TOK_DEV)
    expert_ids_turns = jax.random.permutation(jax.random.fold_in(splits[2], 3), TOKENS // TOK_DEV)
    expert_ids = jax.vmap(lambda own, number: deal_out(jax.random.fold_in(splits[2], 2), own, number, TOK_DEV, EXPERTS, TOP, CAP, 2))(expert_ids_keys, expert_ids_turns).reshape((TOKENS, TOP))
    route_weight = jnp.clip(0.05 + 0.35 * jax.random.uniform(splits[3], (TOKENS, TOP), jnp.float32) ** block_scale(splits[3], (TOKENS, TOP), ((0, 128),), -0.2, 0.2), 0.05, 0.4)
    gate_weight = noise(splits[4], (EXPERTS, FF, D), D ** -0.5, 0.09375, ((0, 8), (1, 16)))
    up_weight = noise(splits[5], (EXPERTS, FF, D), D ** -0.5, 0.09375, ((0, 8), (1, 16)))
    down_weight = noise(splits[6], (EXPERTS, FF, D), FF ** -0.5, 0.15625, ((0, 8), (1, 16)))
    gate_clip = jnp.clip(4.0 * jax.random.uniform(splits[7], (2, EXPERTS, FF), jnp.float32) ** block_scale(splits[7], (2, EXPERTS, FF), ((1, 8), (2, 16)), -0.2, 0.2), 0.0, 4.0)
    up_clip = jnp.clip(4.0 * jax.random.uniform(splits[8], (2, EXPERTS, FF), jnp.float32) ** block_scale(splits[8], (2, EXPERTS, FF), ((1, 8), (2, 16)), -0.2, 0.2), 0.0, 4.0)
    down_clip = jnp.clip(4.0 * jax.random.uniform(splits[9], (2, EXPERTS, D), jnp.float32) ** block_scale(splits[9], (2, EXPERTS, D), ((1, 8),), -0.2, 0.2), 0.0, 4.0)
    return dict(x_fp=x_fp, x_q=x_q, expert_ids=expert_ids, route_weight=route_weight, gate_weight=gate_weight, up_weight=up_weight, down_weight=down_weight, gate_clip=gate_clip, up_clip=up_clip, down_clip=down_clip)


def ste_floor(value):
    return value + lax.stop_gradient(jnp.floor(value + 0.5) - value)

def fake_quant(weight_f, upper, lower, col_max, col_min):
    high_end = jax.nn.sigmoid(upper) * col_max
    low_end = jax.nn.sigmoid(lower) * col_min
    step_size = (high_end - low_end) / 15.0
    zero_point = ste_floor(-low_end / step_size)
    levels = jnp.clip(ste_floor(weight_f / step_size) + zero_point, 0.0, 15.0)
    return (levels - zero_point) * step_size

def reference(x_fp, x_q, expert_ids, route_weight, gate_weight, up_weight, down_weight, gate_clip, up_clip, down_clip):
    devices = N_GRP * N_UNIT
    rows_per = devices * CAP
    ff_block = FF // N_UNIT
    flat_ids = expert_ids.reshape(devices, TOK_DEV * TOP)
    flat_w = route_weight.reshape(devices, TOK_DEV * TOP)
    onehot = (flat_ids[:, :, None] == jnp.arange(EXPERTS, dtype=jnp.int32)[None, None, :]).astype(jnp.int32)
    slot_pos = lax.optimization_barrier(jnp.sum(jnp.cumsum(onehot, axis=1) * onehot, axis=2)) - 1
    slot_range = jnp.arange(CAP, dtype=jnp.int32)
    fp_dev = x_fp.astype(jnp.float32).reshape(devices, TOK_DEV, D)
    q_dev = x_q.astype(jnp.float32).reshape(devices, TOK_DEV, D)
    hp = lax.Precision.HIGHEST

    def matched(expert):
        hit = (flat_ids == expert)[:, None, :] & (slot_pos[:, None, :] == slot_range[None, :, None])
        return hit.astype(jnp.float32)

    def quant_all(params):
        gate_w, up_w, down_w, gate_c, up_c, down_c = params
        gate_f = gate_w.astype(jnp.float32).T
        up_f = up_w.astype(jnp.float32).T
        down_f = down_w.astype(jnp.float32)
        gate_fn = lambda upper, lower: fake_quant(gate_f, upper[None, :], lower[None, :], lax.optimization_barrier(jnp.max(gate_f, axis=0, keepdims=True)), lax.optimization_barrier(jnp.min(gate_f, axis=0, keepdims=True)))
        up_fn = lambda upper, lower: fake_quant(up_f, upper[None, :], lower[None, :], lax.optimization_barrier(jnp.max(up_f, axis=0, keepdims=True)), lax.optimization_barrier(jnp.min(up_f, axis=0, keepdims=True)))
        down_fn = lambda upper, lower: fake_quant(down_f, upper[None, :], lower[None, :], lax.optimization_barrier(jnp.max(down_f, axis=0, keepdims=True)), lax.optimization_barrier(jnp.min(down_f, axis=0, keepdims=True)))
        gate_q, gate_back = jax.vjp(gate_fn, gate_c[0], gate_c[1])
        up_q, up_back = jax.vjp(up_fn, up_c[0], up_c[1])
        down_q, down_back = jax.vjp(down_fn, down_c[0], down_c[1])
        return (gate_q.astype(jnp.bfloat16), up_q.astype(jnp.bfloat16), down_q.astype(jnp.bfloat16), gate_back, up_back, down_back)

    def forward(args):
        expert, gate_w, up_w, down_w, gate_c, up_c, down_c = args
        pick_rows = lax.optimization_barrier(jnp.sum(matched(expert).reshape(devices, CAP, TOK_DEV, TOP), axis=3))
        teacher_rows = jnp.einsum('dct,dtx->dcx', pick_rows, fp_dev, precision=hp).reshape(rows_per, D).astype(jnp.bfloat16)
        student_rows = jnp.einsum('dct,dtx->dcx', pick_rows, q_dev, precision=hp).reshape(rows_per, D).astype(jnp.bfloat16)
        gate_q, up_q, down_q, _, _, _ = quant_all((gate_w, up_w, down_w, gate_c, up_c, down_c))
        teacher_gate = jnp.dot(teacher_rows, gate_w.T, preferred_element_type=jnp.float32)
        teacher_up = jnp.dot(teacher_rows, up_w.T, preferred_element_type=jnp.float32)
        teacher_hidden = (jax.nn.silu(teacher_gate) * teacher_up).astype(jnp.bfloat16)
        student_gate = jnp.dot(student_rows, gate_q, preferred_element_type=jnp.float32)
        student_up = jnp.dot(student_rows, up_q, preferred_element_type=jnp.float32)
        student_hidden = (jax.nn.silu(student_gate) * student_up).astype(jnp.bfloat16)
        teacher_blocks = teacher_hidden.reshape(rows_per, N_UNIT, ff_block).transpose(1, 0, 2)
        student_blocks = student_hidden.reshape(rows_per, N_UNIT, ff_block).transpose(1, 0, 2)
        down_blocks = down_w.reshape(N_UNIT, ff_block, D)
        quant_blocks = down_q.reshape(N_UNIT, ff_block, D)

        def add_block(total, piece):
            teacher_b, student_b, down_b, quant_b = piece
            part = jnp.dot(student_b, quant_b, preferred_element_type=jnp.float32) - jnp.dot(teacher_b, down_b, preferred_element_type=jnp.float32)
            rounded = lax.optimization_barrier(part.astype(jnp.bfloat16)).astype(jnp.float32)
            return (total + rounded, None)
        total, _ = lax.scan(add_block, jnp.zeros((rows_per, D), jnp.float32), (teacher_blocks, student_blocks, down_blocks, quant_blocks))
        return (total.astype(jnp.bfloat16), student_gate, student_up, student_hidden, student_rows)
    expert_range = jnp.arange(EXPERTS, dtype=jnp.int32)
    gate_cs = gate_clip.transpose(1, 0, 2)
    up_cs = up_clip.transpose(1, 0, 2)
    down_cs = down_clip.transpose(1, 0, 2)
    slot_diff, student_gate, student_up, student_hidden, student_rows = lax.map(forward, (expert_range, gate_weight, up_weight, down_weight, gate_cs, up_cs, down_cs))
    row_index = flat_ids * rows_per + jnp.arange(devices, dtype=jnp.int32)[:, None] * CAP + slot_pos
    gathered = slot_diff.reshape(EXPERTS * rows_per, D)[row_index.reshape(-1)].astype(jnp.float32)
    gathered = gathered.reshape(devices, TOK_DEV, TOP, D) * flat_w.reshape(devices, TOK_DEV, TOP)[:, :, :, None]
    token_diff = lax.optimization_barrier(jnp.sum(gathered, axis=2))
    token_cot = token_diff.astype(jnp.bfloat16)
    cot_f = token_cot.astype(jnp.float32)

    def backward(args):
        expert, gate_w, up_w, down_w, gate_c, up_c, down_c, s_gate, s_up, s_hidden, s_rows = args
        weighted = lax.optimization_barrier(jnp.sum((matched(expert) * flat_w[:, None, :]).reshape(devices, CAP, TOK_DEV, TOP), axis=3))
        slot_cot = jnp.einsum('dct,dtx->dcx', weighted, cot_f, precision=hp).reshape(rows_per, D).astype(jnp.bfloat16)
        gate_q, up_q, down_q, gate_back, up_back, down_back = quant_all((gate_w, up_w, down_w, gate_c, up_c, down_c))
        d_hidden = jnp.dot(slot_cot, down_q.T, preferred_element_type=jnp.float32)
        gate_sig = jax.nn.sigmoid(s_gate)
        d_gate = (d_hidden * s_up * gate_sig * (1.0 + s_gate * (1.0 - gate_sig))).astype(jnp.bfloat16)
        d_up = (d_hidden * s_gate * gate_sig).astype(jnp.bfloat16)
        dq_gate = jnp.dot(s_rows.T, d_gate, preferred_element_type=jnp.float32)
        dq_up = jnp.dot(s_rows.T, d_up, preferred_element_type=jnp.float32)
        dq_down = jnp.dot(s_hidden.T, slot_cot, preferred_element_type=jnp.float32)
        return (jnp.stack(gate_back(dq_gate)), jnp.stack(up_back(dq_up)), jnp.stack(down_back(dq_down)))
    gate_grad, up_grad, down_grad = lax.map(backward, (expert_range, gate_weight, up_weight, down_weight, gate_cs, up_cs, down_cs, student_gate, student_up, student_hidden, student_rows))
    return (gate_grad.transpose(1, 0, 2), up_grad.transpose(1, 0, 2), down_grad.transpose(1, 0, 2))
```

```python
import jax
import jax.numpy as jnp
from jax import lax
from jax.experimental import pallas as pl
from jax.experimental.pallas import tpu as pltpu
from jax.sharding import PartitionSpec as P

MESH = pl.DeviceIdType.MESH
D = 4096
BF = jnp.bfloat16
F32 = jnp.float32
ORDERS = ("xyz", "yzx", "zxy")


def place():
    g, u = lax.axis_index("grp"), lax.axis_index("unit")
    x, z = lax.div(g, 2), lax.rem(g, 2) * 2 + lax.div(u, 8)
    y, c = lax.rem(lax.div(u, 2), 4), lax.rem(u, 2)
    return dict(x=x, y=y, z=z, c=c)


def device(at):
    return (at["x"] * 2 + lax.div(at["z"], 2), lax.rem(at["z"], 2) * 8 + at["y"] * 2 + at["c"])


def moved(at, **by):
    out = dict(at)
    for axis, step in by.items():
        out[axis] = lax.rem(at[axis] + step, 2 if axis == "c" else 4)
    return out


def remote(src, dst, send, recv, to):
    return pltpu.make_async_remote_copy(
        src_ref=src, dst_ref=dst, send_sem=send, recv_sem=recv, device_id=device(to), device_id_type=MESH)


def columns(y, c, full):
    if full:
        return pl.ds(pl.multiple_of(c * 2048, 2048), 2048)
    return pl.ds(pl.multiple_of(c * 2048 + y * 512, 512), 512)


def slab(at, part, phase, pos, half, mats):
    order = ORDERS[part]
    done, axis = order[:phase], order[phase]
    where = dict(at)
    where[axis] = pos
    rows = [slice(None) if a in done else pl.ds(where[a], 1) for a in "zx"]
    full = "y" in done
    width = 2048 if full else 512
    base = where["c"] * 2048 + (0 if full else where["y"] * 512)
    if mats == 2:
        lead = pl.ds(half, 1) if half is not None else slice(None)
    else:
        lead = slice(None)
        if half is not None:
            width = width // 2
            base = base + half * width
    cols = pl.ds(pl.multiple_of(base, width), width)
    return (lead, pl.ds(part, 1), rows[0], rows[1], slice(None), cols)


def gather(at, buf, send, recv, mats, between=None):
    partner = moved(at, c=1)
    sends, lands = [], []

    def push(idx, sems, to):
        cp = remote(buf.at[idx], buf.at[idx], send.at[sems], recv.at[sems], to)
        cp.start()
        sends.append(cp)

    def landed(idx, sems, at_from):
        remote(buf.at[idx], buf.at[idx], send.at[sems], recv.at[sems], at_from).wait_recv()

    def to_partner(idx, sems):
        push(idx, sems, partner)
        lands.append((idx, sems))

    def mirrored(idx, base_c):
        return idx

    for part in range(3):
        idx = slab(at, part, 0, at[ORDERS[part][0]], None, mats)
        push(idx, (part, 0, 8), partner)
        lands.append(((part, 0, at[ORDERS[part][0]], None), (part, 0, 8)))
    for phase in range(3):
        for part in range(3):
            axis = ORDERS[part][phase]
            idx = slab(at, part, phase, at[axis], None, mats)
            push(idx, (part, phase, 0), moved(at, **{axis: 1}))
            push(idx, (part, phase, 1), moved(at, **{axis: 3}))
        if between is not None:
            between(phase)
        for part in range(3):
            axis = ORDERS[part][phase]
            for side, step in ((0, 1), (1, 3)):
                origin = lax.rem(at[axis] + 4 - step, 4)
                idx = slab(at, part, phase, origin, None, mats)
                landed(idx, (part, phase, side), moved(at, **{axis: 4 - step}))
                half = slab(at, part, phase, origin, side, mats)
                push(half, (part, phase, 2 + side), moved(at, **{axis: step}))
                push(idx, (part, phase, 4 + side), partner)
                lands.append(((part, phase, origin, None), (part, phase, 4 + side)))
        for part in range(3):
            axis = ORDERS[part][phase]
            origin = lax.rem(at[axis] + 2, 4)
            for side, step in ((0, 1), (1, 3)):
                idx = slab(at, part, phase, origin, side, mats)
                landed(idx, (part, phase, 2 + side), moved(at, **{axis: 4 - step}))
                push(idx, (part, phase, 6 + side), partner)
                lands.append(((part, phase, origin, side), (part, phase, 6 + side)))
    for (part, phase, pos, half), sems in lands:
        landed(slab(partner, part, phase, pos, half, mats), sems, partner)
    for cp in sends:
        cp.wait_send()


def peer(at, n):
    u = lax.rem(lax.rem(at["z"], 2) * 8 + at["y"] * 2 + at["c"] + n, 16)
    return dict(x=at["x"], z=lax.div(at["z"], 2) * 2 + lax.div(u, 8), y=lax.rem(lax.div(u, 2), 4), c=lax.rem(u, 2)), u


def friends(at):
    out = [peer(at, n)[0] for n in range(1, 16)] + [moved(at, x=n) for n in (1, 2, 3)]
    low = lax.rem(at["z"], 2)
    return out + [dict(at, z=lax.rem(at["z"] - low + n, 4)) for n in (2, 3)]


def greet(at, others):
    barrier = pltpu.get_barrier_semaphore()
    for to in others:
        pl.semaphore_signal(barrier, inc=1, device_id=device(to), device_id_type=MESH)
    pl.semaphore_wait(barrier, len(others))


def pack_rows(xf_ref, xq_ref, ids_ref, route_ref, rows_f, packed):
    lane = lax.broadcasted_iota(jnp.int32, (6, 128), 1)
    base = lax.broadcasted_iota(jnp.int32, (6, 128), 0) * 16
    dense = jnp.zeros((6, 128), F32)
    for k in range(8):
        dense = dense + jnp.where(lane == base + ids_ref[:, k:k + 1], route_ref[:, k:k + 1], 0.0)
    weights = jnp.sum(dense, axis=0, keepdims=True)
    rest = weights - weights.astype(BF).astype(F32)
    rows_f[0:6, :] = xf_ref[...].astype(F32)
    rows_f[8:14, :] = xq_ref[...].astype(F32)
    for n in range(8):
        rows_f[6:7, 512 * n:512 * n + 128] = weights
        rows_f[7:8, 512 * n:512 * n + 128] = rest
    packed[...] = rows_f[...].astype(BF)


def turn_start(at, packed, stage, sem_a, sem_b):
    sends = []
    mine = at["c"] * 4 + at["y"]
    for n in range(1, 8):
        to = moved(at, y=n // 2, c=n % 2)
        cp = remote(packed.at[:, columns(to["y"], to["c"], False)], stage.at[mine], sem_a.at[n], sem_b.at[n], to)
        cp.start()
        sends.append(cp)
    stage[mine] = packed[:, columns(at["y"], at["c"], False)]
    return sends


def turn_end(at, stage, spread, xb, wb, sem_a, sem_b, sends):
    for n in range(1, 8):
        back = moved(at, y=(4 - n // 2) % 4, c=n % 2)
        slot = back["c"] * 4 + back["y"]
        remote(stage.at[slot], stage.at[slot], sem_a.at[n], sem_b.at[n], back).wait_recv()
    for cp in sends:
        cp.wait_send()
    for j in range(8):
        for q in range(4):
            spread[q * 128 + 16 * j:q * 128 + 16 * j + 16, :] = stage[j, :, 128 * q:128 * q + 128].astype(F32)
    cols = columns(at["y"], at["c"], False)
    for mat in range(2):
        for part in range(3):
            rows = [
                jnp.concatenate(
                    [spread[pl.ds(q * 128 + 8 * mat + 2 * part + r, 8, stride=16), :] for q in range(4)], axis=1)
                for r in range(2)
            ]
            xb[mat, part, at["z"], at["x"], :, cols] = jnp.concatenate(rows, axis=0).astype(BF)
    split = [spread[pl.ds(6 + r, 8, stride=16), :] for r in range(2)]
    wb[at["x"], at["z"]] = jnp.concatenate(split, axis=0).astype(BF)


def route_start(at, wb, axis, send, recv):
    sends = []
    for n in range(1, 4):
        to = moved(at, **{axis: n})
        idx = (at["x"], at["z"]) if axis == "z" else (at["x"],)
        cp = remote(wb.at[idx], wb.at[idx], send.at[n], recv.at[n], to)
        cp.start()
        sends.append(cp)
    return sends


def route_end(at, wb, axis, send, recv, sends):
    for n in range(1, 4):
        back = moved(at, **{axis: 4 - n})
        idx = (at["x"], back["z"]) if axis == "z" else (back["x"],)
        remote(wb.at[idx], wb.at[idx], send.at[n], recv.at[n], back).wait_recv()
    for cp in sends:
        cp.wait_send()


def unit_cols(u):
    return pl.ds(pl.multiple_of(u * 256, 256), 256)


def stats_local(down_ref, most):
    for e in range(2):
        w = down_ref[e].astype(F32)
        most[e:e + 1, :] = jnp.max(w, axis=0, keepdims=True)
        most[2 + e:3 + e, :] = -jnp.min(w, axis=0, keepdims=True)
    most[4:8, :] = jnp.zeros((4, D), F32)


def spread_start(at, src, dst, send, recv):
    sends = []
    for n in range(1, 16):
        to, u = peer(at, n)
        cp = remote(src.at[:, unit_cols(u)], dst.at[n], send.at[n], recv.at[n], to)
        cp.start()
        sends.append(cp)
    return sends


def spread_end(at, dst, send, recv, sends):
    for n in range(1, 16):
        back, _ = peer(at, 16 - n)
        remote(dst.at[n], dst.at[n], send.at[n], recv.at[n], back).wait_recv()
    for cp in sends:
        cp.wait_send()


def stats_share(at, most, fin, inbox, send, recv):
    _, me = peer(at, 0)
    top = most[:, unit_cols(me)]
    for n in range(1, 16):
        top = jnp.maximum(top, inbox[n])
    fin[:, unit_cols(me)] = top
    sends = []
    for n in range(1, 16):
        to, _ = peer(at, n)
        cp = remote(fin.at[:, unit_cols(me)], fin.at[:, unit_cols(me)], send.at[n], recv.at[n], to)
        cp.start()
        sends.append(cp)
    return sends


def stats_end(at, fin, send, recv, sends):
    for n in range(1, 16):
        back, u = peer(at, 16 - n)
        remote(fin.at[:, unit_cols(u)], fin.at[:, unit_cols(u)], send.at[n], recv.at[n], back).wait_recv()
    for cp in sends:
        cp.wait_send()


def kernel(xf_ref, xq_ref, ids_ref, route_ref, down_ref, xb, wb, most_out, packed, stage, rows_f, spread,
           most, inbox, t_s, t_r, z_s, z_r, x_s, x_r, m_s, m_r, n_s, n_r, send, recv):
    at = place()
    pack_rows(xf_ref, xq_ref, ids_ref, route_ref, rows_f, packed)
    greet(at, friends(at))
    turned = turn_start(at, packed, stage, t_s, t_r)
    stats_local(down_ref, most)
    m_sends = spread_start(at, most, inbox, m_s, m_r)
    turn_end(at, stage, spread, xb, wb, t_s, t_r, turned)
    z_sends = route_start(at, wb, "z", z_s, z_r)
    held = {}

    def between(phase):
        if phase == 0:
            spread_end(at, inbox, m_s, m_r, m_sends)
            held["n"] = stats_share(at, most, most_out, inbox, n_s, n_r)
            route_end(at, wb, "z", z_s, z_r, z_sends)
            held["x"] = route_start(at, wb, "x", x_s, x_r)
        if phase == 1:
            stats_end(at, most_out, n_s, n_r, held["n"])
            route_end(at, wb, "x", x_s, x_r, held["x"])

    gather(at, xb, send, recv, 2, between)


SEM = pltpu.SemaphoreType.DMA
VM = pl.BlockSpec(memory_space=pltpu.VMEM)


def gather_x(x_fp, x_q, expert_ids, route_weight, down_weight):
    return pl.pallas_call(
        kernel,
        out_shape=(
            jax.ShapeDtypeStruct((2, 3, 4, 4, 16, D), BF),
            jax.ShapeDtypeStruct((4, 4, 16, 128), BF),
            jax.ShapeDtypeStruct((8, D), F32),
        ),
        in_specs=[VM] * 5,
        out_specs=(VM, VM, VM),
        scratch_shapes=[
            pltpu.VMEM((16, D), BF),
            pltpu.VMEM((8, 16, 512), BF),
            pltpu.VMEM((16, D), F32),
            pltpu.VMEM((512, 128), F32),
            pltpu.VMEM((8, D), F32),
            pltpu.VMEM((16, 8, 256), F32),
            SEM((8,)), SEM((8,)), SEM((4,)), SEM((4,)), SEM((4,)), SEM((4,)),
            SEM((16,)), SEM((16,)), SEM((16,)), SEM((16,)),
            SEM((3, 3, 9)), SEM((3, 3, 9)),
        ],
        compiler_params=pltpu.CompilerParams(collective_id=0, has_side_effects=True, vmem_limit_bytes=60 << 20),
    )(x_fp, x_q, expert_ids, route_weight, down_weight)


def reduce_shapes():
    out = {}
    for phase in (2, 1, 0):
        for part in range(3):
            done = ORDERS[part][:phase]
            out[phase, part] = (4 if "z" in done else 1, 4 if "x" in done else 1, 2048 if "y" in done else 512)
    return out


def local_slab(at, part, phase, pos, half):
    order = ORDERS[part]
    done, axis = order[:phase], order[phase]
    where = dict(at)
    where[axis] = pos
    rows = [slice(None) if a in done else pl.ds(where[a], 1) for a in "zx"]
    full = "y" in done
    width = 2048 if full else 512
    base = 0 if full else where["y"] * 512
    if half is not None:
        width = width // 2
        base = base + half * width
    return (part, rows[0], rows[1], slice(None), pl.ds(pl.multiple_of(base, width), width))


def add(dst, dst_idx, *others):
    total = dst[dst_idx].astype(F32)
    for ref, idx in others:
        total = total + ref[idx].astype(F32)
    dst[dst_idx] = total.astype(BF)


def reduce_scatter(at, acc, halves, fulls, send, recv):
    sends = []

    def push(src, dst, sems, to):
        cp = remote(src, dst, send.at[sems], recv.at[sems], to)
        cp.start()
        sends.append(cp)

    def landed(dst, sems, at_from):
        remote(dst, dst, send.at[sems], recv.at[sems], at_from).wait_recv()

    for phase in (2, 1, 0):
        for part in range(3):
            axis = ORDERS[part][phase]
            width = reduce_shapes()[phase, part][2] // 2
            opposite = lax.rem(at[axis] + 2, 4)
            hb = halves[phase][part]
            fb = fulls[phase][part]
            for side, step in ((0, 1), (1, 3)):
                to = moved(at, **{axis: step})
                push(acc.at[local_slab(at, part, phase, opposite, side)], hb.at[side], (part, phase, side), to)
                near = lax.rem(at[axis] + step, 4)
                other = 1 - side
                push(acc.at[local_slab(at, part, phase, near, other)],
                     fb.at[side, :, :, :, pl.ds(other * width, width)], (part, phase, 2 + side), to)
        for part in range(3):
            axis = ORDERS[part][phase]
            width = reduce_shapes()[phase, part][2] // 2
            hb = halves[phase][part]
            fb = fulls[phase][part]
            for side, step in ((0, 1), (1, 3)):
                back = moved(at, **{axis: 4 - step})
                to = moved(at, **{axis: step})
                landed(hb.at[side], (part, phase, side), back)
                near = lax.rem(at[axis] + step, 4)
                idx = local_slab(at, part, phase, near, side)
                add(acc, idx, (hb, side))
                push(acc.at[idx], fb.at[side, :, :, :, pl.ds(side * width, width)], (part, phase, 4 + side), to)
        for part in range(3):
            axis = ORDERS[part][phase]
            width = reduce_shapes()[phase, part][2] // 2
            fb = fulls[phase][part]
            for side, step in ((0, 1), (1, 3)):
                back = moved(at, **{axis: 4 - step})
                other = 1 - side
                landed(fb.at[side, :, :, :, pl.ds(other * width, width)], (part, phase, 2 + side), back)
                landed(fb.at[side, :, :, :, pl.ds(side * width, width)], (part, phase, 4 + side), back)
            add(acc, local_slab(at, part, phase, at[axis], None), (fb, 0), (fb, 1))
    for cp in sends:
        cp.wait_send()


def ar_kernel(diff, cot, acc, theirs, *rest):
    halves = {ph: rest[3 * n:3 * n + 3] for n, ph in enumerate((2, 1, 0))}
    fulls = {ph: rest[9 + 3 * n:12 + 3 * n] for n, ph in enumerate((2, 1, 0))}
    swap_s, swap_r, rs_s, rs_r, ag_s, ag_r = rest[18:]
    at = place()
    partner = moved(at, c=1)
    others = [partner] + [moved(at, **{a: s}) for a in "xyz" for s in (1, 3)]
    greet(at, others)
    mine = pl.ds(pl.multiple_of(at["c"] * 2048, 2048), 2048)
    yours = pl.ds(pl.multiple_of(partner["c"] * 2048, 2048), 2048)
    cps = []
    for part in range(3):
        cp = remote(diff.at[part, :, :, :, yours], theirs.at[part], swap_s.at[part], swap_r.at[part], partner)
        cp.start()
        cps.append(cp)
    for part in range(3):
        cps[part].wait_recv()

        def rows(n, carry):
            acc[part, n] = (diff[part, n, :, :, mine].astype(F32) + theirs[part, n].astype(F32)).astype(BF)
            return carry
        lax.fori_loop(0, 4, rows, 0)
    reduce_scatter(at, acc, halves, fulls, rs_s, rs_r)
    for part in range(3):
        block = acc[part, at["z"], at["x"], :, pl.ds(pl.multiple_of(at["y"] * 512, 512), 512)]
        cot[0, part, at["z"], at["x"], :, columns(at["y"], at["c"], False)] = block
    gather(at, cot, ag_s, ag_r, 1)
    for cp in cps:
        cp.wait_send()


def all_reduce(diff):
    shapes = reduce_shapes()
    bufs = [pltpu.VMEM((2, shapes[ph, p][0], shapes[ph, p][1], 16, shapes[ph, p][2] // 2), BF) for ph in (2, 1, 0) for p in range(3)]
    bufs += [pltpu.VMEM((2, shapes[ph, p][0], shapes[ph, p][1], 16, shapes[ph, p][2]), BF) for ph in (2, 1, 0) for p in range(3)]
    return pl.pallas_call(
        ar_kernel,
        out_shape=jax.ShapeDtypeStruct((1, 3, 4, 4, 16, D), BF),
        in_specs=[pl.BlockSpec(memory_space=pltpu.VMEM)],
        out_specs=pl.BlockSpec(memory_space=pltpu.VMEM),
        scratch_shapes=[pltpu.VMEM((3, 4, 4, 16, 2048), BF), pltpu.VMEM((3, 4, 4, 16, 2048), BF)] + bufs + [
            pltpu.SemaphoreType.DMA((3,)), pltpu.SemaphoreType.DMA((3,)),
            pltpu.SemaphoreType.DMA((3, 3, 6)), pltpu.SemaphoreType.DMA((3, 3, 6)),
            pltpu.SemaphoreType.DMA((3, 3, 9)), pltpu.SemaphoreType.DMA((3, 3, 9)),
        ],
        compiler_params=pltpu.CompilerParams(collective_id=1, has_side_effects=True, vmem_limit_bytes=60 << 20),
    )(diff)


HI = lax.Precision.HIGHEST


def nt(a, b, **kw):
    return lax.dot_general(a, b, (((1,), (1,)), ((), ())), preferred_element_type=F32, **kw)


def tn(a, b, **kw):
    return lax.dot_general(a, b, (((0,), (0,)), ((), ())), preferred_element_type=F32, **kw)


def route_rows(wb, w2):
    g = lax.axis_index("grp")
    both = (wb[:, :, 0:8, :].astype(F32) + wb[:, :, 8:16, :].astype(F32)).reshape(128, 128)
    row8 = lax.broadcasted_iota(jnp.int32, (8, 128), 0)
    lane8 = lax.broadcasted_iota(jnp.int32, (8, 128), 1)
    m = lax.broadcasted_iota(jnp.int32, (128, 256), 0)
    n = lax.broadcasted_iota(jnp.int32, (128, 256), 1)
    home = ((m >> 3) & 3) * 64 + (m >> 5) * 16 + (m & 7)
    for part in range(3):
        total = jnp.zeros((8, 256), F32)
        for r in range(2):
            pick = ((lane8 == (2 * part + r) * 16 + 2 * g + row8) & (row8 < 2)).astype(F32)
            chosen = nt(pick, both, precision=HI)
            move = (n == home + 8 * r).astype(F32)
            total = total + jnp.dot(chosen, move, preferred_element_type=F32, precision=HI)
        w2[0:96, 256 * part:256 * part + 256] = jnp.broadcast_to(total[0:1], (96, 256))
        w2[96:192, 256 * part:256 * part + 256] = jnp.broadcast_to(total[1:2], (96, 256))


def to_column(row):
    n = row.shape[1]
    eye = lax.broadcasted_iota(jnp.int32, (n, n), 0) == lax.broadcasted_iota(jnp.int32, (n, n), 1)
    return jnp.sum(jnp.where(eye, jnp.broadcast_to(row, (n, n)), 0.0), axis=1, keepdims=True)


def to_row(col):
    n = col.shape[0]
    eye = lax.broadcasted_iota(jnp.int32, (n, n), 0) == lax.broadcasted_iota(jnp.int32, (n, n), 1)
    return jnp.sum(jnp.where(eye, jnp.broadcast_to(col, (n, n)), 0.0), axis=0, keepdims=True)


def scales(upper, lower, top, low):
    high_end = jax.nn.sigmoid(upper) * top
    low_end = jax.nn.sigmoid(lower) * low
    step = (high_end - low_end) / 15.0
    zero = jnp.floor(-low_end / step + 0.5)
    return low_end, step, zero


def quantize(w, step, inv, zero):
    v = w * inv
    q = jnp.floor(v + 0.5)
    lev = jnp.clip(q, -zero, 15.0 - zero)
    m = jnp.clip(8.0 - jnp.abs(q + zero - 7.5), 0.0, 1.0)
    return lev * step, lev - m * v, m - 1.0


def quant_rows(w_ref, clip_ref, side, ws, keep):
    for e in range(2):
        keep[side, 0, 96 * e:96 * e + 96, :] = to_column(clip_ref[0, e:e + 1, :])
        keep[side, 1, 96 * e:96 * e + 96, :] = to_column(clip_ref[1, e:e + 1, :])

        def rows(n, carry):
            at = pl.multiple_of(n * 16, 16)
            w = w_ref[e, pl.ds(at, 16), :].astype(F32)
            here = pl.ds(pl.multiple_of(96 * e + n * 16, 16), 16)
            top = jnp.max(w, axis=1, keepdims=True)
            low = jnp.min(w, axis=1, keepdims=True)
            keep[side, 2, here, :] = top
            keep[side, 3, here, :] = low
            _, step, zero = scales(keep[side, 0, here, :], keep[side, 1, here, :], top, low)
            val, slope, zs = quantize(w, step, 1.0 / step, zero)
            for k, a in enumerate((val, slope, zs)):
                ws[pl.ds(pl.multiple_of(384 * k + 192 * side + 96 * e + n * 16, 16), 16), :] = a.astype(BF)
            return carry
        lax.fori_loop(0, 6, rows, 0)


def quant_down(w_ref, clip_ref, most, wd):
    for e in range(2):
        def cols(n, carry):
            c = pl.ds(pl.multiple_of(n * 512, 512), 512)
            _, step, zero = scales(clip_ref[0, e:e + 1, c], clip_ref[1, e:e + 1, c], most[e:e + 1, c], -most[2 + e:3 + e, c])
            inv = 1.0 / step

            def rows(k, carry):
                r = pl.ds(pl.multiple_of(k * 16, 16), 16)
                val, slope, zs = quantize(w_ref[e, r, c].astype(F32), step, inv, zero)
                for i, a in enumerate((val, slope, zs)):
                    wd[i, e, r, c] = a.astype(BF)
                return carry
            return lax.fori_loop(0, 6, rows, carry)
        lax.fori_loop(0, 8, cols, 0)


def silu(v):
    return v * jax.nn.sigmoid(v)


def tokens(xb, mat, part):
    return xb[mat, part].reshape(256, D)


def teacher(xb, part, gate_ref, up_ref, w2, hid):
    x = tokens(xb, 0, part)
    cols = pl.ds(pl.multiple_of(part * 256, 256), 256)
    g = nt(gate_ref[...].reshape(192, D), x)
    u = nt(up_ref[...].reshape(192, D), x)
    hid[192:384, cols] = (-(silu(g) * u * w2[:, cols])).astype(BF)


def student(xb, part, ws, w2, hid, sgu):
    x = tokens(xb, 1, part)
    cols = pl.ds(pl.multiple_of(part * 256, 256), 256)
    g = nt(ws[0:192, :], x)
    u = nt(ws[192:384, :], x)
    sgu[0, :, cols] = g
    sgu[1, :, cols] = u
    hid[0:192, cols] = (silu(g) * u * w2[:, cols]).astype(BF)


def difference(part, hid, wd, down_ref, diff):
    cols = pl.ds(pl.multiple_of(part * 256, 256), 256)
    h = hid[:, cols]

    def chunk(n, carry):
        c = pl.ds(pl.multiple_of(n * 1024, 1024), 1024)
        w = jnp.concatenate([wd[0, :, :, c].reshape(192, 1024), down_ref[:, :, c].reshape(192, 1024)], axis=0)
        diff[part, :, :, :, c] = tn(h, w).astype(BF).reshape(4, 4, 16, 1024)
        return carry
    lax.fori_loop(0, 4, chunk, 0)


def factors(xb, part, ws, w2, sgu, fac):
    x = tokens(xb, 1, part)
    cols = pl.ds(pl.multiple_of(part * 256, 256), 256)
    g, u = sgu[0, :, cols], sgu[1, :, cols]
    s = jax.nn.sigmoid(g)
    cg = w2[:, cols] * u * s * (1.0 + g * (1.0 - s))
    cu = w2[:, cols] * g * s
    for k in range(2):
        fac[k, :, cols] = cg * nt(ws[384 + 384 * k:576 + 384 * k, :], x)
        fac[2 + k, :, cols] = cu * nt(ws[576 + 384 * k:768 + 384 * k, :], x)


def each_part(fn):
    def body(part, carry):
        fn(part)
        return carry
    lax.fori_loop(0, 3, body, 0)


def back_sums(cot, part, wd, fac, sums):
    y = cot[0, part].reshape(256, D)
    cols = pl.ds(pl.multiple_of(part * 256, 256), 256)
    dh = nt(wd[0].reshape(192, D), y)
    for k in range(4):
        sums[k] = sums[k] + jnp.sum(fac[k, :, cols] * dh, axis=1, keepdims=True)


def slopes(s1, s2, upper, lower, top, low):
    low_end, step, _ = scales(upper, lower, top, low)
    d_step = s1 + s2 * low_end / step
    d_high = d_step / 15.0
    d_low = -s2 - d_high
    su, sl = jax.nn.sigmoid(upper), jax.nn.sigmoid(lower)
    return d_high * top * su * (1.0 - su), d_low * low * sl * (1.0 - sl)


def row_grads(side, sums, keep, out):
    du, dl = slopes(sums[2 * side], sums[2 * side + 1], *[keep[side, n] for n in range(4)])
    for e in range(2):
        out[0, e:e + 1, :] = to_row(du[96 * e:96 * e + 96, :])
        out[1, e:e + 1, :] = to_row(dl[96 * e:96 * e + 96, :])


def down_sums(cot, hid, wd, clip_ref, most, part_grad):
    def cols(n, carry):
        c = pl.ds(pl.multiple_of(n * 512, 512), 512)
        dq = jnp.zeros((192, 512), F32)
        for part in range(3):
            dq = dq + jnp.dot(hid[0:192, 256 * part:256 * part + 256], cot[0, part, :, :, :, c].reshape(256, 512), preferred_element_type=F32)
        for e in range(2):
            d = dq[96 * e:96 * e + 96]
            s1 = jnp.sum(d * wd[1, e, :, c].astype(F32), axis=0, keepdims=True)
            s2 = jnp.sum(d * wd[2, e, :, c].astype(F32), axis=0, keepdims=True)
            du, dl = slopes(s1, s2, clip_ref[0, e:e + 1, c], clip_ref[1, e:e + 1, c], most[e:e + 1, c], -most[2 + e:3 + e, c])
            part_grad[e:e + 1, c] = du
            part_grad[2 + e:3 + e, c] = dl
        return carry
    lax.fori_loop(0, 8, cols, 0)


def fwd_kernel(xb, wb, most, gate_ref, up_ref, down_ref, gc, uc, dc, diff, wd, fac, hid_o, keep_o, ws, hid, sgu, w2, keep):
    route_rows(wb, w2)
    quant_rows(gate_ref, gc, 0, ws, keep)
    quant_rows(up_ref, uc, 1, ws, keep)
    quant_down(down_ref, dc, most, wd)
    each_part(lambda p: teacher(xb, p, gate_ref, up_ref, w2, hid))
    each_part(lambda p: student(xb, p, ws, w2, hid, sgu))
    each_part(lambda p: difference(p, hid, wd, down_ref, diff))
    each_part(lambda p: factors(xb, p, ws, w2, sgu, fac))
    hid_o[...] = hid[0:192, :]
    keep_o[...] = keep[...]


def bwd_kernel(cot, wd, fac, hid, keep, most, dc, g_out, u_out, d_out, sums, grad, inbox, send, recv):
    at = place()
    greet(at, [peer(at, n)[0] for n in range(1, 16)])
    down_sums(cot, hid, wd, dc, most, grad)
    grad[4:8, :] = jnp.zeros((4, D), F32)
    sends = spread_start(at, grad, inbox, send, recv)
    sums[...] = jnp.zeros_like(sums)
    each_part(lambda p: back_sums(cot, p, wd, fac, sums))
    row_grads(0, sums, keep, g_out)
    row_grads(1, sums, keep, u_out)
    spread_end(at, inbox, send, recv, sends)
    _, me = peer(at, 0)
    total = grad[:, unit_cols(me)]
    for n in range(1, 16):
        total = total + inbox[n]
    for k in range(2):
        d_out[k] = total[2 * k:2 * k + 2]


def sds(shape, dt):
    return jax.ShapeDtypeStruct(shape, dt)


def on_device(x_fp, x_q, expert_ids, route_weight, gate_weight, up_weight, down_weight, gate_clip, up_clip, down_clip):
    xb, wb, most = gather_x(x_fp, x_q, expert_ids, route_weight, down_weight)
    diff, wd, fac, hid, keep = pl.pallas_call(
        fwd_kernel,
        out_shape=(sds((3, 4, 4, 16, D), BF), sds((3, 2, 96, D), BF), sds((4, 192, 768), F32), sds((192, 768), BF), sds((2, 4, 192, 1), F32)),
        in_specs=[VM] * 9,
        out_specs=(VM,) * 5,
        scratch_shapes=[pltpu.VMEM((1152, D), BF), pltpu.VMEM((384, 768), BF), pltpu.VMEM((2, 192, 768), F32),
                        pltpu.VMEM((192, 768), F32), pltpu.VMEM((2, 4, 192, 1), F32)],
        compiler_params=pltpu.CompilerParams(vmem_limit_bytes=60 << 20),
    )(xb, wb, most, gate_weight, up_weight, down_weight, gate_clip, up_clip, down_clip)
    cot = all_reduce(diff)
    return pl.pallas_call(
        bwd_kernel,
        out_shape=(sds((2, 2, 96), F32), sds((2, 2, 96), F32), sds((2, 2, 256), F32)),
        in_specs=[VM] * 7,
        out_specs=(VM,) * 3,
        scratch_shapes=[pltpu.VMEM((4, 192, 1), F32), pltpu.VMEM((8, D), F32), pltpu.VMEM((16, 8, 256), F32), SEM((16,)), SEM((16,))],
        compiler_params=pltpu.CompilerParams(collective_id=2, has_side_effects=True, vmem_limit_bytes=60 << 20),
    )(cot, wd, fac, hid, keep, most, down_clip)


def solution(mesh):
    token = P(("grp", "unit"), None)
    weight = P("grp", "unit", None)
    clip = P(None, "grp", "unit")
    return jax.shard_map(
        on_device,
        mesh=mesh,
        in_specs=(token,) * 4 + (weight,) * 3 + (clip, clip, P(None, "grp", None)),
        out_specs=(clip,) * 3,
        check_vma=False,
    )
```

```python
import jax
import jax.numpy as jnp
from jax import lax
from jax.experimental import pallas as pl
from jax.experimental.pallas import tpu as pltpu
from jax.sharding import PartitionSpec as P

MESH = pl.DeviceIdType.MESH
D = 4096
BF = jnp.bfloat16
F32 = jnp.float32
ORDERS = ("xyz", "yzx", "zxy")


def place():
    g, u = lax.axis_index("grp"), lax.axis_index("unit")
    x, z = lax.div(g, 2), lax.rem(g, 2) * 2 + lax.div(u, 8)
    y, c = lax.rem(lax.div(u, 2), 4), lax.rem(u, 2)
    return dict(x=x, y=y, z=z, c=c)


def device(at):
    return (at["x"] * 2 + lax.div(at["z"], 2), lax.rem(at["z"], 2) * 8 + at["y"] * 2 + at["c"])


def moved(at, **by):
    out = dict(at)
    for axis, step in by.items():
        out[axis] = lax.rem(at[axis] + step, 2 if axis == "c" else 4)
    return out


def remote(src, dst, send, recv, to):
    return pltpu.make_async_remote_copy(
        src_ref=src, dst_ref=dst, send_sem=send, recv_sem=recv, device_id=device(to), device_id_type=MESH)


def columns(y, c, full):
    if full:
        return pl.ds(pl.multiple_of(c * 2048, 2048), 2048)
    return pl.ds(pl.multiple_of(c * 2048 + y * 512, 512), 512)


def block_index(at, part, phase, pos):
    order = ORDERS[part]
    done = order[:phase]
    where = dict(at)
    if phase < 3:
        where[order[phase]] = pos
    rows = [slice(None) if a in done else pl.ds(where[a], 1) for a in "zx"]
    if "y" in done:
        return rows, where["c"] * 2048, 2048
    return rows, where["c"] * 2048 + where["y"] * 512, 512


def slab(at, mat, part, phase, pos, half=None):
    rows, base, width = block_index(at, part, phase, pos)
    if half is not None:
        width = width // 2
        base = base + half * width
    return (mat, part, rows[0], rows[1], slice(None), pl.ds(pl.multiple_of(base, width), width))


class Gather:
    def __init__(self, at, buf, mat, part, send, recv, pending):
        self.at, self.buf, self.mat, self.part = at, buf, mat, part
        self.send, self.recv, self.pending = send, recv, pending
        self.partner = moved(at, c=1)

    def push(self, idx, sem, to):
        ref = self.buf.at[idx]
        cp = remote(ref, ref, self.send.at[sem], self.recv.at[sem], to)
        cp.start()
        self.pending.append(cp)

    def landed(self, idx, sem, back):
        ref = self.buf.at[idx]
        remote(ref, ref, self.send.at[sem], self.recv.at[sem], back).wait_recv()

    def idx(self, phase, ahead, half=None, at=None):
        at = at or self.at
        pos = None
        if phase < 3:
            pos = lax.rem(at[ORDERS[self.part][phase]] + ahead, 4)
        return slab(at, self.mat, self.part, phase, pos, half)

    def ring(self, phase, n):
        return moved(self.at, **{ORDERS[self.part][phase]: n})

    def spread(self, phase):
        for n in (1, 3, 2):
            self.push(self.idx(phase, 0), 3 * phase + n - 1, self.ring(phase, n))

    def spread_wait(self, phase):
        for n in (1, 3, 2):
            self.landed(self.idx(phase, 4 - n), 3 * phase + n - 1, self.ring(phase, 4 - n))

    def last(self):
        for side, step in ((0, 1), (1, 3)):
            self.push(self.idx(2, 0, side), 6 + side, self.ring(2, step))
        for side, step in ((0, 1), (1, 3)):
            self.push(self.idx(2, 0, 1 - side), 8 + side, self.ring(2, step))
        self.push(self.idx(2, 0), 12, self.partner)

    def last_mid(self):
        for side, step in ((0, 1), (1, 3)):
            idx = self.idx(2, 4 - step, side)
            self.landed(idx, 6 + side, self.ring(2, 4 - step))
            self.push(idx, 10 + side, self.ring(2, step))

    def last_near(self):
        for side, step in ((0, 1), (1, 3)):
            self.landed(self.idx(2, 4 - step, 1 - side), 8 + side, self.ring(2, 4 - step))
            self.push(self.idx(2, 4 - step), 13 + side, self.partner)

    def last_far(self):
        for side, step in ((0, 1), (1, 3)):
            idx = self.idx(2, 2, side)
            self.landed(idx, 10 + side, self.ring(2, 4 - step))
            self.push(idx, 15 + side, self.partner)

    def finish(self):
        self.landed(self.idx(2, 0, at=self.partner), 12, self.partner)
        for side, step in ((0, 1), (1, 3)):
            self.landed(self.idx(2, 4 - step, at=self.partner), 13 + side, self.partner)
        for side in (0, 1):
            self.landed(self.idx(2, 2, side, at=self.partner), 15 + side, self.partner)


def phase_shape(part, phase):
    done = ORDERS[part][:phase]
    return (4 if "z" in done else 1, 4 if "x" in done else 1, 16, 2048 if "y" in done else 512)


class Reduce:
    def __init__(self, at, part, acc, out, theirs, halves, fulls, b_in, c_in, buf, send, recv, pending):
        self.at, self.part, self.acc, self.out, self.theirs = at, part, acc, out, theirs
        self.halves, self.fulls, self.b_in, self.c_in, self.buf = halves, fulls, b_in, c_in, buf
        self.send, self.recv, self.pending = send, recv, pending
        self.partner = moved(at, c=1)

    def push(self, src, dst, sem, to):
        cp = remote(src, dst, self.send.at[sem], self.recv.at[sem], to)
        cp.start()
        self.pending.append(cp)

    def landed(self, dst, sem, back):
        remote(dst, dst, self.send.at[sem], self.recv.at[sem], back).wait_recv()

    def idx(self, phase, ahead, half=None):
        rows, _, width = block_index(self.at, self.part, phase, 0)
        order = ORDERS[self.part]
        where = dict(self.at)
        where[order[phase]] = lax.rem(self.at[order[phase]] + ahead, 4)
        rows = [slice(None) if a in order[:phase] else pl.ds(where[a], 1) for a in "zx"]
        base = 0 if width == 2048 else where["y"] * 512
        if half is not None:
            width = width // 2
            base = base + half * width
        return (self.part, rows[0], rows[1], slice(None), pl.ds(pl.multiple_of(base, width), width))

    def ring(self, phase, n):
        return moved(self.at, **{ORDERS[self.part][phase]: n})

    def add(self, idx, *others):
        total = self.acc[idx].astype(F32)
        for v in others:
            total = total + v.astype(F32)
        return total

    def swap(self):
        self.push(self.out.at[self.part], self.theirs.at[self.part], 0, self.partner)

    def swap_sum(self):
        self.landed(self.theirs.at[self.part], 0, self.partner)

        def rows(n, carry):
            self.acc[self.part, n] = self.add((self.part, n), self.theirs[self.part, n]).astype(BF)
            return carry
        lax.fori_loop(0, 4, rows, 0)

    def first(self):
        half = phase_shape(self.part, 2)[3] // 2
        for side, step in ((0, 1), (1, 3)):
            self.push(self.acc.at[self.idx(2, 2, side)], self.halves.at[side], 1 + side, self.ring(2, step))
        for side, step in ((0, 1), (1, 3)):
            other = 1 - side
            self.push(self.acc.at[self.idx(2, step, other)], self.fulls.at[side, :, :, :, pl.ds(other * half, half)],
                      3 + side, self.ring(2, step))

    def first_mid(self):
        half = phase_shape(self.part, 2)[3] // 2
        for side, step in ((0, 1), (1, 3)):
            self.landed(self.halves.at[side], 1 + side, self.ring(2, 4 - step))
            idx = self.idx(2, step, side)
            self.acc[idx] = self.add(idx, self.halves[side]).astype(BF)
            self.push(self.acc.at[idx], self.fulls.at[side, :, :, :, pl.ds(side * half, half)], 5 + side, self.ring(2, step))

    def first_end(self):
        half = phase_shape(self.part, 2)[3] // 2
        for side, step in ((0, 1), (1, 3)):
            for which, sem in ((1 - side, 3 + side), (side, 5 + side)):
                self.landed(self.fulls.at[side, :, :, :, pl.ds(which * half, half)], sem, self.ring(2, 4 - step))
        idx = self.idx(2, 0)
        self.acc[idx] = self.add(idx, self.fulls[0], self.fulls[1]).astype(BF)
        for n in (1, 3, 2):
            self.push(self.acc.at[self.idx(1, n)], self.b_in.at[n - 1], 6 + n, self.ring(1, n))

    def second_end(self):
        for n in (1, 3, 2):
            self.landed(self.b_in.at[n - 1], 6 + n, self.ring(1, 4 - n))
        idx = self.idx(1, 0)
        self.acc[idx] = self.add(idx, *[self.b_in[n] for n in range(3)]).astype(BF)
        for n in (1, 3, 2):
            self.push(self.acc.at[idx], self.c_in.at[n - 1], 9 + n, self.ring(0, n))

    def third_end(self):
        for n in (1, 3, 2):
            self.landed(self.c_in.at[n - 1], 9 + n, self.ring(0, 4 - n))
        total = self.add(self.idx(1, 0), *[self.c_in[n] for n in range(3)])
        pos = self.at[ORDERS[self.part][1]]
        self.buf[slab(self.at, 0, self.part, 1, pos)] = total.astype(BF)


def peer(at, n):
    u = lax.rem(lax.rem(at["z"], 2) * 8 + at["y"] * 2 + at["c"] + n, 16)
    return dict(x=at["x"], z=lax.div(at["z"], 2) * 2 + lax.div(u, 8), y=lax.rem(lax.div(u, 2), 4), c=lax.rem(u, 2)), u


def friends(at):
    out = [peer(at, n)[0] for n in range(1, 16)] + [moved(at, x=n) for n in (1, 2, 3)]
    low = lax.rem(at["z"], 2)
    return out + [dict(at, z=lax.rem(at["z"] - low + n, 4)) for n in (2, 3)]


def greet_signal(others):
    barrier = pltpu.get_barrier_semaphore()
    for to in others:
        pl.semaphore_signal(barrier, inc=1, device_id=device(to), device_id_type=MESH)


def greet_wait(others):
    pl.semaphore_wait(pltpu.get_barrier_semaphore(), len(others))


def pack_rows(xf_ref, xq_ref, ids_ref, route_ref, rows_f, packed):
    lane = lax.broadcasted_iota(jnp.int32, (6, 128), 1)
    base = lax.broadcasted_iota(jnp.int32, (6, 128), 0) * 16
    dense = jnp.zeros((6, 128), F32)
    for k in range(8):
        dense = dense + jnp.where(lane == base + ids_ref[:, k:k + 1], route_ref[:, k:k + 1], 0.0)
    weights = jnp.sum(dense, axis=0, keepdims=True)
    rest = weights - weights.astype(BF).astype(F32)
    rows_f[0:6, :] = xf_ref[...].astype(F32)
    rows_f[8:14, :] = xq_ref[...].astype(F32)
    for n in range(8):
        rows_f[6:7, 512 * n:512 * n + 128] = weights
        rows_f[7:8, 512 * n:512 * n + 128] = rest
    packed[...] = rows_f[...].astype(BF)


def turn_start(at, packed, stage, sem_a, sem_b):
    sends = []
    mine = at["c"] * 4 + at["y"]
    for n in range(1, 8):
        to = moved(at, y=n // 2, c=n % 2)
        cp = remote(packed.at[:, columns(to["y"], to["c"], False)], stage.at[mine], sem_a.at[n], sem_b.at[n], to)
        cp.start()
        sends.append(cp)
    stage[mine] = packed[:, columns(at["y"], at["c"], False)]
    return sends


def turn_end(at, stage, spread, xb, wb, sem_a, sem_b, sends):
    for n in range(1, 8):
        back = moved(at, y=(4 - n // 2) % 4, c=n % 2)
        slot = back["c"] * 4 + back["y"]
        remote(stage.at[slot], stage.at[slot], sem_a.at[n], sem_b.at[n], back).wait_recv()
    for cp in sends:
        cp.wait_send()
    for j in range(8):
        for q in range(4):
            spread[q * 128 + 16 * j:q * 128 + 16 * j + 16, :] = stage[j, :, 128 * q:128 * q + 128].astype(F32)
    cols = columns(at["y"], at["c"], False)
    for mat in range(2):
        for part in range(3):
            rows = [
                jnp.concatenate(
                    [spread[pl.ds(q * 128 + 8 * mat + 2 * part + r, 8, stride=16), :] for q in range(4)], axis=1)
                for r in range(2)
            ]
            xb[mat, part, at["z"], at["x"], :, cols] = jnp.concatenate(rows, axis=0).astype(BF)
    split = [spread[pl.ds(6 + r, 8, stride=16), :] for r in range(2)]
    wb[at["x"], at["z"]] = jnp.concatenate(split, axis=0).astype(BF)


def route_start(at, wb, axis, send, recv):
    sends = []
    for n in range(1, 4):
        to = moved(at, **{axis: n})
        idx = (at["x"], at["z"]) if axis == "z" else (at["x"],)
        cp = remote(wb.at[idx], wb.at[idx], send.at[n], recv.at[n], to)
        cp.start()
        sends.append(cp)
    return sends


def route_end(at, wb, axis, send, recv, sends):
    for n in range(1, 4):
        back = moved(at, **{axis: 4 - n})
        idx = (at["x"], back["z"]) if axis == "z" else (back["x"],)
        remote(wb.at[idx], wb.at[idx], send.at[n], recv.at[n], back).wait_recv()
    for cp in sends:
        cp.wait_send()


def unit_cols(u):
    return pl.ds(pl.multiple_of(u * 256, 256), 256)


def stats_local(down_ref, most):
    for e in range(2):
        w = down_ref[e].astype(F32)
        most[e:e + 1, :] = jnp.max(w, axis=0, keepdims=True)
        most[2 + e:3 + e, :] = -jnp.min(w, axis=0, keepdims=True)
    most[4:8, :] = jnp.zeros((4, D), F32)


def spread_start(at, src, dst, send, recv):
    sends = []
    for n in range(1, 16):
        to, u = peer(at, n)
        cp = remote(src.at[:, unit_cols(u)], dst.at[n], send.at[n], recv.at[n], to)
        cp.start()
        sends.append(cp)
    return sends


def spread_end(at, dst, send, recv, sends):
    for n in range(1, 16):
        back, _ = peer(at, 16 - n)
        remote(dst.at[n], dst.at[n], send.at[n], recv.at[n], back).wait_recv()
    for cp in sends:
        cp.wait_send()


def stats_share(at, most, fin, inbox, send, recv):
    _, me = peer(at, 0)
    top = most[:, unit_cols(me)]
    for n in range(1, 16):
        top = jnp.maximum(top, inbox[n])
    fin[:, unit_cols(me)] = top
    sends = []
    for n in range(1, 16):
        to, _ = peer(at, n)
        cp = remote(fin.at[:, unit_cols(me)], fin.at[:, unit_cols(me)], send.at[n], recv.at[n], to)
        cp.start()
        sends.append(cp)
    return sends


def stats_end(at, fin, send, recv, sends):
    for n in range(1, 16):
        back, u = peer(at, 16 - n)
        remote(fin.at[:, unit_cols(u)], fin.at[:, unit_cols(u)], send.at[n], recv.at[n], back).wait_recv()
    for cp in sends:
        cp.wait_send()


HI = lax.Precision.HIGHEST


def nt(a, b, **kw):
    return lax.dot_general(a, b, (((1,), (1,)), ((), ())), preferred_element_type=F32, **kw)


def tn(a, b, **kw):
    return lax.dot_general(a, b, (((0,), (0,)), ((), ())), preferred_element_type=F32, **kw)


def route_rows(wb, w2):
    g = lax.axis_index("grp")
    both = (wb[:, :, 0:8, :].astype(F32) + wb[:, :, 8:16, :].astype(F32)).reshape(128, 128)
    row8 = lax.broadcasted_iota(jnp.int32, (8, 128), 0)
    lane8 = lax.broadcasted_iota(jnp.int32, (8, 128), 1)
    m = lax.broadcasted_iota(jnp.int32, (128, 256), 0)
    n = lax.broadcasted_iota(jnp.int32, (128, 256), 1)
    home = ((m >> 3) & 3) * 64 + (m >> 5) * 16 + (m & 7)
    for part in range(3):
        total = jnp.zeros((8, 256), F32)
        for r in range(2):
            pick = ((lane8 == (2 * part + r) * 16 + 2 * g + row8) & (row8 < 2)).astype(F32)
            chosen = nt(pick, both, precision=HI)
            move = (n == home + 8 * r).astype(F32)
            total = total + jnp.dot(chosen, move, preferred_element_type=F32, precision=HI)
        w2[0:96, 256 * part:256 * part + 256] = jnp.broadcast_to(total[0:1], (96, 256))
        w2[96:192, 256 * part:256 * part + 256] = jnp.broadcast_to(total[1:2], (96, 256))


def to_column(row):
    n = row.shape[1]
    eye = lax.broadcasted_iota(jnp.int32, (n, n), 0) == lax.broadcasted_iota(jnp.int32, (n, n), 1)
    return jnp.sum(jnp.where(eye, jnp.broadcast_to(row, (n, n)), 0.0), axis=1, keepdims=True)


def to_row(col):
    n = col.shape[0]
    eye = lax.broadcasted_iota(jnp.int32, (n, n), 0) == lax.broadcasted_iota(jnp.int32, (n, n), 1)
    return jnp.sum(jnp.where(eye, jnp.broadcast_to(col, (n, n)), 0.0), axis=0, keepdims=True)


def scales(upper, lower, top, low):
    high_end = jax.nn.sigmoid(upper) * top
    low_end = jax.nn.sigmoid(lower) * low
    step = (high_end - low_end) / 15.0
    zero = jnp.floor(-low_end / step + 0.5)
    return low_end, step, zero


def quantize(w, step, inv, zero):
    v = w * inv
    q = jnp.floor(v + 0.5)
    lev = jnp.clip(q, -zero, 15.0 - zero)
    m = jnp.clip(8.0 - jnp.abs(q + zero - 7.5), 0.0, 1.0)
    return lev * step, lev - m * v, m - 1.0


def quant_rows(w_ref, clip_ref, side, ws, keep):
    for e in range(2):
        keep[side, 0, 96 * e:96 * e + 96, :] = to_column(clip_ref[0, e:e + 1, :])
        keep[side, 1, 96 * e:96 * e + 96, :] = to_column(clip_ref[1, e:e + 1, :])

    def rows(n, carry):
        here = pl.ds(pl.multiple_of(n * 16, 16), 16)
        line = pl.ds(pl.multiple_of(192 * side + n * 16, 16), 16)
        w = w_ref[line, :].astype(F32)
        top = jnp.max(w, axis=1, keepdims=True)
        low = jnp.min(w, axis=1, keepdims=True)
        keep[side, 2, here, :] = top
        keep[side, 3, here, :] = low
        _, step, zero = scales(keep[side, 0, here, :], keep[side, 1, here, :], top, low)
        inv = 1.0 / step

        def cols(k, carry):
            c = pl.ds(pl.multiple_of(k * 512, 512), 512)
            made = quantize(w_ref[line, c].astype(F32), step, inv, zero)
            for i, a in enumerate(made):
                ws[pl.ds(pl.multiple_of(384 * i + 192 * side + n * 16, 16), 16), c] = a.astype(BF)
            return carry
        return lax.fori_loop(0, 8, cols, carry)
    lax.fori_loop(0, 12, rows, 0)


def quant_down(w_ref, clip_ref, most, wd):
    for e in range(2):
        def cols(n, carry):
            c = pl.ds(pl.multiple_of(n * 512, 512), 512)
            _, step, zero = scales(clip_ref[0, e:e + 1, c], clip_ref[1, e:e + 1, c], most[e:e + 1, c], -most[2 + e:3 + e, c])
            inv = 1.0 / step

            def rows(k, carry):
                r = pl.ds(pl.multiple_of(k * 16, 16), 16)
                val, slope, zs = quantize(w_ref[e, r, c].astype(F32), step, inv, zero)
                for i, a in enumerate((val, slope, zs)):
                    wd[i, e, r, c] = a.astype(BF)
                return carry
            return lax.fori_loop(0, 6, rows, carry)
        lax.fori_loop(0, 8, cols, 0)


def silu(v):
    return v * jax.nn.sigmoid(v)


def tokens(xb, mat, part):
    return xb[mat, part].reshape(256, D)


def part_cols(part):
    return pl.ds(256 * part, 256)


def teacher(xb, part, w_ref, w2, hid):
    cols = part_cols(part)
    gu = nt(w_ref[...], tokens(xb, 0, part))
    hid[192:384, cols] = (-(silu(gu[0:192]) * gu[192:384] * w2[:, cols])).astype(BF)


def student(xb, part, ws, w2, hid, sgu):
    cols = part_cols(part)
    gu = nt(ws[0:384, :], tokens(xb, 1, part))
    sgu[:, cols] = gu
    hid[0:192, cols] = (silu(gu[0:192]) * gu[192:384] * w2[:, cols]).astype(BF)


def difference(at, part, hid, wd, down_ref, acc, out):
    h = hid[:, part_cols(part)]

    def chunk(n, carry):
        for dst, core in ((out, 1 - at["c"]), (acc, at["c"])):
            c = pl.ds(pl.multiple_of(core * 2048 + n * 1024, 1024), 1024)
            w = jnp.concatenate([wd[0, :, :, c].reshape(192, 1024), down_ref[:, :, c].reshape(192, 1024)], axis=0)
            dst[part, :, :, :, pl.ds(pl.multiple_of(n * 1024, 1024), 1024)] = tn(h, w).astype(BF).reshape(4, 4, 16, 1024)
        return carry
    lax.fori_loop(0, 2, chunk, 0)


def factors(xb, part, ws, w2, sgu, fac):
    cols = part_cols(part)
    a = nt(ws[384:1152, :], tokens(xb, 1, part))
    g, u = sgu[0:192, cols], sgu[192:384, cols]
    s = jax.nn.sigmoid(g)
    cg = w2[:, cols] * u * s * (1.0 + g * (1.0 - s))
    cu = w2[:, cols] * g * s
    for k in range(2):
        fac[k, :, cols] = cg * a[384 * k:384 * k + 192]
        fac[2 + k, :, cols] = cu * a[384 * k + 192:384 * k + 384]


def back_sums(xb, part, wd, fac, sums):
    cols = part_cols(part)
    dh = nt(wd[0].reshape(192, D), tokens(xb, 0, part))
    for k in range(4):
        sums[k] = sums[k] + jnp.sum(fac[k, :, cols] * dh, axis=1, keepdims=True)


def slopes(s1, s2, upper, lower, top, low):
    low_end, step, _ = scales(upper, lower, top, low)
    d_step = s1 + s2 * low_end / step
    d_high = d_step / 15.0
    d_low = -s2 - d_high
    su, sl = jax.nn.sigmoid(upper), jax.nn.sigmoid(lower)
    return d_high * top * su * (1.0 - su), d_low * low * sl * (1.0 - sl)


def row_grads(side, sums, keep, out):
    du, dl = slopes(sums[2 * side], sums[2 * side + 1], *[keep[side, n] for n in range(4)])
    for e in range(2):
        out[0, e:e + 1, :] = to_row(du[96 * e:96 * e + 96, :])
        out[1, e:e + 1, :] = to_row(dl[96 * e:96 * e + 96, :])


def down_add(xb, part, hid, dq):
    h = hid[0:192, part_cols(part)]

    def cols(n, carry):
        c = pl.ds(pl.multiple_of(n * 1024, 1024), 1024)
        new = jnp.dot(h, xb[0, part, :, :, :, c].reshape(256, 1024), preferred_element_type=F32)
        dq[:, c] = new if part == 0 else dq[:, c] + new
        return carry
    lax.fori_loop(0, 4, cols, 0)


def down_sums(xb, part, hid, dq, wd, clip_ref, most, grad):
    h = hid[0:192, part_cols(part)]

    def cols(n, carry):
        c = pl.ds(pl.multiple_of(n * 512, 512), 512)
        new = jnp.dot(h, xb[0, part, :, :, :, c].reshape(256, 512), preferred_element_type=F32)
        full = dq[:, c] + new
        for e in range(2):
            d = full[96 * e:96 * e + 96]
            s1 = jnp.sum(d * wd[1, e, :, c].astype(F32), axis=0, keepdims=True)
            s2 = jnp.sum(d * wd[2, e, :, c].astype(F32), axis=0, keepdims=True)
            du, dl = slopes(s1, s2, clip_ref[0, e:e + 1, c], clip_ref[1, e:e + 1, c], most[e:e + 1, c], -most[2 + e:3 + e, c])
            grad[e:e + 1, c] = du
            grad[2 + e:3 + e, c] = dl
        return carry
    lax.fori_loop(0, 8, cols, 0)


def kernel(xf_ref, xq_ref, ids_ref, route_ref, gate_hbm, up_hbm, down_hbm, gc, uc, dc, g_out, u_out, d_out,
           xb, wb, packed, stage, rows_f, spread, raw, down, most, fin, inbox, grad, d_inbox, ws, wd, hid, sgu, w2, keep,
           fac, dq, sums, acc, out, theirs, *rest):
    halves, fulls, b_in, c_in = (rest[3 * k:3 * k + 3] for k in range(4))
    (l_s, t_s, t_r, z_s, z_r, x_s, x_r, m_s, m_r, n_s, n_r, d_s, d_r, ag_s, ag_r, rs_s, rs_r) = rest[12:]
    at = place()
    loads = [pltpu.make_async_copy(down_hbm, down, l_s.at[0])]
    for side, src in enumerate((gate_hbm, up_hbm)):
        for e in range(2):
            lines = pl.ds(192 * side + 96 * e, 96)
            loads.append(pltpu.make_async_copy(src.at[e], raw.at[lines], l_s.at[1 + 2 * side + e]))
    for cp in loads:
        cp.start()
    others = friends(at)
    greet_signal(others)
    pack_rows(xf_ref, xq_ref, ids_ref, route_ref, rows_f, packed)
    loads[0].wait()
    stats_local(down, most)
    greet_wait(others)
    turned = turn_start(at, packed, stage, t_s, t_r)
    m_sends = spread_start(at, most, inbox, m_s, m_r)
    for cp in loads[1:3]:
        cp.wait()
    turn_end(at, stage, spread, xb, wb, t_s, t_r, turned)
    pending = []
    streams = [[Gather(at, xb, mat, p, ag_s.at[s, p], ag_r.at[s, p], pending) for p in range(3)]
               for s, mat in enumerate((0, 1, 0))]
    fp, q, ct = streams

    def each(stream, step, *args):
        for g in stream:
            getattr(g, step)(*args)

    each(fp, "spread", 0)
    each(q, "spread", 0)
    z_sends = route_start(at, wb, "z", z_s, z_r)
    quant_rows(raw, gc, 0, ws, keep)
    spread_end(at, inbox, m_s, m_r, m_sends)
    n_sends = stats_share(at, most, fin, inbox, n_s, n_r)
    each(fp, "spread_wait", 0)
    each(fp, "spread", 1)
    each(q, "spread_wait", 0)
    each(q, "spread", 1)
    route_end(at, wb, "z", z_s, z_r, z_sends)
    x_sends = route_start(at, wb, "x", x_s, x_r)
    for cp in loads[3:5]:
        cp.wait()
    quant_rows(raw, uc, 1, ws, keep)
    each(fp, "spread_wait", 1)
    each(fp, "last")
    each(q, "spread_wait", 1)
    route_end(at, wb, "x", x_s, x_r, x_sends)
    route_rows(wb, w2)
    each(fp, "last_mid")
    each(q, "last")
    stats_end(at, fin, n_s, n_r, n_sends)
    quant_down(down, dc, fin, wd)
    each(fp, "last_near")
    each(fp, "last_far")
    each(fp, "finish")
    teacher(xb, 0, raw, w2, hid)
    each(q, "last_mid")
    teacher(xb, 1, raw, w2, hid)
    teacher(xb, 2, raw, w2, hid)
    each(q, "last_near")
    each(q, "last_far")
    each(q, "finish")
    for cp in pending:
        cp.wait_send()
    del pending[:]
    red = [Reduce(at, p, acc, out, theirs, halves[p], fulls[p], b_in[p], c_in[p], xb, rs_s.at[p], rs_r.at[p], pending)
           for p in range(3)]

    def forward(p):
        student(xb, p, ws, w2, hid, sgu)
        difference(at, p, hid, wd, down, acc, out)
        red[p].swap()

    forward(0)
    forward(1)
    red[0].swap_sum()
    red[0].first()
    forward(2)
    red[1].swap_sum()
    red[1].first()
    red[0].first_mid()
    red[2].swap_sum()
    red[2].first()
    factors(xb, 0, ws, w2, sgu, fac)
    red[0].first_end()
    red[1].first_mid()
    red[2].first_mid()
    factors(xb, 1, ws, w2, sgu, fac)
    red[0].second_end()
    red[1].first_end()
    red[2].first_end()
    factors(xb, 2, ws, w2, sgu, fac)
    sums[...] = jnp.zeros_like(sums)
    grad[4:8, :] = jnp.zeros((4, D), F32)
    for p in range(3):
        red[p].third_end() if p == 0 else red[p].second_end()
        if p == 0:
            ct[0].spread(1)
    for p in (1, 2):
        red[p].third_end()
        ct[p].spread(1)
    for p in range(3):
        ct[p].spread_wait(1)
        ct[p].last()
    each(ct, "last_mid")
    for p in range(3):
        ct[p].last_near()
    for p in range(3):
        ct[p].last_far()
    for p in range(3):
        ct[p].finish()
        if p < 2:
            down_add(xb, p, hid, dq)
            back_sums(xb, p, wd, fac, sums)
    down_sums(xb, 2, hid, dq, wd, dc, fin, grad)
    d_sends = spread_start(at, grad, d_inbox, d_s, d_r)
    back_sums(xb, 2, wd, fac, sums)
    row_grads(0, sums, keep, g_out)
    row_grads(1, sums, keep, u_out)
    for cp in pending:
        cp.wait_send()
    spread_end(at, d_inbox, d_s, d_r, d_sends)
    _, me = peer(at, 0)
    total = grad[:, unit_cols(me)]
    for n in range(1, 16):
        total = total + d_inbox[n]
    for k in range(2):
        d_out[k] = total[2 * k:2 * k + 2]


SEM = pltpu.SemaphoreType.DMA
VM = pl.BlockSpec(memory_space=pltpu.VMEM)
ANY = pl.BlockSpec(memory_space=pl.ANY)


def sds(shape, dt):
    return jax.ShapeDtypeStruct(shape, dt)


def hand_over(a, b, c, x, y, z):
    x[...] = a[...]
    y[...] = b[...]
    z[...] = c[...]


def on_device(x_fp, x_q, expert_ids, route_weight, gate_weight, up_weight, down_weight, gate_clip, up_clip, down_clip):
    shapes = [phase_shape(p, 2) for p in range(3)]
    small = [phase_shape(p, 1) for p in range(3)]
    scratch = [((2, 3, 4, 4, 16, D), BF), ((4, 4, 16, 128), BF), ((16, D), BF), ((8, 16, 512), BF), ((16, D), F32),
               ((512, 128), F32), ((384, D), BF), ((2, 96, D), BF), ((8, D), F32), ((8, D), F32), ((16, 8, 256), F32),
               ((8, D), F32), ((16, 8, 256), F32), ((1152, D), BF), ((3, 2, 96, D), BF), ((384, 768), BF), ((384, 768), F32),
               ((192, 768), F32), ((2, 4, 192, 1), F32), ((4, 192, 768), F32), ((192, D), F32), ((4, 192, 1), F32),
               ((3, 4, 4, 16, 2048), BF), ((3, 4, 4, 16, 2048), BF), ((3, 4, 4, 16, 2048), BF)]
    scratch += [((2,) + s[:3] + (s[3] // 2,), BF) for s in shapes]
    scratch += [((2,) + s, BF) for s in shapes]
    scratch += [((3,) + s, BF) for s in small] * 2
    outs = (sds((2, 2, 96), F32), sds((2, 2, 96), F32), sds((2, 2, 256), F32))
    made = pl.pallas_call(
        kernel,
        out_shape=outs,
        in_specs=[VM] * 4 + [ANY] * 3 + [VM] * 3,
        out_specs=(VM,) * 3,
        scratch_shapes=[pltpu.VMEM(s, t) for s, t in scratch] + [
            SEM((5,)), SEM((8,)), SEM((8,)), SEM((4,)), SEM((4,)), SEM((4,)), SEM((4,)),
            SEM((16,)), SEM((16,)), SEM((16,)), SEM((16,)), SEM((16,)), SEM((16,)),
            SEM((3, 3, 17)), SEM((3, 3, 17)), SEM((3, 13)), SEM((3, 13))],
        compiler_params=pltpu.CompilerParams(collective_id=0, has_side_effects=True, vmem_limit_bytes=62 << 20),
    )(x_fp, x_q, expert_ids, route_weight, gate_weight, up_weight, down_weight, gate_clip, up_clip, down_clip)
    return pl.pallas_call(hand_over, out_shape=outs, in_specs=[VM] * 3, out_specs=(VM,) * 3)(*made)


def solution(mesh):
    token = P(("grp", "unit"), None)
    weight = P("grp", "unit", None)
    clip = P(None, "grp", "unit")
    return jax.shard_map(
        on_device,
        mesh=mesh,
        in_specs=(token,) * 4 + (weight,) * 3 + (clip, clip, P(None, "grp", None)),
        out_specs=(clip,) * 3,
        check_vma=False,
    )
```

```python
import jax
import jax.numpy as jnp
from jax import lax
from jax.experimental import pallas as pl
from jax.experimental.pallas import tpu as pltpu
from jax.sharding import PartitionSpec as P

MESH = pl.DeviceIdType.MESH
D = 4096
BF = jnp.bfloat16
F32 = jnp.float32
ORDERS = ("xyz", "yzx", "zxy")
CHUNKS = 4
WIDE = 2048 // CHUNKS


def place():
    g, u = lax.axis_index("grp"), lax.axis_index("unit")
    x, z = lax.div(g, 2), lax.rem(g, 2) * 2 + lax.div(u, 8)
    y, c = lax.rem(lax.div(u, 2), 4), lax.rem(u, 2)
    return dict(x=x, y=y, z=z, c=c)


def device(at):
    return (at["x"] * 2 + lax.div(at["z"], 2), lax.rem(at["z"], 2) * 8 + at["y"] * 2 + at["c"])


def moved(at, **by):
    out = dict(at)
    for axis, step in by.items():
        out[axis] = lax.rem(at[axis] + step, 2 if axis == "c" else 4)
    return out


def remote(src, dst, send, recv, to):
    return pltpu.make_async_remote_copy(
        src_ref=src, dst_ref=dst, send_sem=send, recv_sem=recv, device_id=device(to), device_id_type=MESH)


def columns(y, c, full):
    if full:
        return pl.ds(pl.multiple_of(c * 2048, 2048), 2048)
    return pl.ds(pl.multiple_of(c * 2048 + y * 512, 512), 512)


def rows_of(at, done):
    return [slice(None) if a in done else pl.ds(at[a], 1) for a in "zx"]


def ring_pos(at, part, phase, ahead):
    axis = ORDERS[part][phase]
    return dict(at, **{axis: lax.rem(at[axis] + ahead, 4)})


def ring_step(at, part, phase, n):
    return moved(at, **{ORDERS[part][phase]: n})


class Gather:
    def __init__(self, at, buf, mat, send, recv):
        self.at, self.buf, self.mat = at, buf, mat
        self.send, self.recv = send, recv
        self.partner = moved(at, c=1)

    def block(self, part, phase, ahead, half=None, at=None):
        where = ring_pos(at or self.at, part, phase, ahead)
        done = ORDERS[part][:phase]
        width = 2048 if "y" in done else 512
        base = where["c"] * 2048 + (0 if "y" in done else where["y"] * 512)
        if half is not None:
            width = width // 2
            base = base + half * width
        rows = rows_of(where, done)
        return self.buf.at[self.mat, part, rows[0], rows[1], :, pl.ds(pl.multiple_of(base, width), width)]

    def push(self, ref, send, recv, to):
        remote(ref, ref, self.send.at[send], self.recv.at[recv], to).start()

    def landed(self, ref, recv):
        remote(ref, ref, self.send.at[0], self.recv.at[recv], self.partner).wait_recv()

    def spread(self, phase):
        for n in (2, 1, 3):
            for part in range(3):
                self.push(self.block(part, phase, 0), 0, phase, ring_step(self.at, part, phase, n))

    def spread_wait(self, phase):
        self.landed(self.buf.at[self.mat, :, 0:3, 0:1, :, 0:(512, 2048)[phase]], phase)

    def last(self):
        for swap in (0, 1):
            for part in range(3):
                for side, step in ((0, 1), (1, 3)):
                    self.push(self.block(part, 2, 0, side ^ swap), 1, 2 + swap, ring_step(self.at, part, 2, step))
        for part in range(3):
            self.push(self.block(part, 2, 0), 2, 5, self.partner)

    def last_mid(self):
        self.landed(self.buf.at[self.mat, :, 0:2, 0:1], 2)
        for part in range(3):
            for side, step in ((0, 1), (1, 3)):
                self.push(self.block(part, 2, 4 - step, side), 1, 4, ring_step(self.at, part, 2, step))

    def last_near(self):
        self.landed(self.buf.at[self.mat, :, 0:2, 0:1], 3)
        for part in range(3):
            for step in (1, 3):
                self.push(self.block(part, 2, step), 2, 5, self.partner)

    def last_far(self):
        self.landed(self.buf.at[self.mat, :, 0:2, 0:1], 4)
        for part in range(3):
            self.push(self.block(part, 2, 2), 2, 5, self.partner)

    def finish(self):
        self.landed(self.buf.at[self.mat, :, 0:2], 5)


def gathers_sent(buf, send, recv, to):
    for sem, ref in enumerate((buf.at[0, :, 0:3, 0:2, :, 0:2560], buf.at[0, :, 0:3, :], buf.at[0])):
        remote(ref, ref, send.at[sem], recv.at[0], to).wait_send()


def phase_shape(part, phase):
    done = ORDERS[part][:phase]
    return (4 if "z" in done else 1, 4 if "x" in done else 1, 16, WIDE if "y" in done else WIDE // 4)


class Reduce:
    def __init__(self, at, chunk, acc, out, theirs, a_in, b_in, c_in, buf, send, recv):
        self.at, self.chunk, self.acc, self.out, self.theirs = at, chunk, acc, out, theirs
        self.ins = {2: a_in, 1: b_in, 0: c_in}
        self.buf, self.send, self.recv = buf, send, recv
        self.partner = moved(at, c=1)

    def push(self, src, dst, send, recv, to):
        remote(src, dst, self.send.at[send], self.recv.at[self.chunk, recv], to).start()

    def landed(self, ref, recv):
        remote(ref, ref, self.send.at[0], self.recv.at[self.chunk, recv], self.partner).wait_recv()

    def own(self, part, phase, ahead):
        where = ring_pos(self.at, part, phase, ahead)
        done = ORDERS[part][:phase]
        rows = rows_of(where, done)
        width = WIDE if "y" in done else WIDE // 4
        base = 0 if "y" in done else where["y"] * width
        return (self.chunk, part, rows[0], rows[1], slice(None), pl.ds(pl.multiple_of(base, width), width))

    def whole(self, part, phase):
        done = ORDERS[part][:phase]
        rows = rows_of(self.at, done)
        width = WIDE if "y" in done else WIDE // 4
        base = self.chunk * 2 * WIDE + self.at["c"] * WIDE + (0 if "y" in done else self.at["y"] * width)
        return (0, part, rows[0], rows[1], slice(None), pl.ds(pl.multiple_of(base, width), width))

    def swap(self):
        self.push(self.out.at[self.chunk], self.theirs.at[self.chunk], 0, 0, self.partner)

    def total(self, part, phase, arrived):
        sums = self.acc[self.own(part, phase, 0)].astype(F32)
        for n in range(3):
            sums = sums + self.ins[arrived][part][self.chunk, n].astype(F32)
        return sums

    def hand_on(self, part, phase):
        for n in (2, 1, 3):
            self.push(self.acc.at[self.own(part, phase, n if phase else 0)], self.ins[phase][part].at[self.chunk, n - 1],
                      1 if phase == 2 else 2, 3 - phase, ring_step(self.at, part, phase, n))

    def first(self):
        self.landed(self.theirs.at[self.chunk], 0)

        def rows(n, carry):
            part, z = lax.div(n, 4), lax.rem(n, 4)
            mine = self.acc[self.chunk, part, z].astype(F32) + self.theirs[self.chunk, part, z].astype(F32)
            self.acc[self.chunk, part, z] = mine.astype(BF)
            return carry
        lax.fori_loop(0, 12, rows, 0)
        for part in range(3):
            self.hand_on(part, 2)

    def first_end(self):
        self.landed(self.acc.at[self.chunk, :, 0:3], 1)
        for part in range(3):
            self.acc[self.own(part, 2, 0)] = self.total(part, 2, 2).astype(BF)
            self.hand_on(part, 1)

    def second_end(self):
        self.landed(self.acc.at[self.chunk, :, 0:3, 0:1], 2)
        for part in range(3):
            self.acc[self.own(part, 1, 0)] = self.total(part, 1, 1).astype(BF)
            for n in (2, 1, 3):
                self.push(self.acc.at[self.own(part, 1, 0)], self.ins[0][part].at[self.chunk, n - 1], 2, 3,
                          ring_step(self.at, part, 0, n))

    def third_end(self):
        self.landed(self.acc.at[self.chunk, :, 0:3, 0:1], 3)
        for part in range(3):
            block = self.whole(part, 1)
            self.buf[block] = self.total(part, 1, 0).astype(BF)
            for n in (2, 1, 3):
                self.push(self.buf.at[block], self.buf.at[block], 2, 4, ring_step(self.at, part, 1, n))

    def fourth_end(self):
        self.landed(self.acc.at[self.chunk, :, 0:3, 0:1], 4)
        for n in (2, 1, 3):
            for part in range(3):
                block = self.buf.at[self.whole(part, 2)]
                self.push(block, block, 1, 5, ring_step(self.at, part, 2, n))

    def fifth_end(self):
        self.landed(self.acc.at[self.chunk, :, 0:3], 5)
        base = self.chunk * 2 * WIDE + self.at["c"] * WIDE
        block = self.buf.at[0, :, :, :, :, pl.ds(pl.multiple_of(base, WIDE), WIDE)]
        self.push(block, block, 0, 6, self.partner)

    def done(self):
        self.landed(self.acc.at[self.chunk], 6)


def reduces_sent(buf, send, recv, to):
    for sem, ref in enumerate((buf.at[0], buf.at[0, :, 0:3], buf.at[0, :, 0:3, 0:3, :, 0:2048])):
        remote(ref, ref, send.at[sem], recv.at[0, 0], to).wait_send()


def peer(at, n):
    u = lax.rem(lax.rem(at["z"], 2) * 8 + at["y"] * 2 + at["c"] + n, 16)
    return dict(x=at["x"], z=lax.div(at["z"], 2) * 2 + lax.div(u, 8), y=lax.rem(lax.div(u, 2), 4), c=lax.rem(u, 2)), u


def friends(at):
    out = [peer(at, n)[0] for n in range(1, 16)] + [moved(at, x=n) for n in (1, 2, 3)]
    low = lax.rem(at["z"], 2)
    return out + [dict(at, z=lax.rem(at["z"] - low + n, 4)) for n in (2, 3)]


def greet_signal(others):
    barrier = pltpu.get_barrier_semaphore()
    for to in others:
        pl.semaphore_signal(barrier, inc=1, device_id=device(to), device_id_type=MESH)


def greet_wait(others):
    pl.semaphore_wait(pltpu.get_barrier_semaphore(), len(others))


def pack_rows(xf_ref, xq_ref, ids_ref, route_ref, rows_f, packed):
    lane = lax.broadcasted_iota(jnp.int32, (6, 128), 1)
    base = lax.broadcasted_iota(jnp.int32, (6, 128), 0) * 16
    dense = jnp.zeros((6, 128), F32)
    for k in range(8):
        dense = dense + jnp.where(lane == base + ids_ref[:, k:k + 1], route_ref[:, k:k + 1], 0.0)
    weights = jnp.sum(dense, axis=0, keepdims=True)
    rest = weights - weights.astype(BF).astype(F32)
    rows_f[0:6, :] = xf_ref[...].astype(F32)
    rows_f[8:14, :] = xq_ref[...].astype(F32)
    for n in range(8):
        rows_f[6:7, 512 * n:512 * n + 128] = weights
        rows_f[7:8, 512 * n:512 * n + 128] = rest
    packed[...] = rows_f[...].astype(BF)


def turn_start(at, packed, stage, sems):
    mine = at["c"] * 4 + at["y"]
    for n in (4, 5, 2, 3, 6, 7, 1):
        to = moved(at, y=n // 2, c=n % 2)
        remote(packed.at[:, columns(to["y"], to["c"], False)], stage.at[mine], sems.at[0], sems.at[1], to).start()
    stage[mine] = packed[:, columns(at["y"], at["c"], False)]


def both_wait(ref, sems, to):
    cp = remote(ref, ref, sems.at[0], sems.at[1], to)
    cp.wait_recv()
    cp.wait_send()


def turn_end(at, stage, spread, xb, wb, sems):
    both_wait(stage.at[0:7], sems, moved(at, c=1))
    for j in range(8):
        for q in range(4):
            spread[q * 128 + 16 * j:q * 128 + 16 * j + 16, :] = stage[j, :, 128 * q:128 * q + 128].astype(F32)
    cols = columns(at["y"], at["c"], False)
    for mat in range(2):
        for part in range(3):
            rows = [
                jnp.concatenate(
                    [spread[pl.ds(q * 128 + 8 * mat + 2 * part + r, 8, stride=16), :] for q in range(4)], axis=1)
                for r in range(2)
            ]
            xb[mat, part, at["z"], at["x"], :, cols] = jnp.concatenate(rows, axis=0).astype(BF)
    split = [spread[pl.ds(6 + r, 8, stride=16), :] for r in range(2)]
    wb[at["x"], at["z"]] = jnp.concatenate(split, axis=0).astype(BF)


def route_start(at, wb, axis, sems):
    for n in (2, 1, 3):
        idx = (at["x"], at["z"]) if axis == "z" else (at["x"],)
        remote(wb.at[idx], wb.at[idx], sems.at[0], sems.at[1], moved(at, **{axis: n})).start()


def route_end(at, wb, axis, sems):
    both_wait(wb.at[0, 0:3] if axis == "z" else wb.at[0:3], sems, moved(at, c=1))


def unit_cols(u):
    return pl.ds(pl.multiple_of(u * 256, 256), 256)


def stats_local(down_ref, most):
    for e in range(2):
        w = down_ref[e].astype(F32)
        most[e:e + 1, :] = jnp.max(w, axis=0, keepdims=True)
        most[2 + e:3 + e, :] = -jnp.min(w, axis=0, keepdims=True)
    most[4:8, :] = jnp.zeros((4, D), F32)


def spread_start(at, src, dst, sems):
    for n in range(1, 16):
        to, u = peer(at, n)
        remote(src.at[:, unit_cols(u)], dst.at[n], sems.at[0], sems.at[1], to).start()


def spread_end(at, dst, sems):
    both_wait(dst.at[1:16], sems, moved(at, c=1))


def stats_share(at, most, fin, inbox, sems):
    _, me = peer(at, 0)
    top = most[:, unit_cols(me)]
    for n in range(1, 16):
        top = jnp.maximum(top, inbox[n])
    fin[:, unit_cols(me)] = top
    for n in range(1, 16):
        to, _ = peer(at, n)
        remote(fin.at[:, unit_cols(me)], fin.at[:, unit_cols(me)], sems.at[0], sems.at[1], to).start()


HI = lax.Precision.HIGHEST


def nt(a, b, **kw):
    return lax.dot_general(a, b, (((1,), (1,)), ((), ())), preferred_element_type=F32, **kw)


def tn(a, b, **kw):
    return lax.dot_general(a, b, (((0,), (0,)), ((), ())), preferred_element_type=F32, **kw)


def route_rows(wb, w2):
    g = lax.axis_index("grp")
    both = (wb[:, :, 0:8, :].astype(F32) + wb[:, :, 8:16, :].astype(F32)).reshape(128, 128)
    row8 = lax.broadcasted_iota(jnp.int32, (8, 128), 0)
    lane8 = lax.broadcasted_iota(jnp.int32, (8, 128), 1)
    m = lax.broadcasted_iota(jnp.int32, (128, 256), 0)
    n = lax.broadcasted_iota(jnp.int32, (128, 256), 1)
    home = ((m >> 3) & 3) * 64 + (m >> 5) * 16 + (m & 7)
    for part in range(3):
        total = jnp.zeros((8, 256), F32)
        for r in range(2):
            pick = ((lane8 == (2 * part + r) * 16 + 2 * g + row8) & (row8 < 2)).astype(F32)
            chosen = nt(pick, both, precision=HI)
            move = (n == home + 8 * r).astype(F32)
            total = total + jnp.dot(chosen, move, preferred_element_type=F32, precision=HI)
        w2[0:96, 256 * part:256 * part + 256] = jnp.broadcast_to(total[0:1], (96, 256))
        w2[96:192, 256 * part:256 * part + 256] = jnp.broadcast_to(total[1:2], (96, 256))


def to_column(row):
    n = row.shape[1]
    eye = lax.broadcasted_iota(jnp.int32, (n, n), 0) == lax.broadcasted_iota(jnp.int32, (n, n), 1)
    return jnp.sum(jnp.where(eye, jnp.broadcast_to(row, (n, n)), 0.0), axis=1, keepdims=True)


def to_row(col):
    n = col.shape[0]
    eye = lax.broadcasted_iota(jnp.int32, (n, n), 0) == lax.broadcasted_iota(jnp.int32, (n, n), 1)
    return jnp.sum(jnp.where(eye, jnp.broadcast_to(col, (n, n)), 0.0), axis=0, keepdims=True)


def scales(upper, lower, top, low):
    high_end = jax.nn.sigmoid(upper) * top
    low_end = jax.nn.sigmoid(lower) * low
    step = (high_end - low_end) / 15.0
    zero = jnp.floor(-low_end / step + 0.5)
    return low_end, step, zero


def quantize(w, step, inv, zero):
    v = w * inv
    q = jnp.floor(v + 0.5)
    lev = jnp.clip(q, -zero, 15.0 - zero)
    m = jnp.clip(8.0 - jnp.abs(q + zero - 7.5), 0.0, 1.0)
    return lev * step, lev - m * v, m - 1.0


def quant_rows(w_ref, clip_ref, side, ws, keep):
    for e in range(2):
        keep[side, 0, 96 * e:96 * e + 96, :] = to_column(clip_ref[0, e:e + 1, :])
        keep[side, 1, 96 * e:96 * e + 96, :] = to_column(clip_ref[1, e:e + 1, :])

    def rows(n, carry):
        here = pl.ds(pl.multiple_of(n * 16, 16), 16)
        line = pl.ds(pl.multiple_of(192 * side + n * 16, 16), 16)
        w = w_ref[line, :].astype(F32)
        top = jnp.max(w, axis=1, keepdims=True)
        low = jnp.min(w, axis=1, keepdims=True)
        keep[side, 2, here, :] = top
        keep[side, 3, here, :] = low
        _, step, zero = scales(keep[side, 0, here, :], keep[side, 1, here, :], top, low)
        inv = 1.0 / step

        def cols(k, carry):
            c = pl.ds(pl.multiple_of(k * 512, 512), 512)
            made = quantize(w_ref[line, c].astype(F32), step, inv, zero)
            for i, a in enumerate(made):
                ws[pl.ds(pl.multiple_of(384 * i + 192 * side + n * 16, 16), 16), c] = a.astype(BF)
            return carry
        return lax.fori_loop(0, 8, cols, carry)
    lax.fori_loop(0, 12, rows, 0)


def quant_down(w_ref, clip_ref, most, wd):
    for e in range(2):
        def cols(n, carry):
            c = pl.ds(pl.multiple_of(n * 512, 512), 512)
            _, step, zero = scales(clip_ref[0, e:e + 1, c], clip_ref[1, e:e + 1, c], most[e:e + 1, c], -most[2 + e:3 + e, c])
            inv = 1.0 / step

            def rows(k, carry):
                r = pl.ds(pl.multiple_of(k * 16, 16), 16)
                val, slope, zs = quantize(w_ref[e, r, c].astype(F32), step, inv, zero)
                for i, a in enumerate((val, slope, zs)):
                    wd[i, e, r, c] = a.astype(BF)
                return carry
            return lax.fori_loop(0, 6, rows, carry)
        lax.fori_loop(0, 8, cols, 0)


def silu(v):
    return v * jax.nn.sigmoid(v)


def tokens(xb, mat, part):
    return xb[mat, part].reshape(256, D)


def part_cols(part):
    return pl.ds(256 * part, 256)


def teacher(xb, part, w_ref, w2, hid):
    cols = part_cols(part)
    gu = nt(w_ref[...], tokens(xb, 0, part))
    hid[part, 192:384, :] = (-(silu(gu[0:192]) * gu[192:384] * w2[:, cols])).astype(BF)


def student(xb, part, ws, w2, hid, sgu):
    cols = part_cols(part)
    gu = nt(ws[0:384, :], tokens(xb, 1, part))
    sgu[:, cols] = gu
    hid[part, 0:192, :] = (silu(gu[0:192]) * gu[192:384] * w2[:, cols]).astype(BF)


def difference(at, chunk, hid, wd, down_ref, acc, out):
    for dst, core in ((out, 1 - at["c"]), (acc, at["c"])):
        c = pl.ds(pl.multiple_of(chunk * 2 * WIDE + core * WIDE, WIDE), WIDE)
        w = jnp.concatenate([wd[0, :, :, c].reshape(192, WIDE), down_ref[:, :, c].reshape(192, WIDE)], axis=0)

        def body(part, carry):
            h = hid[part]
            dst[chunk, part] = tn(h, w).astype(BF).reshape(4, 4, 16, WIDE)
            return carry
        lax.fori_loop(0, 3, body, 0)


def factors(xb, part, kind, ws, w2, sgu, fac):
    cols = part_cols(part)
    a = nt(ws[384 + 384 * kind:768 + 384 * kind, :], tokens(xb, 1, part))
    g, u = sgu[0:192, cols], sgu[192:384, cols]
    s = jax.nn.sigmoid(g)
    fac[kind, :, cols] = w2[:, cols] * u * s * (1.0 + g * (1.0 - s)) * a[0:192]
    fac[2 + kind, :, cols] = w2[:, cols] * g * s * a[192:384]


def back(chunk, xb, hid, wd, clip_ref, most, dh, grad):
    k = pl.ds(chunk * 2 * WIDE, 2 * WIDE)
    w = wd[0, :, :, k].reshape(192, 2 * WIDE)
    for part in range(3):
        new = nt(w, xb[0, part, :, :, :, k].reshape(256, 2 * WIDE))
        cols = part_cols(part)
        dh[:, cols] = new if chunk == 0 else dh[:, cols] + new

    def cols(n, carry):
        c = pl.ds(pl.multiple_of(chunk * 2 * WIDE + n * 512, 512), 512)
        dq = jnp.zeros((192, 512), F32)
        for part in range(3):
            dq = dq + jnp.dot(hid[part, 0:192, :], xb[0, part, :, :, :, c].reshape(256, 512), preferred_element_type=F32)
        for e in range(2):
            d = dq[96 * e:96 * e + 96]
            s1 = jnp.sum(d * wd[1, e, :, c].astype(F32), axis=0, keepdims=True)
            s2 = jnp.sum(d * wd[2, e, :, c].astype(F32), axis=0, keepdims=True)
            du, dl = slopes(s1, s2, clip_ref[0, e:e + 1, c], clip_ref[1, e:e + 1, c], most[e:e + 1, c], -most[2 + e:3 + e, c])
            grad[e:e + 1, c] = du
            grad[2 + e:3 + e, c] = dl
        return carry
    lax.fori_loop(0, WIDE // 256, cols, 0)


def slopes(s1, s2, upper, lower, top, low):
    low_end, step, _ = scales(upper, lower, top, low)
    d_step = s1 + s2 * low_end / step
    d_high = d_step / 15.0
    d_low = -s2 - d_high
    su, sl = jax.nn.sigmoid(upper), jax.nn.sigmoid(lower)
    return d_high * top * su * (1.0 - su), d_low * low * sl * (1.0 - sl)


def row_grads(side, fac, dh, keep, out):
    sums = [jnp.sum(fac[2 * side + k] * dh[...], axis=1, keepdims=True) for k in range(2)]
    du, dl = slopes(sums[0], sums[1], *[keep[side, n] for n in range(4)])
    for e in range(2):
        out[0, e:e + 1, :] = to_row(du[96 * e:96 * e + 96, :])
        out[1, e:e + 1, :] = to_row(dl[96 * e:96 * e + 96, :])


def kernel(xf_ref, xq_ref, ids_ref, route_ref, gate_hbm, up_hbm, down_hbm, gc, uc, dc, g_out, u_out, d_out,
           xb, wb, packed, stage, rows_f, spread, raw, down, most, fin, inbox, grad, d_inbox, ws, wd, hid, sgu, w2, keep,
           fac, dh, acc, out, theirs, *rest):
    a_in, b_in, c_in = (rest[3 * k:3 * k + 3] for k in range(3))
    l_s, t_s, z_s, x_s, m_s, n_s, d_s, ag_s, ag_r, rs_s, rs_r = rest[9:]
    at = place()
    loads = [pltpu.make_async_copy(down_hbm, down, l_s.at[0])]
    for side, src in enumerate((gate_hbm, up_hbm)):
        for e in range(2):
            lines = pl.ds(192 * side + 96 * e, 96)
            loads.append(pltpu.make_async_copy(src.at[e], raw.at[lines], l_s.at[1 + 2 * side + e]))
    others = friends(at)
    greet_signal(others)
    for cp in loads:
        cp.start()
    pack_rows(xf_ref, xq_ref, ids_ref, route_ref, rows_f, packed)
    greet_wait(others)
    turn_start(at, packed, stage, t_s)
    loads[0].wait()
    stats_local(down, most)
    spread_start(at, most, inbox, m_s)
    turn_end(at, stage, spread, xb, wb, t_s)
    fp, q = (Gather(at, xb, mat, ag_s, ag_r.at[mat]) for mat in range(2))
    fp.spread(0)
    q.spread(0)
    route_start(at, wb, "z", z_s)
    for cp in loads[1:3]:
        cp.wait()
    quant_rows(raw, gc, 0, ws, keep)
    fp.spread_wait(0)
    fp.spread(1)
    q.spread_wait(0)
    q.spread(1)
    route_end(at, wb, "z", z_s)
    route_start(at, wb, "x", x_s)
    spread_end(at, inbox, m_s)
    stats_share(at, most, fin, inbox, n_s)
    for cp in loads[3:5]:
        cp.wait()
    quant_rows(raw, uc, 1, ws, keep)
    fp.spread_wait(1)
    fp.last()
    route_end(at, wb, "x", x_s)
    route_rows(wb, w2)
    fp.last_mid()
    q.spread_wait(1)
    q.last()
    both_wait(inbox.at[1:16], n_s, moved(at, c=1))
    quant_down(down, dc, fin, wd)
    fp.last_near()
    q.last_mid()
    fp.last_far()
    fp.finish()
    for p in range(3):
        teacher(xb, p, raw, w2, hid)
    q.last_near()
    q.last_far()
    q.finish()
    gathers_sent(xb, ag_s, ag_r.at[0], moved(at, c=1))
    red = [Reduce(at, k, acc, out, theirs, a_in, b_in, c_in, xb, rs_s, rs_r) for k in range(CHUNKS)]
    for p in range(3):
        student(xb, p, ws, w2, hid, sgu)
    grad[4:8, :] = jnp.zeros((4, D), F32)
    difference(at, 0, hid, wd, down, acc, out)
    red[0].swap()
    difference(at, 1, hid, wd, down, acc, out)
    red[1].swap()
    red[0].first()
    difference(at, 2, hid, wd, down, acc, out)
    red[2].swap()
    red[1].first()
    difference(at, 3, hid, wd, down, acc, out)
    red[3].swap()
    red[2].first()
    red[3].first()
    factors(xb, 0, 0, ws, w2, sgu, fac)
    red[0].first_end()
    factors(xb, 0, 1, ws, w2, sgu, fac)
    red[1].first_end()
    red[0].second_end()
    factors(xb, 1, 0, ws, w2, sgu, fac)
    red[2].first_end()
    red[1].second_end()
    factors(xb, 1, 1, ws, w2, sgu, fac)
    red[3].first_end()
    red[0].third_end()
    red[2].second_end()
    factors(xb, 2, 0, ws, w2, sgu, fac)
    red[1].third_end()
    red[0].fourth_end()
    red[3].second_end()
    factors(xb, 2, 1, ws, w2, sgu, fac)
    red[2].third_end()
    red[1].fourth_end()
    red[0].fifth_end()
    red[3].third_end()
    red[2].fourth_end()
    red[1].fifth_end()
    red[0].done()
    back(0, xb, hid, wd, dc, fin, dh, grad)
    red[3].fourth_end()
    red[2].fifth_end()
    red[1].done()
    back(1, xb, hid, wd, dc, fin, dh, grad)
    red[3].fifth_end()
    red[2].done()
    back(2, xb, hid, wd, dc, fin, dh, grad)
    red[3].done()
    back(3, xb, hid, wd, dc, fin, dh, grad)
    spread_start(at, grad, d_inbox, d_s)
    row_grads(0, fac, dh, keep, g_out)
    row_grads(1, fac, dh, keep, u_out)
    reduces_sent(xb, rs_s, rs_r, moved(at, c=1))
    spread_end(at, d_inbox, d_s)
    _, me = peer(at, 0)
    total = grad[:, unit_cols(me)]
    for n in range(1, 16):
        total = total + d_inbox[n]
    for k in range(2):
        d_out[k] = total[2 * k:2 * k + 2]


SEM = pltpu.SemaphoreType.DMA
VM = pl.BlockSpec(memory_space=pltpu.VMEM)
ANY = pl.BlockSpec(memory_space=pl.ANY)


def sds(shape, dt):
    return jax.ShapeDtypeStruct(shape, dt)


def hand_over(a, b, c, x, y, z):
    x[...] = a[...]
    y[...] = b[...]
    z[...] = c[...]


def on_device(x_fp, x_q, expert_ids, route_weight, gate_weight, up_weight, down_weight, gate_clip, up_clip, down_clip):
    scratch = [((2, 3, 4, 4, 16, D), BF), ((4, 4, 16, 128), BF), ((16, D), BF), ((8, 16, 512), BF), ((16, D), F32),
               ((512, 128), F32), ((384, D), BF), ((2, 96, D), BF), ((8, D), F32), ((8, D), F32), ((16, 8, 256), F32),
               ((8, D), F32), ((16, 8, 256), F32), ((1152, D), BF), ((3, 2, 96, D), BF), ((3, 384, 256), BF), ((384, 768), F32),
               ((192, 768), F32), ((2, 4, 192, 1), F32), ((4, 192, 768), F32), ((192, 768), F32)]
    scratch += [((CHUNKS, 3, 4, 4, 16, WIDE), BF)] * 3
    scratch += [((CHUNKS, 3) + phase_shape(p, phase), BF) for phase in (2, 1, 1) for p in range(3)]
    outs = (sds((2, 2, 96), F32), sds((2, 2, 96), F32), sds((2, 2, 256), F32))
    made = pl.pallas_call(
        kernel,
        out_shape=outs,
        in_specs=[VM] * 4 + [ANY] * 3 + [VM] * 3,
        out_specs=(VM,) * 3,
        scratch_shapes=[pltpu.VMEM(s, t) for s, t in scratch] + [SEM((5,))] + [SEM((2,))] * 6 + [
            SEM((3,)), SEM((2, 6)), SEM((3,)), SEM((CHUNKS, 7))],
        compiler_params=pltpu.CompilerParams(collective_id=0, has_side_effects=True, vmem_limit_bytes=62 << 20),
    )(x_fp, x_q, expert_ids, route_weight, gate_weight, up_weight, down_weight, gate_clip, up_clip, down_clip)
    return pl.pallas_call(hand_over, out_shape=outs, in_specs=[VM] * 3, out_specs=(VM,) * 3)(*made)


def solution(mesh):
    token = P(("grp", "unit"), None)
    weight = P("grp", "unit", None)
    clip = P(None, "grp", "unit")
    return jax.shard_map(
        on_device,
        mesh=mesh,
        in_specs=(token,) * 4 + (weight,) * 3 + (clip, clip, P(None, "grp", None)),
        out_specs=(clip,) * 3,
        check_vma=False,
    )
```

```python
import jax
import jax.numpy as jnp
from jax import lax
from jax.experimental import pallas as pl
from jax.experimental.pallas import tpu as pltpu
from jax.sharding import PartitionSpec as P

MESH = pl.DeviceIdType.MESH
D = 4096
BF = jnp.bfloat16
F32 = jnp.float32
ORDERS = ("xyz", "yzx", "zxy")
CHUNKS = 4
WIDE = 2048 // CHUNKS


def place():
    g, u = lax.axis_index("grp"), lax.axis_index("unit")
    x, z = lax.div(g, 2), lax.rem(g, 2) * 2 + lax.div(u, 8)
    y, c = lax.rem(lax.div(u, 2), 4), lax.rem(u, 2)
    return dict(x=x, y=y, z=z, c=c)


def device(at):
    return (at["x"] * 2 + lax.div(at["z"], 2), lax.rem(at["z"], 2) * 8 + at["y"] * 2 + at["c"])


def moved(at, **by):
    out = dict(at)
    for axis, step in by.items():
        out[axis] = lax.rem(at[axis] + step, 2 if axis == "c" else 4)
    return out


def remote(src, dst, send, recv, to):
    return pltpu.make_async_remote_copy(
        src_ref=src, dst_ref=dst, send_sem=send, recv_sem=recv, device_id=device(to), device_id_type=MESH)


def columns(y, c, full):
    if full:
        return pl.ds(pl.multiple_of(c * 2048, 2048), 2048)
    return pl.ds(pl.multiple_of(c * 2048 + y * 512, 512), 512)


def rows_of(at, done):
    return [slice(None) if a in done else pl.ds(at[a], 1) for a in "zx"]


def ring_pos(at, part, phase, ahead):
    axis = ORDERS[part][phase]
    return dict(at, **{axis: lax.rem(at[axis] + ahead, 4)})


def ring_step(at, part, phase, n):
    return moved(at, **{ORDERS[part][phase]: n})


class Gather:
    def __init__(self, at, buf, mat, send, recv):
        self.at, self.buf, self.mat = at, buf, mat
        self.send, self.recv = send, recv
        self.partner = moved(at, c=1)

    def block(self, part, phase, ahead, half=None, at=None):
        where = ring_pos(at or self.at, part, phase, ahead)
        done = ORDERS[part][:phase]
        width = 2048 if "y" in done else 512
        base = where["c"] * 2048 + (0 if "y" in done else where["y"] * 512)
        if half is not None:
            width = width // 2
            base = base + half * width
        rows = rows_of(where, done)
        return self.buf.at[self.mat, part, rows[0], rows[1], :, pl.ds(pl.multiple_of(base, width), width)]

    def push(self, ref, send, recv, to):
        remote(ref, ref, self.send.at[send], self.recv.at[recv], to).start()

    def landed(self, ref, recv):
        remote(ref, ref, self.send.at[0], self.recv.at[recv], self.partner).wait_recv()

    def spread(self, phase):
        for n in (2, 1, 3):
            for part in range(3):
                self.push(self.block(part, phase, 0), 0, phase, ring_step(self.at, part, phase, n))

    def spread_wait(self, phase):
        self.landed(self.buf.at[self.mat, :, 0:3, 0:1, :, 0:(512, 2048)[phase]], phase)

    def last(self):
        for swap in (0, 1):
            for part in range(3):
                for side, step in ((0, 1), (1, 3)):
                    self.push(self.block(part, 2, 0, side ^ swap), 1, 2 + swap, ring_step(self.at, part, 2, step))
        for part in range(3):
            self.push(self.block(part, 2, 0), 2, 5, self.partner)

    def last_mid(self):
        self.landed(self.buf.at[self.mat, :, 0:2, 0:1], 2)
        for part in range(3):
            for side, step in ((0, 1), (1, 3)):
                self.push(self.block(part, 2, 4 - step, side), 1, 4, ring_step(self.at, part, 2, step))

    def last_near(self):
        self.landed(self.buf.at[self.mat, :, 0:2, 0:1], 3)
        for part in range(3):
            for step in (1, 3):
                self.push(self.block(part, 2, step), 2, 5, self.partner)

    def last_far(self):
        self.landed(self.buf.at[self.mat, :, 0:2, 0:1], 4)
        for part in range(3):
            self.push(self.block(part, 2, 2), 2, 5, self.partner)

    def finish(self):
        self.landed(self.buf.at[self.mat, :, 0:2], 5)


def gathers_sent(buf, send, recv, to):
    for sem, ref in enumerate((buf.at[0, :, 0:3, 0:2, :, 0:2560], buf.at[0, :, 0:3, :], buf.at[0])):
        remote(ref, ref, send.at[sem], recv.at[0], to).wait_send()


def phase_shape(part, phase):
    done = ORDERS[part][:phase]
    return (4 if "z" in done else 1, 4 if "x" in done else 1, 16, WIDE if "y" in done else WIDE // 4)


class Reduce:
    def __init__(self, at, chunk, acc, out, theirs, a_in, b_in, c_in, buf, send, recv):
        self.at, self.chunk, self.acc, self.out, self.theirs = at, chunk, acc, out, theirs
        self.ins = {2: a_in, 1: b_in, 0: c_in}
        self.buf, self.send, self.recv = buf, send, recv
        self.partner = moved(at, c=1)

    def push(self, src, dst, send, recv, to):
        remote(src, dst, self.send.at[send], self.recv.at[self.chunk, recv], to).start()

    def landed(self, ref, recv):
        remote(ref, ref, self.send.at[0], self.recv.at[self.chunk, recv], self.partner).wait_recv()

    def own(self, part, phase, ahead):
        where = ring_pos(self.at, part, phase, ahead)
        done = ORDERS[part][:phase]
        rows = rows_of(where, done)
        width = WIDE if "y" in done else WIDE // 4
        base = 0 if "y" in done else where["y"] * width
        return (self.chunk, part, rows[0], rows[1], slice(None), pl.ds(pl.multiple_of(base, width), width))

    def whole(self, part, phase):
        done = ORDERS[part][:phase]
        rows = rows_of(self.at, done)
        width = WIDE if "y" in done else WIDE // 4
        base = self.chunk * 2 * WIDE + self.at["c"] * WIDE + (0 if "y" in done else self.at["y"] * width)
        return (0, part, rows[0], rows[1], slice(None), pl.ds(pl.multiple_of(base, width), width))

    def swap(self):
        self.push(self.out.at[self.chunk], self.theirs.at[self.chunk], 0, 0, self.partner)

    def total(self, part, phase, arrived):
        sums = self.acc[self.own(part, phase, 0)].astype(F32)
        for n in range(3):
            sums = sums + self.ins[arrived][part][self.chunk, n].astype(F32)
        return sums

    def hand_on(self, part, phase):
        for n in (2, 1, 3):
            self.push(self.acc.at[self.own(part, phase, n if phase else 0)], self.ins[phase][part].at[self.chunk, n - 1],
                      1 if phase == 2 else 2, 3 - phase, ring_step(self.at, part, phase, n))

    def first(self):
        self.landed(self.theirs.at[self.chunk], 0)

        def rows(n, carry):
            part, z = lax.div(n, 4), lax.rem(n, 4)
            mine = self.acc[self.chunk, part, z].astype(F32) + self.theirs[self.chunk, part, z].astype(F32)
            self.acc[self.chunk, part, z] = mine.astype(BF)
            return carry
        lax.fori_loop(0, 12, rows, 0)
        for part in range(3):
            self.hand_on(part, 2)

    def first_end(self):
        self.landed(self.acc.at[self.chunk, :, 0:3], 1)
        for part in range(3):
            self.acc[self.own(part, 2, 0)] = self.total(part, 2, 2).astype(BF)
            self.hand_on(part, 1)

    def second_end(self):
        self.landed(self.acc.at[self.chunk, :, 0:3, 0:1], 2)
        for part in range(3):
            self.acc[self.own(part, 1, 0)] = self.total(part, 1, 1).astype(BF)
            for n in (2, 1, 3):
                self.push(self.acc.at[self.own(part, 1, 0)], self.ins[0][part].at[self.chunk, n - 1], 2, 3,
                          ring_step(self.at, part, 0, n))

    def third_end(self):
        self.landed(self.acc.at[self.chunk, :, 0:3, 0:1], 3)
        for part in range(3):
            block = self.whole(part, 1)
            self.buf[block] = self.total(part, 1, 0).astype(BF)
            for n in (2, 1, 3):
                self.push(self.buf.at[block], self.buf.at[block], 2, 4, ring_step(self.at, part, 1, n))

    def fourth_end(self):
        self.landed(self.acc.at[self.chunk, :, 0:3, 0:1], 4)
        for n in (2, 1, 3):
            for part in range(3):
                block = self.buf.at[self.whole(part, 2)]
                self.push(block, block, 1, 5, ring_step(self.at, part, 2, n))

    def fifth_end(self):
        self.landed(self.acc.at[self.chunk, :, 0:3], 5)
        base = self.chunk * 2 * WIDE + self.at["c"] * WIDE
        block = self.buf.at[0, :, :, :, :, pl.ds(pl.multiple_of(base, WIDE), WIDE)]
        self.push(block, block, 0, 6, self.partner)

    def done(self):
        self.landed(self.acc.at[self.chunk], 6)


def reduces_sent(buf, send, recv, to):
    for sem, ref in enumerate((buf.at[0], buf.at[0, :, 0:3], buf.at[0, :, 0:3, 0:3, :, 0:2048])):
        remote(ref, ref, send.at[sem], recv.at[0, 0], to).wait_send()


def peer(at, n):
    u = lax.rem(lax.rem(at["z"], 2) * 8 + at["y"] * 2 + at["c"] + n, 16)
    return dict(x=at["x"], z=lax.div(at["z"], 2) * 2 + lax.div(u, 8), y=lax.rem(lax.div(u, 2), 4), c=lax.rem(u, 2)), u


def friends(at):
    out = [peer(at, n)[0] for n in range(1, 16)] + [moved(at, x=n) for n in (1, 2, 3)]
    low = lax.rem(at["z"], 2)
    return out + [dict(at, z=lax.rem(at["z"] - low + n, 4)) for n in (2, 3)]


def greet_signal(others):
    barrier = pltpu.get_barrier_semaphore()
    for to in others:
        pl.semaphore_signal(barrier, inc=1, device_id=device(to), device_id_type=MESH)


def greet_wait(others):
    pl.semaphore_wait(pltpu.get_barrier_semaphore(), len(others))


def pack_rows(xf_ref, xq_ref, ids_ref, route_ref, rows_f, packed):
    lane = lax.broadcasted_iota(jnp.int32, (6, 128), 1)
    base = lax.broadcasted_iota(jnp.int32, (6, 128), 0) * 16
    dense = jnp.zeros((6, 128), F32)
    for k in range(8):
        dense = dense + jnp.where(lane == base + ids_ref[:, k:k + 1], route_ref[:, k:k + 1], 0.0)
    weights = jnp.sum(dense, axis=0, keepdims=True)
    rest = weights - weights.astype(BF).astype(F32)
    rows_f[0:6, :] = xf_ref[...].astype(F32)
    rows_f[8:14, :] = xq_ref[...].astype(F32)
    for n in range(8):
        rows_f[6:7, 512 * n:512 * n + 128] = weights
        rows_f[7:8, 512 * n:512 * n + 128] = rest
    packed[...] = rows_f[...].astype(BF)


def turn_start(at, packed, stage, sems):
    mine = at["c"] * 4 + at["y"]
    for n in (4, 5, 2, 3, 6, 7, 1):
        to = moved(at, y=n // 2, c=n % 2)
        remote(packed.at[:, columns(to["y"], to["c"], False)], stage.at[mine], sems.at[0], sems.at[1], to).start()
    stage[mine] = packed[:, columns(at["y"], at["c"], False)]


def both_wait(ref, sems, to):
    cp = remote(ref, ref, sems.at[0], sems.at[1], to)
    cp.wait_recv()
    cp.wait_send()


def turn_end(at, stage, spread, xb, wb, sems):
    both_wait(stage.at[0:7], sems, moved(at, c=1))
    for j in range(8):
        for q in range(4):
            spread[q * 128 + 16 * j:q * 128 + 16 * j + 16, :] = stage[j, :, 128 * q:128 * q + 128].astype(F32)
    cols = columns(at["y"], at["c"], False)
    for mat in range(2):
        for part in range(3):
            rows = [
                jnp.concatenate(
                    [spread[pl.ds(q * 128 + 8 * mat + 2 * part + r, 8, stride=16), :] for q in range(4)], axis=1)
                for r in range(2)
            ]
            xb[mat, part, at["z"], at["x"], :, cols] = jnp.concatenate(rows, axis=0).astype(BF)
    split = [spread[pl.ds(6 + r, 8, stride=16), :] for r in range(2)]
    wb[at["x"], at["z"]] = jnp.concatenate(split, axis=0).astype(BF)


def route_start(at, wb, axis, sems):
    for n in (2, 1, 3):
        idx = (at["x"], at["z"]) if axis == "z" else (at["x"],)
        remote(wb.at[idx], wb.at[idx], sems.at[0], sems.at[1], moved(at, **{axis: n})).start()


def route_end(at, wb, axis, sems):
    both_wait(wb.at[0, 0:3] if axis == "z" else wb.at[0:3], sems, moved(at, c=1))


def unit_cols(u):
    return pl.ds(pl.multiple_of(u * 256, 256), 256)


def stats_local(down_ref, most):
    for e in range(2):
        w = down_ref[e].astype(F32)
        most[e:e + 1, :] = jnp.max(w, axis=0, keepdims=True)
        most[2 + e:3 + e, :] = -jnp.min(w, axis=0, keepdims=True)
    most[4:8, :] = jnp.zeros((4, D), F32)


def spread_start(at, src, dst, sems):
    for n in range(1, 16):
        to, u = peer(at, n)
        remote(src.at[:, unit_cols(u)], dst.at[n], sems.at[0], sems.at[1], to).start()


def spread_end(at, dst, sems):
    both_wait(dst.at[1:16], sems, moved(at, c=1))


def stats_share(at, most, fin, inbox, sems):
    _, me = peer(at, 0)
    top = most[:, unit_cols(me)]
    for n in range(1, 16):
        top = jnp.maximum(top, inbox[n])
    fin[:, unit_cols(me)] = top
    for n in range(1, 16):
        to, _ = peer(at, n)
        remote(fin.at[:, unit_cols(me)], fin.at[:, unit_cols(me)], sems.at[0], sems.at[1], to).start()


HI = lax.Precision.HIGHEST


def nt(a, b, **kw):
    return lax.dot_general(a, b, (((1,), (1,)), ((), ())), preferred_element_type=F32, **kw)


def tn(a, b, **kw):
    return lax.dot_general(a, b, (((0,), (0,)), ((), ())), preferred_element_type=F32, **kw)


def route_rows(wb, w2):
    g = lax.axis_index("grp")
    both = (wb[:, :, 0:8, :].astype(F32) + wb[:, :, 8:16, :].astype(F32)).reshape(128, 128)
    row8 = lax.broadcasted_iota(jnp.int32, (8, 128), 0)
    lane8 = lax.broadcasted_iota(jnp.int32, (8, 128), 1)
    m = lax.broadcasted_iota(jnp.int32, (128, 256), 0)
    n = lax.broadcasted_iota(jnp.int32, (128, 256), 1)
    home = ((m >> 3) & 3) * 64 + (m >> 5) * 16 + (m & 7)
    for part in range(3):
        total = jnp.zeros((8, 256), F32)
        for r in range(2):
            pick = ((lane8 == (2 * part + r) * 16 + 2 * g + row8) & (row8 < 2)).astype(F32)
            chosen = nt(pick, both, precision=HI)
            move = (n == home + 8 * r).astype(F32)
            total = total + jnp.dot(chosen, move, preferred_element_type=F32, precision=HI)
        w2[0:96, 256 * part:256 * part + 256] = jnp.broadcast_to(total[0:1], (96, 256))
        w2[96:192, 256 * part:256 * part + 256] = jnp.broadcast_to(total[1:2], (96, 256))


def to_column(row):
    n = row.shape[1]
    eye = lax.broadcasted_iota(jnp.int32, (n, n), 0) == lax.broadcasted_iota(jnp.int32, (n, n), 1)
    return jnp.sum(jnp.where(eye, jnp.broadcast_to(row, (n, n)), 0.0), axis=1, keepdims=True)


def to_row(col):
    n = col.shape[0]
    eye = lax.broadcasted_iota(jnp.int32, (n, n), 0) == lax.broadcasted_iota(jnp.int32, (n, n), 1)
    return jnp.sum(jnp.where(eye, jnp.broadcast_to(col, (n, n)), 0.0), axis=0, keepdims=True)


def scales(upper, lower, top, low):
    high_end = jax.nn.sigmoid(upper) * top
    low_end = jax.nn.sigmoid(lower) * low
    step = (high_end - low_end) / 15.0
    zero = jnp.floor(-low_end / step + 0.5)
    return low_end, step, zero


def quantize(w, step, inv, zero):
    v = w * inv
    q = jnp.floor(v + 0.5)
    lev = jnp.clip(q, -zero, 15.0 - zero)
    m = jnp.clip(8.0 - jnp.abs(q + zero - 7.5), 0.0, 1.0)
    return lev * step, lev - m * v, m - 1.0


def quant_rows(w_ref, clip_ref, side, ws, keep, wide):
    base = 192 * side
    for e in range(2):
        keep[side, 0, 96 * e:96 * e + 96, :] = to_column(clip_ref[0, e:e + 1, :])
        keep[side, 1, 96 * e:96 * e + 96, :] = to_column(clip_ref[1, e:e + 1, :])
    for block in range(4):
        lines = pl.ds(base + 48 * block, 48)
        first = w_ref[lines, 0:128].astype(F32)

        def extremes(n, carry):
            top, low = carry
            for k in range(4):
                w = w_ref[lines, pl.ds(pl.multiple_of(n * 512 + 128 * k, 128), 128)].astype(F32)
                top, low = jnp.maximum(top, w), jnp.minimum(low, w)
            return top, low
        top, low = lax.fori_loop(0, 8, extremes, (first, first))
        keep[side, 2, 48 * block:48 * block + 48, :] = jnp.max(top, axis=1, keepdims=True)
        keep[side, 3, 48 * block:48 * block + 48, :] = jnp.min(low, axis=1, keepdims=True)
    _, step, zero = scales(*[keep[side, k] for k in range(4)])
    for k, a in enumerate((step, 1.0 / step, zero)):
        wide[k] = jnp.broadcast_to(a, (192, 128))

    def rows(n, carry):
        here = pl.ds(pl.multiple_of(n * 16, 16), 16)
        step, inv, zero = (jnp.concatenate([wide[k, here, :]] * 4, axis=1) for k in range(3))
        for c in range(8):
            w = w_ref[pl.ds(pl.multiple_of(base + n * 16, 16), 16), 512 * c:512 * c + 512].astype(F32)
            for i, a in enumerate(quantize(w, step, inv, zero)):
                ws[pl.ds(pl.multiple_of(384 * i + base + n * 16, 16), 16), 512 * c:512 * c + 512] = a.astype(BF)
        return carry
    lax.fori_loop(0, 12, rows, 0)


def quant_down(w_ref, clip_ref, most, wd):
    for e in range(2):
        def cols(n, carry):
            c = pl.ds(pl.multiple_of(n * 512, 512), 512)
            _, step, zero = scales(clip_ref[0, e:e + 1, c], clip_ref[1, e:e + 1, c], most[e:e + 1, c], -most[2 + e:3 + e, c])
            inv = 1.0 / step

            def rows(k, carry):
                r = pl.ds(pl.multiple_of(k * 16, 16), 16)
                val, slope, zs = quantize(w_ref[e, r, c].astype(F32), step, inv, zero)
                for i, a in enumerate((val, slope, zs)):
                    wd[i, e, r, c] = a.astype(BF)
                return carry
            return lax.fori_loop(0, 6, rows, carry)
        lax.fori_loop(0, 8, cols, 0)


def silu(v):
    return v * jax.nn.sigmoid(v)


def tokens(xb, mat, part):
    return xb[mat, part].reshape(256, D)


def part_cols(part):
    return pl.ds(256 * part, 256)


def teacher(xb, part, w_ref, w2, hid):
    cols = part_cols(part)
    gu = nt(w_ref[...], tokens(xb, 0, part))
    hid[part, 192:384, :] = (-(silu(gu[0:192]) * gu[192:384] * w2[:, cols])).astype(BF)


def student(xb, part, ws, w2, hid, hid_t, sgu):
    cols = part_cols(part)
    gu = nt(ws[0:384, :], tokens(xb, 1, part))
    sgu[:, cols] = gu
    hid[part, 0:192, :] = (silu(gu[0:192]) * gu[192:384] * w2[:, cols]).astype(BF)
    hid_t[part] = jnp.transpose(hid[part].astype(F32)).astype(BF)


def difference(chunk, core, hid_t, wd, down_ref, dst):
    c = pl.ds(pl.multiple_of(chunk * 2 * WIDE + core * WIDE, WIDE), WIDE)
    w = jnp.concatenate([wd[0, :, :, c].reshape(192, WIDE), down_ref[:, :, c].reshape(192, WIDE)], axis=0)
    made = jnp.dot(hid_t[...].reshape(768, 384), w, preferred_element_type=F32)
    dst[chunk] = made.astype(BF).reshape(3, 4, 4, 16, WIDE)


def factors(xb, part, kind, ws, w2, sgu, fac):
    cols = part_cols(part)
    a = nt(ws[384 + 384 * kind:768 + 384 * kind, :], tokens(xb, 1, part))
    g, u = sgu[0:192, cols], sgu[192:384, cols]
    s = jax.nn.sigmoid(g)
    fac[kind, :, cols] = w2[:, cols] * u * s * (1.0 + g * (1.0 - s)) * a[0:192]
    fac[2 + kind, :, cols] = w2[:, cols] * g * s * a[192:384]


def back(chunk, xb, hid, wd, clip_ref, most, dh, grad):
    k = pl.ds(chunk * 2 * WIDE, 2 * WIDE)
    w = wd[0, :, :, k].reshape(192, 2 * WIDE)
    for part in range(3):
        new = nt(w, xb[0, part, :, :, :, k].reshape(256, 2 * WIDE))
        cols = part_cols(part)
        dh[:, cols] = new if chunk == 0 else dh[:, cols] + new

    def cols(n, carry):
        c = pl.ds(pl.multiple_of(chunk * 2 * WIDE + n * 512, 512), 512)
        dq = jnp.zeros((192, 512), F32)
        for part in range(3):
            dq = dq + jnp.dot(hid[part, 0:192, :], xb[0, part, :, :, :, c].reshape(256, 512), preferred_element_type=F32)
        for e in range(2):
            d = dq[96 * e:96 * e + 96]
            s1 = jnp.sum(d * wd[1, e, :, c].astype(F32), axis=0, keepdims=True)
            s2 = jnp.sum(d * wd[2, e, :, c].astype(F32), axis=0, keepdims=True)
            du, dl = slopes(s1, s2, clip_ref[0, e:e + 1, c], clip_ref[1, e:e + 1, c], most[e:e + 1, c], -most[2 + e:3 + e, c])
            grad[e:e + 1, c] = du
            grad[2 + e:3 + e, c] = dl
        return carry
    lax.fori_loop(0, WIDE // 256, cols, 0)


def slopes(s1, s2, upper, lower, top, low):
    low_end, step, _ = scales(upper, lower, top, low)
    d_step = s1 + s2 * low_end / step
    d_high = d_step / 15.0
    d_low = -s2 - d_high
    su, sl = jax.nn.sigmoid(upper), jax.nn.sigmoid(lower)
    return d_high * top * su * (1.0 - su), d_low * low * sl * (1.0 - sl)


def row_grads(side, fac, dh, keep, out):
    sums = [jnp.sum(fac[2 * side + k] * dh[...], axis=1, keepdims=True) for k in range(2)]
    du, dl = slopes(sums[0], sums[1], *[keep[side, n] for n in range(4)])
    for e in range(2):
        out[0, e:e + 1, :] = to_row(du[96 * e:96 * e + 96, :])
        out[1, e:e + 1, :] = to_row(dl[96 * e:96 * e + 96, :])


def kernel(xf_ref, xq_ref, ids_ref, route_ref, gate_hbm, up_hbm, down_hbm, gc, uc, dc, g_out, u_out, d_out,
           xb, wb, packed, stage, rows_f, spread, raw, down, most, fin, inbox, grad, d_inbox, ws, wd, hid, hid_t, wide, sgu, w2, keep,
           fac, dh, acc, out, theirs, *rest):
    a_in, b_in, c_in = (rest[3 * k:3 * k + 3] for k in range(3))
    l_s, t_s, z_s, x_s, m_s, n_s, d_s, ag_s, ag_r, rs_s, rs_r = rest[9:]
    at = place()
    loads = [pltpu.make_async_copy(down_hbm, down, l_s.at[0])]
    for side, src in enumerate((gate_hbm, up_hbm)):
        for e in range(2):
            lines = pl.ds(192 * side + 96 * e, 96)
            loads.append(pltpu.make_async_copy(src.at[e], raw.at[lines], l_s.at[1 + 2 * side + e]))
    others = friends(at)
    greet_signal(others)
    for cp in loads:
        cp.start()
    pack_rows(xf_ref, xq_ref, ids_ref, route_ref, rows_f, packed)
    greet_wait(others)
    turn_start(at, packed, stage, t_s)
    loads[0].wait()
    stats_local(down, most)
    spread_start(at, most, inbox, m_s)
    turn_end(at, stage, spread, xb, wb, t_s)
    fp, q = (Gather(at, xb, mat, ag_s, ag_r.at[mat]) for mat in range(2))
    fp.spread(0)
    q.spread(0)
    route_start(at, wb, "z", z_s)
    for cp in loads[1:3]:
        cp.wait()
    quant_rows(raw, gc, 0, ws, keep, wide)
    fp.spread_wait(0)
    fp.spread(1)
    q.spread_wait(0)
    q.spread(1)
    route_end(at, wb, "z", z_s)
    route_start(at, wb, "x", x_s)
    spread_end(at, inbox, m_s)
    stats_share(at, most, fin, inbox, n_s)
    for cp in loads[3:5]:
        cp.wait()
    quant_rows(raw, uc, 1, ws, keep, wide)
    fp.spread_wait(1)
    fp.last()
    route_end(at, wb, "x", x_s)
    route_rows(wb, w2)
    fp.last_mid()
    q.spread_wait(1)
    q.last()
    both_wait(inbox.at[1:16], n_s, moved(at, c=1))
    quant_down(down, dc, fin, wd)
    fp.last_near()
    q.last_mid()
    fp.last_far()
    fp.finish()
    for p in range(3):
        teacher(xb, p, raw, w2, hid)
    q.last_near()
    q.last_far()
    q.finish()
    gathers_sent(xb, ag_s, ag_r.at[0], moved(at, c=1))
    red = [Reduce(at, k, acc, out, theirs, a_in, b_in, c_in, xb, rs_s, rs_r) for k in range(CHUNKS)]
    for p in range(3):
        student(xb, p, ws, w2, hid, hid_t, sgu)
    grad[4:8, :] = jnp.zeros((4, D), F32)
    difference(0, 1 - at["c"], hid_t, wd, down, out)
    red[0].swap()
    difference(0, at["c"], hid_t, wd, down, acc)
    difference(1, 1 - at["c"], hid_t, wd, down, out)
    red[1].swap()
    difference(1, at["c"], hid_t, wd, down, acc)
    red[0].first()
    difference(2, 1 - at["c"], hid_t, wd, down, out)
    red[2].swap()
    difference(2, at["c"], hid_t, wd, down, acc)
    red[1].first()
    difference(3, 1 - at["c"], hid_t, wd, down, out)
    red[3].swap()
    difference(3, at["c"], hid_t, wd, down, acc)
    red[2].first()
    red[3].first()
    factors(xb, 0, 0, ws, w2, sgu, fac)
    red[0].first_end()
    factors(xb, 0, 1, ws, w2, sgu, fac)
    red[1].first_end()
    red[0].second_end()
    factors(xb, 1, 0, ws, w2, sgu, fac)
    red[2].first_end()
    red[1].second_end()
    factors(xb, 1, 1, ws, w2, sgu, fac)
    red[3].first_end()
    red[0].third_end()
    red[2].second_end()
    factors(xb, 2, 0, ws, w2, sgu, fac)
    red[1].third_end()
    red[0].fourth_end()
    red[3].second_end()
    factors(xb, 2, 1, ws, w2, sgu, fac)
    red[2].third_end()
    red[1].fourth_end()
    red[0].fifth_end()
    red[3].third_end()
    red[2].fourth_end()
    red[1].fifth_end()
    red[0].done()
    back(0, xb, hid, wd, dc, fin, dh, grad)
    red[3].fourth_end()
    red[2].fifth_end()
    red[1].done()
    back(1, xb, hid, wd, dc, fin, dh, grad)
    red[3].fifth_end()
    red[2].done()
    back(2, xb, hid, wd, dc, fin, dh, grad)
    red[3].done()
    back(3, xb, hid, wd, dc, fin, dh, grad)
    spread_start(at, grad, d_inbox, d_s)
    row_grads(0, fac, dh, keep, g_out)
    row_grads(1, fac, dh, keep, u_out)
    reduces_sent(xb, rs_s, rs_r, moved(at, c=1))
    spread_end(at, d_inbox, d_s)
    _, me = peer(at, 0)
    total = grad[:, unit_cols(me)]
    for n in range(1, 16):
        total = total + d_inbox[n]
    for k in range(2):
        d_out[k] = total[2 * k:2 * k + 2]


SEM = pltpu.SemaphoreType.DMA
VM = pl.BlockSpec(memory_space=pltpu.VMEM)
ANY = pl.BlockSpec(memory_space=pl.ANY)


def sds(shape, dt):
    return jax.ShapeDtypeStruct(shape, dt)


def hand_over(a, b, c, x, y, z):
    x[...] = a[...]
    y[...] = b[...]
    z[...] = c[...]


def on_device(x_fp, x_q, expert_ids, route_weight, gate_weight, up_weight, down_weight, gate_clip, up_clip, down_clip):
    scratch = [((2, 3, 4, 4, 16, D), BF), ((4, 4, 16, 128), BF), ((16, D), BF), ((8, 16, 512), BF), ((16, D), F32),
               ((512, 128), F32), ((384, D), BF), ((2, 96, D), BF), ((8, D), F32), ((8, D), F32), ((16, 8, 256), F32),
               ((8, D), F32), ((16, 8, 256), F32), ((1152, D), BF), ((3, 2, 96, D), BF), ((3, 384, 256), BF), ((3, 256, 384), BF), ((3, 192, 128), F32),
               ((384, 768), F32),
               ((192, 768), F32), ((2, 4, 192, 1), F32), ((4, 192, 768), F32), ((192, 768), F32)]
    scratch += [((CHUNKS, 3, 4, 4, 16, WIDE), BF)] * 3
    scratch += [((CHUNKS, 3) + phase_shape(p, phase), BF) for phase in (2, 1, 1) for p in range(3)]
    outs = (sds((2, 2, 96), F32), sds((2, 2, 96), F32), sds((2, 2, 256), F32))
    made = pl.pallas_call(
        kernel,
        out_shape=outs,
        in_specs=[VM] * 4 + [ANY] * 3 + [VM] * 3,
        out_specs=(VM,) * 3,
        scratch_shapes=[pltpu.VMEM(s, t) for s, t in scratch] + [SEM((5,))] + [SEM((2,))] * 6 + [
            SEM((3,)), SEM((2, 6)), SEM((3,)), SEM((CHUNKS, 7))],
        compiler_params=pltpu.CompilerParams(collective_id=0, has_side_effects=True, vmem_limit_bytes=62 << 20),
    )(x_fp, x_q, expert_ids, route_weight, gate_weight, up_weight, down_weight, gate_clip, up_clip, down_clip)
    return pl.pallas_call(hand_over, out_shape=outs, in_specs=[VM] * 3, out_specs=(VM,) * 3)(*made)


def solution(mesh):
    token = P(("grp", "unit"), None)
    weight = P("grp", "unit", None)
    clip = P(None, "grp", "unit")
    return jax.shard_map(
        on_device,
        mesh=mesh,
        in_specs=(token,) * 4 + (weight,) * 3 + (clip, clip, P(None, "grp", None)),
        out_specs=(clip,) * 3,
        check_vma=False,
    )
```

```python
import jax
import jax.numpy as jnp
from jax import lax
from jax.experimental import pallas as pl
from jax.experimental.pallas import tpu as pltpu
from jax.sharding import PartitionSpec as P

MESH = pl.DeviceIdType.MESH
D = 4096
BF = jnp.bfloat16
F32 = jnp.float32
ORDERS = ("xyz", "yzx", "zxy")
CHUNKS = 4
WIDE = 2048 // CHUNKS


def place():
    g, u = lax.axis_index("grp"), lax.axis_index("unit")
    x, z = lax.div(g, 2), lax.rem(g, 2) * 2 + lax.div(u, 8)
    y, c = lax.rem(lax.div(u, 2), 4), lax.rem(u, 2)
    return dict(x=x, y=y, z=z, c=c)


def device(at):
    return (at["x"] * 2 + lax.div(at["z"], 2), lax.rem(at["z"], 2) * 8 + at["y"] * 2 + at["c"])


def moved(at, **by):
    out = dict(at)
    for axis, step in by.items():
        out[axis] = lax.rem(at[axis] + step, 2 if axis == "c" else 4)
    return out


def remote(src, dst, send, recv, to):
    return pltpu.make_async_remote_copy(
        src_ref=src, dst_ref=dst, send_sem=send, recv_sem=recv, device_id=device(to), device_id_type=MESH)


def columns(y, c, full):
    if full:
        return pl.ds(pl.multiple_of(c * 2048, 2048), 2048)
    return pl.ds(pl.multiple_of(c * 2048 + y * 512, 512), 512)


def rows_of(at, done):
    return [slice(None) if a in done else pl.ds(at[a], 1) for a in "zx"]


def ring_pos(at, part, phase, ahead):
    axis = ORDERS[part][phase]
    return dict(at, **{axis: lax.rem(at[axis] + ahead, 4)})


def ring_step(at, part, phase, n):
    return moved(at, **{ORDERS[part][phase]: n})


class Gather:
    def __init__(self, at, buf, mat, send, recv):
        self.at, self.buf, self.mat = at, buf, mat
        self.send, self.recv = send, recv
        self.partner = moved(at, c=1)

    def block(self, part, phase, ahead, half=None, at=None):
        where = ring_pos(at or self.at, part, phase, ahead)
        done = ORDERS[part][:phase]
        width = 2048 if "y" in done else 512
        base = where["c"] * 2048 + (0 if "y" in done else where["y"] * 512)
        if half is not None:
            width = width // 2
            base = base + half * width
        rows = rows_of(where, done)
        return self.buf.at[self.mat, part, rows[0], rows[1], :, pl.ds(pl.multiple_of(base, width), width)]

    def push(self, ref, send, recv, to):
        remote(ref, ref, self.send.at[send], self.recv.at[recv], to).start()

    def landed(self, ref, recv):
        remote(ref, ref, self.send.at[0], self.recv.at[recv], self.partner).wait_recv()

    def spread(self, phase):
        for n in (2, 1, 3):
            for part in range(3):
                self.push(self.block(part, phase, 0), 0, phase, ring_step(self.at, part, phase, n))

    def spread_wait(self, phase):
        self.landed(self.buf.at[self.mat, :, 0:3, 0:1, :, 0:(512, 2048)[phase]], phase)

    def last(self):
        for swap in (0, 1):
            for part in range(3):
                for side, step in ((0, 1), (1, 3)):
                    self.push(self.block(part, 2, 0, side ^ swap), 1, 2 + swap, ring_step(self.at, part, 2, step))
        for part in range(3):
            self.push(self.block(part, 2, 0), 2, 5, self.partner)

    def last_mid(self):
        self.landed(self.buf.at[self.mat, :, 0:2, 0:1], 2)
        for part in range(3):
            for side, step in ((0, 1), (1, 3)):
                self.push(self.block(part, 2, 4 - step, side), 1, 4, ring_step(self.at, part, 2, step))

    def last_near(self):
        self.landed(self.buf.at[self.mat, :, 0:2, 0:1], 3)
        for part in range(3):
            for step in (1, 3):
                self.push(self.block(part, 2, step), 2, 5, self.partner)

    def last_far(self):
        self.landed(self.buf.at[self.mat, :, 0:2, 0:1], 4)
        for part in range(3):
            self.push(self.block(part, 2, 2), 2, 5, self.partner)

    def finish(self):
        self.landed(self.buf.at[self.mat, :, 0:2], 5)


def gathers_sent(buf, send, recv, to):
    for sem, ref in enumerate((buf.at[0, :, 0:3, 0:2, :, 0:2560], buf.at[0, :, 0:3, :], buf.at[0])):
        remote(ref, ref, send.at[sem], recv.at[0], to).wait_send()


def phase_shape(part, phase):
    done = ORDERS[part][:phase]
    return (4 if "z" in done else 1, 4 if "x" in done else 1, 16, WIDE if "y" in done else WIDE // 4)


class Reduce:
    def __init__(self, at, chunk, acc, out, theirs, a_in, b_in, c_in, buf, send, recv):
        self.at, self.chunk, self.acc, self.out, self.theirs = at, chunk, acc, out, theirs
        self.ins = {2: a_in, 1: b_in, 0: c_in}
        self.buf, self.send, self.recv = buf, send, recv
        self.partner = moved(at, c=1)

    def push(self, src, dst, send, recv, to):
        remote(src, dst, self.send.at[send], self.recv.at[self.chunk, recv], to).start()

    def landed(self, ref, recv):
        remote(ref, ref, self.send.at[0], self.recv.at[self.chunk, recv], self.partner).wait_recv()

    def own(self, part, phase, ahead):
        where = ring_pos(self.at, part, phase, ahead)
        done = ORDERS[part][:phase]
        rows = rows_of(where, done)
        width = WIDE if "y" in done else WIDE // 4
        base = 0 if "y" in done else where["y"] * width
        return (self.chunk, part, rows[0], rows[1], slice(None), pl.ds(pl.multiple_of(base, width), width))

    def whole(self, part, phase):
        done = ORDERS[part][:phase]
        rows = rows_of(self.at, done)
        width = WIDE if "y" in done else WIDE // 4
        base = self.chunk * 2 * WIDE + self.at["c"] * WIDE + (0 if "y" in done else self.at["y"] * width)
        return (0, part, rows[0], rows[1], slice(None), pl.ds(pl.multiple_of(base, width), width))

    def swap(self):
        self.push(self.out.at[self.chunk], self.theirs.at[self.chunk], 0, 0, self.partner)

    def total(self, part, phase, arrived):
        sums = self.acc[self.own(part, phase, 0)].astype(F32)
        for n in range(3):
            sums = sums + self.ins[arrived][part][self.chunk, n].astype(F32)
        return sums

    def hand_on(self, part, phase):
        for n in (2, 1, 3):
            self.push(self.acc.at[self.own(part, phase, n if phase else 0)], self.ins[phase][part].at[self.chunk, n - 1],
                      1 if phase == 2 else 2, 3 - phase, ring_step(self.at, part, phase, n))

    def first(self):
        self.landed(self.theirs.at[self.chunk], 0)

        def rows(n, carry):
            part, z = lax.div(n, 4), lax.rem(n, 4)
            mine = self.acc[self.chunk, part, z].astype(F32) + self.theirs[self.chunk, part, z].astype(F32)
            self.acc[self.chunk, part, z] = mine.astype(BF)
            return carry
        lax.fori_loop(0, 12, rows, 0)
        for part in range(3):
            self.hand_on(part, 2)

    def first_end(self):
        self.landed(self.acc.at[self.chunk, :, 0:3], 1)
        for part in range(3):
            self.acc[self.own(part, 2, 0)] = self.total(part, 2, 2).astype(BF)
            self.hand_on(part, 1)

    def second_end(self):
        self.landed(self.acc.at[self.chunk, :, 0:3, 0:1], 2)
        for part in range(3):
            self.acc[self.own(part, 1, 0)] = self.total(part, 1, 1).astype(BF)
            for n in (2, 1, 3):
                self.push(self.acc.at[self.own(part, 1, 0)], self.ins[0][part].at[self.chunk, n - 1], 2, 3,
                          ring_step(self.at, part, 0, n))

    def third_end(self):
        self.landed(self.acc.at[self.chunk, :, 0:3, 0:1], 3)
        for part in range(3):
            block = self.whole(part, 1)
            self.buf[block] = self.total(part, 1, 0).astype(BF)
            for n in (2, 1, 3):
                self.push(self.buf.at[block], self.buf.at[block], 2, 4, ring_step(self.at, part, 1, n))

    def fourth_end(self):
        self.landed(self.acc.at[self.chunk, :, 0:3, 0:1], 4)
        for n in (2, 1, 3):
            for part in range(3):
                block = self.buf.at[self.whole(part, 2)]
                self.push(block, block, 1, 5, ring_step(self.at, part, 2, n))

    def fifth_end(self):
        self.landed(self.acc.at[self.chunk, :, 0:3], 5)
        base = self.chunk * 2 * WIDE + self.at["c"] * WIDE
        block = self.buf.at[0, :, :, :, :, pl.ds(pl.multiple_of(base, WIDE), WIDE)]
        self.push(block, block, 0, 6, self.partner)

    def done(self):
        self.landed(self.acc.at[self.chunk], 6)


def reduces_sent(buf, send, recv, to):
    for sem, ref in enumerate((buf.at[0], buf.at[0, :, 0:3], buf.at[0, :, 0:3, 0:3, :, 0:2048])):
        remote(ref, ref, send.at[sem], recv.at[0, 0], to).wait_send()


def peer(at, n):
    u = lax.rem(lax.rem(at["z"], 2) * 8 + at["y"] * 2 + at["c"] + n, 16)
    return dict(x=at["x"], z=lax.div(at["z"], 2) * 2 + lax.div(u, 8), y=lax.rem(lax.div(u, 2), 4), c=lax.rem(u, 2)), u


def friends(at):
    out = [peer(at, n)[0] for n in range(1, 16)] + [moved(at, x=n) for n in (1, 2, 3)]
    low = lax.rem(at["z"], 2)
    return out + [dict(at, z=lax.rem(at["z"] - low + n, 4)) for n in (2, 3)]


def greet_signal(others):
    barrier = pltpu.get_barrier_semaphore()
    for to in others:
        pl.semaphore_signal(barrier, inc=1, device_id=device(to), device_id_type=MESH)


def greet_wait(others):
    pl.semaphore_wait(pltpu.get_barrier_semaphore(), len(others))


def pack_rows(xf_ref, xq_ref, ids_ref, route_ref, rows_f, packed):
    lane = lax.broadcasted_iota(jnp.int32, (6, 128), 1)
    base = lax.broadcasted_iota(jnp.int32, (6, 128), 0) * 16
    dense = jnp.zeros((6, 128), F32)
    for k in range(8):
        dense = dense + jnp.where(lane == base + ids_ref[:, k:k + 1], route_ref[:, k:k + 1], 0.0)
    weights = jnp.sum(dense, axis=0, keepdims=True)
    rest = weights - weights.astype(BF).astype(F32)
    rows_f[0:6, :] = xf_ref[...].astype(F32)
    rows_f[8:14, :] = xq_ref[...].astype(F32)
    for n in range(8):
        rows_f[6:7, 512 * n:512 * n + 128] = weights
        rows_f[7:8, 512 * n:512 * n + 128] = rest
    packed[...] = rows_f[...].astype(BF)


def turn_start(at, packed, stage, sems):
    mine = at["c"] * 4 + at["y"]
    for n in (4, 5, 2, 3, 6, 7, 1):
        to = moved(at, y=n // 2, c=n % 2)
        remote(packed.at[:, columns(to["y"], to["c"], False)], stage.at[mine], sems.at[0], sems.at[1], to).start()
    stage[mine] = packed[:, columns(at["y"], at["c"], False)]


def both_wait(ref, sems, to):
    cp = remote(ref, ref, sems.at[0], sems.at[1], to)
    cp.wait_recv()
    cp.wait_send()


def turn_end(at, stage, spread, xb, wb, sems):
    both_wait(stage.at[0:7], sems, moved(at, c=1))
    for j in range(8):
        for q in range(4):
            spread[q * 128 + 16 * j:q * 128 + 16 * j + 16, :] = stage[j, :, 128 * q:128 * q + 128].astype(F32)
    cols = columns(at["y"], at["c"], False)
    for mat in range(2):
        for part in range(3):
            rows = [
                jnp.concatenate(
                    [spread[pl.ds(q * 128 + 8 * mat + 2 * part + r, 8, stride=16), :] for q in range(4)], axis=1)
                for r in range(2)
            ]
            xb[mat, part, at["z"], at["x"], :, cols] = jnp.concatenate(rows, axis=0).astype(BF)
    split = [spread[pl.ds(6 + r, 8, stride=16), :] for r in range(2)]
    wb[at["x"], at["z"]] = jnp.concatenate(split, axis=0).astype(BF)


def route_start(at, wb, axis, sems):
    for n in (2, 1, 3):
        idx = (at["x"], at["z"]) if axis == "z" else (at["x"],)
        remote(wb.at[idx], wb.at[idx], sems.at[0], sems.at[1], moved(at, **{axis: n})).start()


def route_end(at, wb, axis, sems):
    both_wait(wb.at[0, 0:3] if axis == "z" else wb.at[0:3], sems, moved(at, c=1))


def unit_cols(u):
    return pl.ds(pl.multiple_of(u * 256, 256), 256)


def stats_local(down_ref, most):
    for e in range(2):
        w = down_ref[e].astype(F32)
        most[e:e + 1, :] = jnp.max(w, axis=0, keepdims=True)
        most[2 + e:3 + e, :] = -jnp.min(w, axis=0, keepdims=True)
    most[4:8, :] = jnp.zeros((4, D), F32)


def spread_start(at, src, dst, sems):
    for n in range(1, 16):
        to, u = peer(at, n)
        remote(src.at[:, unit_cols(u)], dst.at[n], sems.at[0], sems.at[1], to).start()


def spread_end(at, dst, sems):
    both_wait(dst.at[1:16], sems, moved(at, c=1))


def stats_share(at, most, fin, inbox, sems):
    _, me = peer(at, 0)
    top = most[:, unit_cols(me)]
    for n in range(1, 16):
        top = jnp.maximum(top, inbox[n])
    fin[:, unit_cols(me)] = top
    for n in range(1, 16):
        to, _ = peer(at, n)
        remote(fin.at[:, unit_cols(me)], fin.at[:, unit_cols(me)], sems.at[0], sems.at[1], to).start()


HI = lax.Precision.HIGHEST


def nt(a, b, **kw):
    return lax.dot_general(a, b, (((1,), (1,)), ((), ())), preferred_element_type=F32, **kw)


def tn(a, b, **kw):
    return lax.dot_general(a, b, (((0,), (0,)), ((), ())), preferred_element_type=F32, **kw)


def route_rows(wb, w2):
    g = lax.axis_index("grp")
    both = (wb[:, :, 0:8, :].astype(F32) + wb[:, :, 8:16, :].astype(F32)).reshape(128, 128)
    row8 = lax.broadcasted_iota(jnp.int32, (8, 128), 0)
    lane8 = lax.broadcasted_iota(jnp.int32, (8, 128), 1)
    m = lax.broadcasted_iota(jnp.int32, (128, 256), 0)
    n = lax.broadcasted_iota(jnp.int32, (128, 256), 1)
    home = ((m >> 3) & 3) * 64 + (m >> 5) * 16 + (m & 7)
    for part in range(3):
        total = jnp.zeros((8, 256), F32)
        for r in range(2):
            pick = ((lane8 == (2 * part + r) * 16 + 2 * g + row8) & (row8 < 2)).astype(F32)
            chosen = nt(pick, both, precision=HI)
            move = (n == home + 8 * r).astype(F32)
            total = total + jnp.dot(chosen, move, preferred_element_type=F32, precision=HI)
        w2[0:96, 256 * part:256 * part + 256] = jnp.broadcast_to(total[0:1], (96, 256))
        w2[96:192, 256 * part:256 * part + 256] = jnp.broadcast_to(total[1:2], (96, 256))


def to_column(row):
    n = row.shape[1]
    eye = lax.broadcasted_iota(jnp.int32, (n, n), 0) == lax.broadcasted_iota(jnp.int32, (n, n), 1)
    return jnp.sum(jnp.where(eye, jnp.broadcast_to(row, (n, n)), 0.0), axis=1, keepdims=True)


def to_row(col):
    n = col.shape[0]
    eye = lax.broadcasted_iota(jnp.int32, (n, n), 0) == lax.broadcasted_iota(jnp.int32, (n, n), 1)
    return jnp.sum(jnp.where(eye, jnp.broadcast_to(col, (n, n)), 0.0), axis=0, keepdims=True)


def scales(upper, lower, top, low):
    high_end = jax.nn.sigmoid(upper) * top
    low_end = jax.nn.sigmoid(lower) * low
    step = (high_end - low_end) / 15.0
    zero = jnp.floor(-low_end / step + 0.5)
    return low_end, step, zero


def quantize(w, step, inv, zero):
    v = w * inv
    q = jnp.floor(v + 0.5)
    lev = jnp.clip(q, -zero, 15.0 - zero)
    m = jnp.clip(8.0 - jnp.abs(q + zero - 7.5), 0.0, 1.0)
    return lev * step, lev - m * v, m - 1.0


def quant_rows(w_ref, clip_ref, side, ws, keep, wide):
    base = 192 * side
    for e in range(2):
        keep[side, 0, 96 * e:96 * e + 96, :] = to_column(clip_ref[0, e:e + 1, :])
        keep[side, 1, 96 * e:96 * e + 96, :] = to_column(clip_ref[1, e:e + 1, :])
    for block in range(4):
        lines = pl.ds(base + 48 * block, 48)
        first = w_ref[lines, 0:128].astype(F32)

        def extremes(n, carry):
            top, low = carry
            for k in range(4):
                w = w_ref[lines, pl.ds(pl.multiple_of(n * 512 + 128 * k, 128), 128)].astype(F32)
                top, low = jnp.maximum(top, w), jnp.minimum(low, w)
            return top, low
        top, low = lax.fori_loop(0, 8, extremes, (first, first))
        keep[side, 2, 48 * block:48 * block + 48, :] = jnp.max(top, axis=1, keepdims=True)
        keep[side, 3, 48 * block:48 * block + 48, :] = jnp.min(low, axis=1, keepdims=True)
    _, step, zero = scales(*[keep[side, k] for k in range(4)])
    for k, a in enumerate((step, 1.0 / step, zero)):
        wide[k] = jnp.broadcast_to(a, (192, 128))

    def rows(n, carry):
        here = pl.ds(pl.multiple_of(n * 16, 16), 16)
        step, inv, zero = (jnp.concatenate([wide[k, here, :]] * 4, axis=1) for k in range(3))
        for c in range(8):
            w = w_ref[pl.ds(pl.multiple_of(base + n * 16, 16), 16), 512 * c:512 * c + 512].astype(F32)
            for i, a in enumerate(quantize(w, step, inv, zero)):
                ws[pl.ds(pl.multiple_of(384 * i + base + n * 16, 16), 16), 512 * c:512 * c + 512] = a.astype(BF)
        return carry
    lax.fori_loop(0, 12, rows, 0)


def quant_down(w_ref, clip_ref, most, wd):
    for e in range(2):
        def cols(n, carry):
            c = pl.ds(pl.multiple_of(n * 512, 512), 512)
            _, step, zero = scales(clip_ref[0, e:e + 1, c], clip_ref[1, e:e + 1, c], most[e:e + 1, c], -most[2 + e:3 + e, c])
            inv = 1.0 / step

            def rows(k, carry):
                r = pl.ds(pl.multiple_of(k * 16, 16), 16)
                val, slope, zs = quantize(w_ref[e, r, c].astype(F32), step, inv, zero)
                for i, a in enumerate((val, slope, zs)):
                    wd[i, e, r, c] = a.astype(BF)
                return carry
            return lax.fori_loop(0, 6, rows, carry)
        lax.fori_loop(0, 8, cols, 0)


def silu(v):
    return v * jax.nn.sigmoid(v)


def tokens(xb, mat, part):
    return xb[mat, part].reshape(256, D)


def part_cols(part):
    return pl.ds(256 * part, 256)


def teacher(xb, part, w_ref, w2, hid):
    cols = part_cols(part)
    gu = nt(w_ref[...], tokens(xb, 0, part))
    hid[part, 192:384, :] = (-(silu(gu[0:192]) * gu[192:384] * w2[:, cols])).astype(BF)


def student_half(xb, part, core, ws, sgu, fresh):
    k = pl.ds(pl.multiple_of(core * 2048, 2048), 2048)
    gu = nt(ws[0:384, k], xb[1, part, :, :, :, k].reshape(256, 2048))
    sgu[:, part_cols(part)] = gu if fresh else sgu[:, part_cols(part)] + gu


def student(part, w2, hid, hid_t, sgu):
    cols = part_cols(part)
    hid[part, 0:192, :] = (silu(sgu[0:192, cols]) * sgu[192:384, cols] * w2[:, cols]).astype(BF)
    hid_t[part] = jnp.transpose(hid[part].astype(F32)).astype(BF)


def difference(chunk, core, hid_t, wd, down_ref, dst):
    c = pl.ds(pl.multiple_of(chunk * 2 * WIDE + core * WIDE, WIDE), WIDE)
    w = jnp.concatenate([wd[0, :, :, c].reshape(192, WIDE), down_ref[:, :, c].reshape(192, WIDE)], axis=0)
    made = jnp.dot(hid_t[...].reshape(768, 384), w, preferred_element_type=F32)
    dst[chunk] = made.astype(BF).reshape(3, 4, 4, 16, WIDE)


def factors(xb, part, kind, ws, w2, sgu, fac):
    cols = part_cols(part)
    a = nt(ws[384 + 384 * kind:768 + 384 * kind, :], tokens(xb, 1, part))
    g, u = sgu[0:192, cols], sgu[192:384, cols]
    s = jax.nn.sigmoid(g)
    fac[kind, :, cols] = w2[:, cols] * u * s * (1.0 + g * (1.0 - s)) * a[0:192]
    fac[2 + kind, :, cols] = w2[:, cols] * g * s * a[192:384]


def back(at, chunk, core, xb, hid, wd, clip_ref, most, dh, grad, inbox, sems, fresh):
    c = pl.ds(pl.multiple_of(chunk * 2 * WIDE + core * WIDE, WIDE), WIDE)
    w = wd[0, :, :, c].reshape(192, WIDE)
    dq = jnp.zeros((192, WIDE), F32)
    for part in range(3):
        y = xb[0, part, :, :, :, c].reshape(256, WIDE)
        new = nt(w, y)
        cols = part_cols(part)
        dh[:, cols] = new if fresh else dh[:, cols] + new
        dq = dq + jnp.dot(hid[part, 0:192, :], y, preferred_element_type=F32)
    for e in range(2):
        d = dq[96 * e:96 * e + 96]
        s1 = jnp.sum(d * wd[1, e, :, c].astype(F32), axis=0, keepdims=True)
        s2 = jnp.sum(d * wd[2, e, :, c].astype(F32), axis=0, keepdims=True)
        du, dl = slopes(s1, s2, clip_ref[0, e:e + 1, c], clip_ref[1, e:e + 1, c], most[e:e + 1, c], -most[2 + e:3 + e, c])
        grad[e:e + 1, c] = du
        grad[2 + e:3 + e, c] = dl
    _, me = peer(at, 0)
    for k in range(WIDE // 256):
        u = (chunk * 2 * WIDE + core * WIDE) // 256 + k
        n = lax.rem(u - me + 16, 16)
        to, _ = peer(at, n)

        @pl.when(n != 0)
        def _():
            remote(grad.at[:, unit_cols(u)], inbox.at[n], sems.at[0], sems.at[1], to).start()


def slopes(s1, s2, upper, lower, top, low):
    low_end, step, _ = scales(upper, lower, top, low)
    d_step = s1 + s2 * low_end / step
    d_high = d_step / 15.0
    d_low = -s2 - d_high
    su, sl = jax.nn.sigmoid(upper), jax.nn.sigmoid(lower)
    return d_high * top * su * (1.0 - su), d_low * low * sl * (1.0 - sl)


def row_grads(side, fac, dh, keep, out):
    sums = [jnp.sum(fac[2 * side + k] * dh[...], axis=1, keepdims=True) for k in range(2)]
    du, dl = slopes(sums[0], sums[1], *[keep[side, n] for n in range(4)])
    for e in range(2):
        out[0, e:e + 1, :] = to_row(du[96 * e:96 * e + 96, :])
        out[1, e:e + 1, :] = to_row(dl[96 * e:96 * e + 96, :])


def kernel(xf_ref, xq_ref, ids_ref, route_ref, gate_hbm, up_hbm, down_hbm, gc, uc, dc, g_out, u_out, d_out,
           xb, wb, packed, stage, rows_f, spread, raw, down, most, fin, inbox, grad, d_inbox, ws, wd, hid, hid_t, wide, sgu, w2, keep,
           fac, dh, acc, out, theirs, *rest):
    a_in, b_in, c_in = (rest[3 * k:3 * k + 3] for k in range(3))
    l_s, t_s, z_s, x_s, m_s, n_s, d_s, ag_s, ag_r, rs_s, rs_r = rest[9:]
    at = place()
    loads = [pltpu.make_async_copy(down_hbm, down, l_s.at[0])]
    for side, src in enumerate((gate_hbm, up_hbm)):
        for e in range(2):
            lines = pl.ds(192 * side + 96 * e, 96)
            loads.append(pltpu.make_async_copy(src.at[e], raw.at[lines], l_s.at[1 + 2 * side + e]))
    others = friends(at)
    greet_signal(others)
    for cp in loads:
        cp.start()
    pack_rows(xf_ref, xq_ref, ids_ref, route_ref, rows_f, packed)
    greet_wait(others)
    turn_start(at, packed, stage, t_s)
    loads[0].wait()
    stats_local(down, most)
    spread_start(at, most, inbox, m_s)
    turn_end(at, stage, spread, xb, wb, t_s)
    fp, q = (Gather(at, xb, mat, ag_s, ag_r.at[mat]) for mat in range(2))
    fp.spread(0)
    q.spread(0)
    route_start(at, wb, "z", z_s)
    for cp in loads[1:3]:
        cp.wait()
    quant_rows(raw, gc, 0, ws, keep, wide)
    fp.spread_wait(0)
    fp.spread(1)
    q.spread_wait(0)
    q.spread(1)
    route_end(at, wb, "z", z_s)
    route_start(at, wb, "x", x_s)
    spread_end(at, inbox, m_s)
    stats_share(at, most, fin, inbox, n_s)
    for cp in loads[3:5]:
        cp.wait()
    quant_rows(raw, uc, 1, ws, keep, wide)
    fp.spread_wait(1)
    fp.last()
    route_end(at, wb, "x", x_s)
    route_rows(wb, w2)
    fp.last_mid()
    q.spread_wait(1)
    q.last()
    both_wait(inbox.at[1:16], n_s, moved(at, c=1))
    quant_down(down, dc, fin, wd)
    fp.last_near()
    q.last_mid()
    fp.last_far()
    fp.finish()
    teacher(xb, 0, raw, w2, hid)
    q.last_near()
    teacher(xb, 1, raw, w2, hid)
    teacher(xb, 2, raw, w2, hid)
    q.last_far()
    for p in range(3):
        student_half(xb, p, at["c"], ws, sgu, True)
    q.finish()
    for p in range(3):
        student_half(xb, p, 1 - at["c"], ws, sgu, False)
        student(p, w2, hid, hid_t, sgu)
    gathers_sent(xb, ag_s, ag_r.at[0], moved(at, c=1))
    red = [Reduce(at, k, acc, out, theirs, a_in, b_in, c_in, xb, rs_s, rs_r) for k in range(CHUNKS)]
    grad[4:8, :] = jnp.zeros((4, D), F32)
    difference(0, 1 - at["c"], hid_t, wd, down, out)
    red[0].swap()
    difference(0, at["c"], hid_t, wd, down, acc)
    difference(1, 1 - at["c"], hid_t, wd, down, out)
    red[1].swap()
    difference(1, at["c"], hid_t, wd, down, acc)
    difference(2, 1 - at["c"], hid_t, wd, down, out)
    red[2].swap()
    difference(2, at["c"], hid_t, wd, down, acc)
    red[0].first()
    red[1].first()
    red[2].first()
    difference(3, 1 - at["c"], hid_t, wd, down, out)
    red[3].swap()
    difference(3, at["c"], hid_t, wd, down, acc)
    factors(xb, 0, 0, ws, w2, sgu, fac)
    factors(xb, 0, 1, ws, w2, sgu, fac)
    red[3].first()
    red[0].first_end()
    factors(xb, 1, 0, ws, w2, sgu, fac)
    factors(xb, 1, 1, ws, w2, sgu, fac)
    red[1].first_end()
    factors(xb, 2, 0, ws, w2, sgu, fac)
    red[2].first_end()
    factors(xb, 2, 1, ws, w2, sgu, fac)
    red[3].first_end()
    red[0].second_end()
    red[1].second_end()
    red[2].second_end()
    red[3].second_end()
    red[0].third_end()
    red[1].third_end()
    red[2].third_end()
    red[3].third_end()
    red[0].fourth_end()
    red[1].fourth_end()
    red[2].fourth_end()
    red[3].fourth_end()
    red[0].fifth_end()
    back(at, 0, at["c"], xb, hid, wd, dc, fin, dh, grad, d_inbox, d_s, True)
    red[0].done()
    back(at, 0, 1 - at["c"], xb, hid, wd, dc, fin, dh, grad, d_inbox, d_s, False)
    red[1].fifth_end()
    back(at, 1, at["c"], xb, hid, wd, dc, fin, dh, grad, d_inbox, d_s, False)
    red[1].done()
    back(at, 1, 1 - at["c"], xb, hid, wd, dc, fin, dh, grad, d_inbox, d_s, False)
    red[2].fifth_end()
    back(at, 2, at["c"], xb, hid, wd, dc, fin, dh, grad, d_inbox, d_s, False)
    red[2].done()
    back(at, 2, 1 - at["c"], xb, hid, wd, dc, fin, dh, grad, d_inbox, d_s, False)
    red[3].fifth_end()
    back(at, 3, at["c"], xb, hid, wd, dc, fin, dh, grad, d_inbox, d_s, False)
    red[3].done()
    back(at, 3, 1 - at["c"], xb, hid, wd, dc, fin, dh, grad, d_inbox, d_s, False)
    row_grads(0, fac, dh, keep, g_out)
    row_grads(1, fac, dh, keep, u_out)
    reduces_sent(xb, rs_s, rs_r, moved(at, c=1))
    spread_end(at, d_inbox, d_s)
    _, me = peer(at, 0)
    total = grad[:, unit_cols(me)]
    for n in range(1, 16):
        total = total + d_inbox[n]
    for k in range(2):
        d_out[k] = total[2 * k:2 * k + 2]


SEM = pltpu.SemaphoreType.DMA
VM = pl.BlockSpec(memory_space=pltpu.VMEM)
ANY = pl.BlockSpec(memory_space=pl.ANY)


def sds(shape, dt):
    return jax.ShapeDtypeStruct(shape, dt)


def hand_over(a, b, c, x, y, z):
    x[...] = a[...]
    y[...] = b[...]
    z[...] = c[...]


def on_device(x_fp, x_q, expert_ids, route_weight, gate_weight, up_weight, down_weight, gate_clip, up_clip, down_clip):
    scratch = [((2, 3, 4, 4, 16, D), BF), ((4, 4, 16, 128), BF), ((16, D), BF), ((8, 16, 512), BF), ((16, D), F32),
               ((512, 128), F32), ((384, D), BF), ((2, 96, D), BF), ((8, D), F32), ((8, D), F32), ((16, 8, 256), F32),
               ((8, D), F32), ((16, 8, 256), F32), ((1152, D), BF), ((3, 2, 96, D), BF), ((3, 384, 256), BF), ((3, 256, 384), BF), ((3, 192, 128), F32),
               ((384, 768), F32),
               ((192, 768), F32), ((2, 4, 192, 1), F32), ((4, 192, 768), F32), ((192, 768), F32)]
    scratch += [((CHUNKS, 3, 4, 4, 16, WIDE), BF)] * 3
    scratch += [((CHUNKS, 3) + phase_shape(p, phase), BF) for phase in (2, 1, 1) for p in range(3)]
    outs = (sds((2, 2, 96), F32), sds((2, 2, 96), F32), sds((2, 2, 256), F32))
    made = pl.pallas_call(
        kernel,
        out_shape=outs,
        in_specs=[VM] * 4 + [ANY] * 3 + [VM] * 3,
        out_specs=(VM,) * 3,
        scratch_shapes=[pltpu.VMEM(s, t) for s, t in scratch] + [SEM((5,))] + [SEM((2,))] * 6 + [
            SEM((3,)), SEM((2, 6)), SEM((3,)), SEM((CHUNKS, 7))],
        compiler_params=pltpu.CompilerParams(collective_id=0, has_side_effects=True, vmem_limit_bytes=62 << 20),
    )(x_fp, x_q, expert_ids, route_weight, gate_weight, up_weight, down_weight, gate_clip, up_clip, down_clip)
    return pl.pallas_call(hand_over, out_shape=outs, in_specs=[VM] * 3, out_specs=(VM,) * 3)(*made)


def solution(mesh):
    token = P(("grp", "unit"), None)
    weight = P("grp", "unit", None)
    clip = P(None, "grp", "unit")
    return jax.shard_map(
        on_device,
        mesh=mesh,
        in_specs=(token,) * 4 + (weight,) * 3 + (clip, clip, P(None, "grp", None)),
        out_specs=(clip,) * 3,
        check_vma=False,
    )
```

```python
import jax
import jax.numpy as jnp
from jax import lax
from jax.experimental import pallas as pl
from jax.experimental.pallas import tpu as pltpu
from jax.sharding import PartitionSpec as P

MESH = pl.DeviceIdType.MESH
D = 4096
BF = jnp.bfloat16
F32 = jnp.float32
ORDERS = ("xyz", "yzx", "zxy")
CHUNKS = 4
TWO_WAY = (False, True, True, False)
RING_OUT = (True, True, True, True)
WIDE = 2048 // CHUNKS


def place():
    g, u = lax.axis_index("grp"), lax.axis_index("unit")
    x, z = lax.div(g, 2), lax.rem(g, 2) * 2 + lax.div(u, 8)
    y, c = lax.rem(lax.div(u, 2), 4), lax.rem(u, 2)
    return dict(x=x, y=y, z=z, c=c)


def device(at):
    return (at["x"] * 2 + lax.div(at["z"], 2), lax.rem(at["z"], 2) * 8 + at["y"] * 2 + at["c"])


def moved(at, **by):
    out = dict(at)
    for axis, step in by.items():
        out[axis] = lax.rem(at[axis] + step, 2 if axis == "c" else 4)
    return out


def remote(src, dst, send, recv, to):
    return pltpu.make_async_remote_copy(
        src_ref=src, dst_ref=dst, send_sem=send, recv_sem=recv, device_id=device(to), device_id_type=MESH)


def columns(y, c, full):
    if full:
        return pl.ds(pl.multiple_of(c * 2048, 2048), 2048)
    return pl.ds(pl.multiple_of(c * 2048 + y * 512, 512), 512)


def rows_of(at, done, half=None):
    rows = [slice(None) if a in done else pl.ds(at[a], 1) for a in "zx"]
    if half is not None:
        rows[0 if "z" in done else 1] = pl.ds(2 * half, 2)
    return rows


def ring_pos(at, part, phase, ahead):
    axis = ORDERS[part][phase]
    return dict(at, **{axis: lax.rem(at[axis] + ahead, 4)})


def ring_step(at, part, phase, n):
    return moved(at, **{ORDERS[part][phase]: n})


class Gather:
    def __init__(self, at, buf, mat, send, recv):
        self.at, self.buf, self.mat = at, buf, mat
        self.send, self.recv = send, recv
        self.partner = moved(at, c=1)

    def block(self, part, phase, ahead, half=None, at=None):
        where = ring_pos(at or self.at, part, phase, ahead)
        done = ORDERS[part][:phase]
        width = 2048 if "y" in done else 512
        base = where["c"] * 2048 + (0 if "y" in done else where["y"] * 512)
        if half is not None:
            width = width // 2
            base = base + half * width
        rows = rows_of(where, done)
        return self.buf.at[self.mat, part, rows[0], rows[1], :, pl.ds(pl.multiple_of(base, width), width)]

    def push(self, ref, send, recv, to):
        remote(ref, ref, self.send.at[send], self.recv.at[recv], to).start()

    def landed(self, ref, recv):
        remote(ref, ref, self.send.at[0], self.recv.at[recv], self.partner).wait_recv()

    def spread(self, phase):
        for n in (2, 1, 3):
            for part in range(3):
                self.push(self.block(part, phase, 0), 0, phase, ring_step(self.at, part, phase, n))

    def spread_wait(self, phase):
        self.landed(self.buf.at[self.mat, :, 0:3, 0:1, :, 0:(512, 2048)[phase]], phase)

    def last(self):
        for swap in (0, 1):
            for part in range(3):
                for side, step in ((0, 1), (1, 3)):
                    self.push(self.block(part, 2, 0, side ^ swap), 1, 2 + swap, ring_step(self.at, part, 2, step))
        for part in range(3):
            self.push(self.block(part, 2, 0), 2, 5, self.partner)

    def last_mid(self):
        self.landed(self.buf.at[self.mat, :, 0:2, 0:1], 2)
        for part in range(3):
            for side, step in ((0, 1), (1, 3)):
                self.push(self.block(part, 2, 4 - step, side), 1, 4, ring_step(self.at, part, 2, step))

    def last_near(self):
        self.landed(self.buf.at[self.mat, :, 0:2, 0:1], 3)
        for part in range(3):
            for step in (1, 3):
                self.push(self.block(part, 2, step), 2, 5, self.partner)

    def last_far(self):
        self.landed(self.buf.at[self.mat, :, 0:2, 0:1], 4)
        for part in range(3):
            self.push(self.block(part, 2, 2), 2, 5, self.partner)

    def finish(self):
        self.landed(self.buf.at[self.mat, :, 0:2], 5)


def gathers_sent(buf, send, recv, to):
    for sem, ref in enumerate((buf.at[0, :, 0:3, 0:2, :, 0:2560], buf.at[0, :, 0:3, :], buf.at[0])):
        remote(ref, ref, send.at[sem], recv.at[0], to).wait_send()


def phase_shape(part, phase):
    done = ORDERS[part][:phase]
    return (4 if "z" in done else 1, 4 if "x" in done else 1, 16, WIDE if "y" in done else WIDE // 4)


class Reduce:
    def __init__(self, at, chunk, acc, out, theirs, h_in, a_in, b_in, c_in, buf, send, recv):
        self.two_way, self.ring_out = TWO_WAY[chunk], RING_OUT[chunk]
        self.at, self.chunk, self.acc, self.out, self.theirs = at, chunk, acc, out, theirs
        self.halves, self.ins = h_in, {2: a_in, 1: b_in, 0: c_in}
        self.buf, self.send, self.recv = buf, send, recv
        self.partner = moved(at, c=1)

    def push(self, src, dst, send, recv, to):
        remote(src, dst, self.send.at[send], self.recv.at[self.chunk, recv], to).start()

    def landed(self, ref, recv):
        remote(ref, ref, self.send.at[0], self.recv.at[self.chunk, recv], self.partner).wait_recv()

    def own(self, part, phase, ahead, half=None):
        where = ring_pos(self.at, part, phase, ahead)
        done = ORDERS[part][:phase]
        rows = rows_of(where, done, half)
        width = WIDE if "y" in done else WIDE // 4
        base = 0 if "y" in done else where["y"] * width
        return (self.chunk, part, rows[0], rows[1], slice(None), pl.ds(pl.multiple_of(base, width), width))

    def whole(self, part, phase, ahead=0, half=None):
        where = ring_pos(self.at, part, phase, ahead)
        done = ORDERS[part][:phase]
        rows = rows_of(where, done, half)
        width = WIDE if "y" in done else WIDE // 4
        base = self.chunk * 2 * WIDE + where["c"] * WIDE + (0 if "y" in done else where["y"] * width)
        return (0, part, rows[0], rows[1], slice(None), pl.ds(pl.multiple_of(base, width), width))

    def swap(self):
        self.push(self.out.at[self.chunk], self.theirs.at[self.chunk], 0, 0, self.partner)

    def total(self, part, phase, arrived):
        sums = self.acc[self.own(part, phase, 0)].astype(F32)
        for n in range(2 if arrived == 2 and self.two_way else 3):
            sums = sums + self.ins[arrived][part][self.chunk, n].astype(F32)
        return sums

    def first(self):
        self.landed(self.theirs.at[self.chunk], 0)

        def rows(n, carry):
            part, z = lax.div(n, 4), lax.rem(n, 4)
            mine = self.acc[self.chunk, part, z].astype(F32) + self.theirs[self.chunk, part, z].astype(F32)
            self.acc[self.chunk, part, z] = mine.astype(BF)
            return carry
        lax.fori_loop(0, 12, rows, 0)
        for part in range(3):
            if not self.two_way:
                for n in (2, 1, 3):
                    self.push(self.acc.at[self.own(part, 2, n)], self.ins[2][part].at[self.chunk, n - 1], 1, 2,
                              ring_step(self.at, part, 2, n))
                continue
            for side, step in ((0, 1), (1, 3)):
                self.push(self.acc.at[self.own(part, 2, 2, side)], self.halves[part].at[self.chunk, side], 1, 1,
                          ring_step(self.at, part, 2, step))

    def first_mid(self):
        self.landed(self.acc.at[self.chunk, :, 0:1], 1)
        for part in range(3):
            for side, step in ((0, 1), (1, 3)):
                idx = self.own(part, 2, step, side)
                self.acc[idx] = (self.acc[idx].astype(F32) + self.halves[part][self.chunk, side].astype(F32)).astype(BF)
                self.push(self.acc.at[self.own(part, 2, step)], self.ins[2][part].at[self.chunk, side], 1, 2,
                          ring_step(self.at, part, 2, step))

    def first_end(self):
        self.landed(self.acc.at[self.chunk, :, 0:2 if self.two_way else 3], 2)
        for part in range(3):
            self.acc[self.own(part, 2, 0)] = self.total(part, 2, 2).astype(BF)
            for n in (2, 1, 3):
                self.push(self.acc.at[self.own(part, 1, n)], self.ins[1][part].at[self.chunk, n - 1], 2, 3,
                          ring_step(self.at, part, 1, n))

    def second_end(self):
        self.landed(self.acc.at[self.chunk, :, 0:3, 0:1], 3)
        for part in range(3):
            self.acc[self.own(part, 1, 0)] = self.total(part, 1, 1).astype(BF)
            for n in (2, 1, 3):
                self.push(self.acc.at[self.own(part, 1, 0)], self.ins[0][part].at[self.chunk, n - 1], 2, 4,
                          ring_step(self.at, part, 0, n))

    def third_end(self):
        self.landed(self.acc.at[self.chunk, :, 0:3, 0:1], 4)
        for part in range(3):
            block = self.whole(part, 1)
            self.buf[block] = self.total(part, 1, 0).astype(BF)
            for n in (2, 1, 3):
                self.push(self.buf.at[block], self.buf.at[block], 2, 5, ring_step(self.at, part, 1, n))

    def fourth_end(self):
        self.landed(self.acc.at[self.chunk, :, 0:3, 0:1], 5)
        for part in range(3):
            block = self.buf.at[self.whole(part, 2)]
            for step in (1, 3) if self.ring_out else (2, 1, 3):
                self.push(block, block, 1, 6, ring_step(self.at, part, 2, step))

    def cross(self, aheads):
        for part in range(3):
            for ahead in aheads:
                block = self.buf.at[self.whole(part, 2, ahead)]
                self.push(block, block, 0, 8, self.partner)

    def fifth_mid(self):
        self.landed(self.acc.at[self.chunk, :, 0:2], 6)
        for part in range(3):
            for side, step in ((0, 1), (1, 3)):
                block = self.buf.at[self.whole(part, 2, 4 - step, side)]
                self.push(block, block, 1, 7, ring_step(self.at, part, 2, step))
        self.cross((0, 1, 3))

    def fifth_end(self):
        if self.ring_out:
            self.landed(self.acc.at[self.chunk, :, 0:1], 7)
            self.cross((2,))
        else:
            self.landed(self.acc.at[self.chunk, :, 0:3], 6)
            self.cross((0, 1, 2, 3))

    def done(self):
        self.landed(self.acc.at[self.chunk], 8)


def reduces_sent(buf, send, recv, to):
    for sem, ref in enumerate((buf.at[0], buf.at[0, :, 0:3], buf.at[0, :, 0:3, 0:3, :, 0:2048])):
        remote(ref, ref, send.at[sem], recv.at[0, 0], to).wait_send()


def peer(at, n):
    u = lax.rem(lax.rem(at["z"], 2) * 8 + at["y"] * 2 + at["c"] + n, 16)
    return dict(x=at["x"], z=lax.div(at["z"], 2) * 2 + lax.div(u, 8), y=lax.rem(lax.div(u, 2), 4), c=lax.rem(u, 2)), u


def friends(at):
    out = [peer(at, n)[0] for n in range(1, 16)] + [moved(at, x=n) for n in (1, 2, 3)]
    low = lax.rem(at["z"], 2)
    return out + [dict(at, z=lax.rem(at["z"] - low + n, 4)) for n in (2, 3)]


def greet_signal(others):
    barrier = pltpu.get_barrier_semaphore()
    for to in others:
        pl.semaphore_signal(barrier, inc=1, device_id=device(to), device_id_type=MESH)


def greet_wait(others):
    pl.semaphore_wait(pltpu.get_barrier_semaphore(), len(others))


def pack_rows(xf_ref, xq_ref, ids_ref, route_ref, rows_f, packed):
    lane = lax.broadcasted_iota(jnp.int32, (6, 128), 1)
    base = lax.broadcasted_iota(jnp.int32, (6, 128), 0) * 16
    dense = jnp.zeros((6, 128), F32)
    for k in range(8):
        dense = dense + jnp.where(lane == base + ids_ref[:, k:k + 1], route_ref[:, k:k + 1], 0.0)
    weights = jnp.sum(dense, axis=0, keepdims=True)
    rest = weights - weights.astype(BF).astype(F32)
    rows_f[0:6, :] = xf_ref[...].astype(F32)
    rows_f[8:14, :] = xq_ref[...].astype(F32)
    for n in range(8):
        rows_f[6:7, 512 * n:512 * n + 128] = weights
        rows_f[7:8, 512 * n:512 * n + 128] = rest
    packed[...] = rows_f[...].astype(BF)


def turn_start(at, packed, stage, sems):
    mine = at["c"] * 4 + at["y"]
    for n in (4, 5, 2, 3, 6, 7, 1):
        to = moved(at, y=n // 2, c=n % 2)
        remote(packed.at[:, columns(to["y"], to["c"], False)], stage.at[mine], sems.at[0], sems.at[1], to).start()
    stage[mine] = packed[:, columns(at["y"], at["c"], False)]


def both_wait(ref, sems, to):
    cp = remote(ref, ref, sems.at[0], sems.at[1], to)
    cp.wait_recv()
    cp.wait_send()


def turn_end(at, stage, spread, xb, wb, sems):
    both_wait(stage.at[0:7], sems, moved(at, c=1))
    for j in range(8):
        for q in range(4):
            spread[q * 128 + 16 * j:q * 128 + 16 * j + 16, :] = stage[j, :, 128 * q:128 * q + 128].astype(F32)
    cols = columns(at["y"], at["c"], False)
    for mat in range(2):
        for part in range(3):
            rows = [
                jnp.concatenate(
                    [spread[pl.ds(q * 128 + 8 * mat + 2 * part + r, 8, stride=16), :] for q in range(4)], axis=1)
                for r in range(2)
            ]
            xb[mat, part, at["z"], at["x"], :, cols] = jnp.concatenate(rows, axis=0).astype(BF)
    split = [spread[pl.ds(6 + r, 8, stride=16), :] for r in range(2)]
    wb[at["x"], at["z"]] = jnp.concatenate(split, axis=0).astype(BF)


def route_start(at, wb, axis, sems):
    for n in (2, 1, 3):
        idx = (at["x"], at["z"]) if axis == "z" else (at["x"],)
        remote(wb.at[idx], wb.at[idx], sems.at[0], sems.at[1], moved(at, **{axis: n})).start()


def route_end(at, wb, axis, sems):
    both_wait(wb.at[0, 0:3] if axis == "z" else wb.at[0:3], sems, moved(at, c=1))


def unit_cols(u):
    return pl.ds(pl.multiple_of(u * 256, 256), 256)


def stats_local(down_ref, most):
    for e in range(2):
        w = down_ref[e].astype(F32)
        most[e:e + 1, :] = jnp.max(w, axis=0, keepdims=True)
        most[2 + e:3 + e, :] = -jnp.min(w, axis=0, keepdims=True)
    most[4:8, :] = jnp.zeros((4, D), F32)


def spread_start(at, src, dst, sems):
    for n in range(1, 16):
        to, u = peer(at, n)
        remote(src.at[:, unit_cols(u)], dst.at[n], sems.at[0], sems.at[1], to).start()


def spread_end(at, dst, sems):
    both_wait(dst.at[1:16], sems, moved(at, c=1))


def stats_share(at, most, fin, inbox, sems):
    _, me = peer(at, 0)
    top = most[:, unit_cols(me)]
    for n in range(1, 16):
        top = jnp.maximum(top, inbox[n])
    fin[:, unit_cols(me)] = top
    for n in range(1, 16):
        to, _ = peer(at, n)
        remote(fin.at[:, unit_cols(me)], fin.at[:, unit_cols(me)], sems.at[0], sems.at[1], to).start()


HI = lax.Precision.HIGHEST


def nt(a, b, **kw):
    return lax.dot_general(a, b, (((1,), (1,)), ((), ())), preferred_element_type=F32, **kw)


def tn(a, b, **kw):
    return lax.dot_general(a, b, (((0,), (0,)), ((), ())), preferred_element_type=F32, **kw)


def route_rows(wb, w2):
    g = lax.axis_index("grp")
    both = (wb[:, :, 0:8, :].astype(F32) + wb[:, :, 8:16, :].astype(F32)).reshape(128, 128)
    row8 = lax.broadcasted_iota(jnp.int32, (8, 128), 0)
    lane8 = lax.broadcasted_iota(jnp.int32, (8, 128), 1)
    m = lax.broadcasted_iota(jnp.int32, (128, 256), 0)
    n = lax.broadcasted_iota(jnp.int32, (128, 256), 1)
    home = ((m >> 3) & 3) * 64 + (m >> 5) * 16 + (m & 7)
    for part in range(3):
        total = jnp.zeros((8, 256), F32)
        for r in range(2):
            pick = ((lane8 == (2 * part + r) * 16 + 2 * g + row8) & (row8 < 2)).astype(F32)
            chosen = nt(pick, both, precision=HI)
            move = (n == home + 8 * r).astype(F32)
            total = total + jnp.dot(chosen, move, preferred_element_type=F32, precision=HI)
        w2[0:96, 256 * part:256 * part + 256] = jnp.broadcast_to(total[0:1], (96, 256))
        w2[96:192, 256 * part:256 * part + 256] = jnp.broadcast_to(total[1:2], (96, 256))


def to_column(row):
    n = row.shape[1]
    eye = lax.broadcasted_iota(jnp.int32, (n, n), 0) == lax.broadcasted_iota(jnp.int32, (n, n), 1)
    return jnp.sum(jnp.where(eye, jnp.broadcast_to(row, (n, n)), 0.0), axis=1, keepdims=True)


def to_row(col):
    n = col.shape[0]
    eye = lax.broadcasted_iota(jnp.int32, (n, n), 0) == lax.broadcasted_iota(jnp.int32, (n, n), 1)
    return jnp.sum(jnp.where(eye, jnp.broadcast_to(col, (n, n)), 0.0), axis=0, keepdims=True)


def scales(upper, lower, top, low):
    high_end = jax.nn.sigmoid(upper) * top
    low_end = jax.nn.sigmoid(lower) * low
    step = (high_end - low_end) / 15.0
    zero = jnp.floor(-low_end / step + 0.5)
    return low_end, step, zero


def quantize(w, step, inv, zero):
    v = w * inv
    q = jnp.floor(v + 0.5)
    lev = jnp.clip(q, -zero, 15.0 - zero)
    m = jnp.clip(8.0 - jnp.abs(q + zero - 7.5), 0.0, 1.0)
    return lev * step, lev - m * v, m - 1.0


def quant_rows(w_ref, clip_ref, side, ws, keep, wide):
    base = 192 * side
    for e in range(2):
        keep[side, 0, 96 * e:96 * e + 96, :] = to_column(clip_ref[0, e:e + 1, :])
        keep[side, 1, 96 * e:96 * e + 96, :] = to_column(clip_ref[1, e:e + 1, :])
    for block in range(4):
        lines = pl.ds(base + 48 * block, 48)
        first = w_ref[lines, 0:128].astype(F32)

        def extremes(n, carry):
            top, low = carry
            for k in range(4):
                w = w_ref[lines, pl.ds(pl.multiple_of(n * 512 + 128 * k, 128), 128)].astype(F32)
                top, low = jnp.maximum(top, w), jnp.minimum(low, w)
            return top, low
        top, low = lax.fori_loop(0, 8, extremes, (first, first))
        keep[side, 2, 48 * block:48 * block + 48, :] = jnp.max(top, axis=1, keepdims=True)
        keep[side, 3, 48 * block:48 * block + 48, :] = jnp.min(low, axis=1, keepdims=True)
    _, step, zero = scales(*[keep[side, k] for k in range(4)])
    for k, a in enumerate((step, 1.0 / step, zero)):
        wide[k] = jnp.broadcast_to(a, (192, 128))

    def rows(n, carry):
        here = pl.ds(pl.multiple_of(n * 16, 16), 16)
        step, inv, zero = (jnp.concatenate([wide[k, here, :]] * 4, axis=1) for k in range(3))
        for c in range(8):
            w = w_ref[pl.ds(pl.multiple_of(base + n * 16, 16), 16), 512 * c:512 * c + 512].astype(F32)
            for i, a in enumerate(quantize(w, step, inv, zero)):
                ws[pl.ds(pl.multiple_of(384 * i + base + n * 16, 16), 16), 512 * c:512 * c + 512] = a.astype(BF)
        return carry
    lax.fori_loop(0, 12, rows, 0)


def quant_down(w_ref, clip_ref, most, wd):
    for e in range(2):
        def cols(n, carry):
            c = pl.ds(pl.multiple_of(n * 512, 512), 512)
            _, step, zero = scales(clip_ref[0, e:e + 1, c], clip_ref[1, e:e + 1, c], most[e:e + 1, c], -most[2 + e:3 + e, c])
            inv = 1.0 / step

            def rows(k, carry):
                r = pl.ds(pl.multiple_of(k * 16, 16), 16)
                val, slope, zs = quantize(w_ref[e, r, c].astype(F32), step, inv, zero)
                for i, a in enumerate((val, slope, zs)):
                    wd[i, e, r, c] = a.astype(BF)
                return carry
            return lax.fori_loop(0, 6, rows, carry)
        lax.fori_loop(0, 8, cols, 0)


def silu(v):
    return v * jax.nn.sigmoid(v)


def tokens(xb, mat, part):
    return xb[mat, part].reshape(256, D)


def part_cols(part):
    return pl.ds(256 * part, 256)


def teacher(xb, part, w_ref, w2, hid):
    cols = part_cols(part)
    gu = nt(w_ref[...], tokens(xb, 0, part))
    hid[part, 192:384, :] = (-(silu(gu[0:192]) * gu[192:384] * w2[:, cols])).astype(BF)


def student_half(xb, part, core, ws, sgu, fresh):
    k = pl.ds(pl.multiple_of(core * 2048, 2048), 2048)
    gu = nt(ws[0:384, k], xb[1, part, :, :, :, k].reshape(256, 2048))
    sgu[:, part_cols(part)] = gu if fresh else sgu[:, part_cols(part)] + gu


def student(part, w2, hid, hid_t, sgu):
    cols = part_cols(part)
    hid[part, 0:192, :] = (silu(sgu[0:192, cols]) * sgu[192:384, cols] * w2[:, cols]).astype(BF)
    hid_t[part] = jnp.transpose(hid[part].astype(F32)).astype(BF)


def difference(chunk, core, hid_t, wd, down_ref, dst):
    c = pl.ds(pl.multiple_of(chunk * 2 * WIDE + core * WIDE, WIDE), WIDE)
    w = jnp.concatenate([wd[0, :, :, c].reshape(192, WIDE), down_ref[:, :, c].reshape(192, WIDE)], axis=0)
    made = jnp.dot(hid_t[...].reshape(768, 384), w, preferred_element_type=F32)
    dst[chunk] = made.astype(BF).reshape(3, 4, 4, 16, WIDE)


def factors(xb, part, kind, ws, w2, sgu, fac):
    cols = part_cols(part)
    a = nt(ws[384 + 384 * kind:768 + 384 * kind, :], tokens(xb, 1, part))
    g, u = sgu[0:192, cols], sgu[192:384, cols]
    s = jax.nn.sigmoid(g)
    fac[kind, :, cols] = w2[:, cols] * u * s * (1.0 + g * (1.0 - s)) * a[0:192]
    fac[2 + kind, :, cols] = w2[:, cols] * g * s * a[192:384]


def back(at, chunk, core, xb, hid, wd, clip_ref, most, dh, grad, inbox, sems, fresh):
    c = pl.ds(pl.multiple_of(chunk * 2 * WIDE + core * WIDE, WIDE), WIDE)
    w = wd[0, :, :, c].reshape(192, WIDE)
    dq = jnp.zeros((192, WIDE), F32)
    for part in range(3):
        y = xb[0, part, :, :, :, c].reshape(256, WIDE)
        new = nt(w, y)
        cols = part_cols(part)
        dh[:, cols] = new if fresh else dh[:, cols] + new
        dq = dq + jnp.dot(hid[part, 0:192, :], y, preferred_element_type=F32)
    for e in range(2):
        d = dq[96 * e:96 * e + 96]
        s1 = jnp.sum(d * wd[1, e, :, c].astype(F32), axis=0, keepdims=True)
        s2 = jnp.sum(d * wd[2, e, :, c].astype(F32), axis=0, keepdims=True)
        du, dl = slopes(s1, s2, clip_ref[0, e:e + 1, c], clip_ref[1, e:e + 1, c], most[e:e + 1, c], -most[2 + e:3 + e, c])
        grad[e:e + 1, c] = du
        grad[2 + e:3 + e, c] = dl
    _, me = peer(at, 0)
    for k in range(WIDE // 256):
        u = (chunk * 2 * WIDE + core * WIDE) // 256 + k
        n = lax.rem(u - me + 16, 16)
        to, _ = peer(at, n)

        @pl.when(n != 0)
        def _():
            remote(grad.at[:, unit_cols(u)], inbox.at[n], sems.at[0], sems.at[1], to).start()


def slopes(s1, s2, upper, lower, top, low):
    low_end, step, _ = scales(upper, lower, top, low)
    d_step = s1 + s2 * low_end / step
    d_high = d_step / 15.0
    d_low = -s2 - d_high
    su, sl = jax.nn.sigmoid(upper), jax.nn.sigmoid(lower)
    return d_high * top * su * (1.0 - su), d_low * low * sl * (1.0 - sl)


def row_grads(side, fac, dh, keep, out):
    sums = [jnp.sum(fac[2 * side + k] * dh[...], axis=1, keepdims=True) for k in range(2)]
    du, dl = slopes(sums[0], sums[1], *[keep[side, n] for n in range(4)])
    for e in range(2):
        out[0, e:e + 1, :] = to_row(du[96 * e:96 * e + 96, :])
        out[1, e:e + 1, :] = to_row(dl[96 * e:96 * e + 96, :])


def kernel(xf_ref, xq_ref, ids_ref, route_ref, gate_hbm, up_hbm, down_hbm, gc, uc, dc, g_out, u_out, d_out,
           xb, wb, packed, stage, rows_f, spread, raw, down, most, fin, inbox, grad, d_inbox, ws, wd, hid, hid_t, wide, sgu, w2, keep,
           fac, dh, acc, out, theirs, *rest):
    h_in, a_in, b_in, c_in = (rest[3 * k:3 * k + 3] for k in range(4))
    l_s, t_s, z_s, x_s, m_s, n_s, d_s, ag_s, ag_r, rs_s, rs_r = rest[12:]
    at = place()
    loads = [pltpu.make_async_copy(down_hbm, down, l_s.at[0])]
    for side, src in enumerate((gate_hbm, up_hbm)):
        for e in range(2):
            lines = pl.ds(192 * side + 96 * e, 96)
            loads.append(pltpu.make_async_copy(src.at[e], raw.at[lines], l_s.at[1 + 2 * side + e]))
    others = friends(at)
    greet_signal(others)
    for cp in loads:
        cp.start()
    pack_rows(xf_ref, xq_ref, ids_ref, route_ref, rows_f, packed)
    greet_wait(others)
    turn_start(at, packed, stage, t_s)
    loads[0].wait()
    stats_local(down, most)
    spread_start(at, most, inbox, m_s)
    turn_end(at, stage, spread, xb, wb, t_s)
    fp, q = (Gather(at, xb, mat, ag_s, ag_r.at[mat]) for mat in range(2))
    fp.spread(0)
    q.spread(0)
    route_start(at, wb, "z", z_s)
    for cp in loads[1:3]:
        cp.wait()
    quant_rows(raw, gc, 0, ws, keep, wide)
    fp.spread_wait(0)
    fp.spread(1)
    q.spread_wait(0)
    q.spread(1)
    route_end(at, wb, "z", z_s)
    route_start(at, wb, "x", x_s)
    spread_end(at, inbox, m_s)
    stats_share(at, most, fin, inbox, n_s)
    for cp in loads[3:5]:
        cp.wait()
    quant_rows(raw, uc, 1, ws, keep, wide)
    fp.spread_wait(1)
    fp.last()
    route_end(at, wb, "x", x_s)
    route_rows(wb, w2)
    fp.last_mid()
    q.spread_wait(1)
    q.last()
    both_wait(inbox.at[1:16], n_s, moved(at, c=1))
    quant_down(down, dc, fin, wd)
    fp.last_near()
    q.last_mid()
    fp.last_far()
    fp.finish()
    teacher(xb, 0, raw, w2, hid)
    q.last_near()
    teacher(xb, 1, raw, w2, hid)
    teacher(xb, 2, raw, w2, hid)
    q.last_far()
    for p in range(3):
        student_half(xb, p, at["c"], ws, sgu, True)
    q.finish()
    for p in range(3):
        student_half(xb, p, 1 - at["c"], ws, sgu, False)
        student(p, w2, hid, hid_t, sgu)
    gathers_sent(xb, ag_s, ag_r.at[0], moved(at, c=1))
    red = [Reduce(at, k, acc, out, theirs, h_in, a_in, b_in, c_in, xb, rs_s, rs_r) for k in range(CHUNKS)]
    grad[4:8, :] = jnp.zeros((4, D), F32)
    difference(0, 1 - at["c"], hid_t, wd, down, out)
    red[0].swap()
    difference(0, at["c"], hid_t, wd, down, acc)
    difference(1, 1 - at["c"], hid_t, wd, down, out)
    red[1].swap()
    difference(1, at["c"], hid_t, wd, down, acc)
    difference(2, 1 - at["c"], hid_t, wd, down, out)
    red[2].swap()
    difference(2, at["c"], hid_t, wd, down, acc)
    red[0].first()
    red[1].first()
    red[2].first()
    difference(3, 1 - at["c"], hid_t, wd, down, out)
    red[3].swap()
    difference(3, at["c"], hid_t, wd, down, acc)
    factors(xb, 0, 0, ws, w2, sgu, fac)
    factors(xb, 0, 1, ws, w2, sgu, fac)
    red[3].first()
    factors(xb, 1, 0, ws, w2, sgu, fac)
    red[0].first_end()
    red[1].first_mid()
    red[2].first_mid()
    factors(xb, 1, 1, ws, w2, sgu, fac)
    factors(xb, 2, 0, ws, w2, sgu, fac)
    factors(xb, 2, 1, ws, w2, sgu, fac)
    red[0].second_end()
    red[1].first_end()
    red[3].first_end()
    red[2].first_end()
    red[0].third_end()
    red[1].second_end()
    red[3].second_end()
    red[2].second_end()
    red[0].fourth_end()
    red[1].third_end()
    red[3].third_end()
    red[2].third_end()
    red[0].fifth_mid()
    red[1].fourth_end()
    red[3].fourth_end()
    red[2].fourth_end()
    red[0].fifth_end()
    back(at, 0, at["c"], xb, hid, wd, dc, fin, dh, grad, d_inbox, d_s, True)
    red[1].fifth_mid()
    red[0].done()
    back(at, 0, 1 - at["c"], xb, hid, wd, dc, fin, dh, grad, d_inbox, d_s, False)
    red[3].fifth_mid()
    red[2].fifth_mid()
    red[1].fifth_end()
    back(at, 1, at["c"], xb, hid, wd, dc, fin, dh, grad, d_inbox, d_s, False)
    red[3].fifth_end()
    back(at, 3, at["c"], xb, hid, wd, dc, fin, dh, grad, d_inbox, d_s, False)
    red[1].done()
    back(at, 1, 1 - at["c"], xb, hid, wd, dc, fin, dh, grad, d_inbox, d_s, False)
    red[2].fifth_end()
    back(at, 2, at["c"], xb, hid, wd, dc, fin, dh, grad, d_inbox, d_s, False)
    red[3].done()
    back(at, 3, 1 - at["c"], xb, hid, wd, dc, fin, dh, grad, d_inbox, d_s, False)
    red[2].done()
    back(at, 2, 1 - at["c"], xb, hid, wd, dc, fin, dh, grad, d_inbox, d_s, False)
    row_grads(0, fac, dh, keep, g_out)
    row_grads(1, fac, dh, keep, u_out)
    reduces_sent(xb, rs_s, rs_r, moved(at, c=1))
    spread_end(at, d_inbox, d_s)
    _, me = peer(at, 0)
    total = grad[:, unit_cols(me)]
    for n in range(1, 16):
        total = total + d_inbox[n]
    for k in range(2):
        d_out[k] = total[2 * k:2 * k + 2]


SEM = pltpu.SemaphoreType.DMA
VM = pl.BlockSpec(memory_space=pltpu.VMEM)
ANY = pl.BlockSpec(memory_space=pl.ANY)


def sds(shape, dt):
    return jax.ShapeDtypeStruct(shape, dt)


def hand_over(a, b, c, x, y, z):
    x[...] = a[...]
    y[...] = b[...]
    z[...] = c[...]


def on_device(x_fp, x_q, expert_ids, route_weight, gate_weight, up_weight, down_weight, gate_clip, up_clip, down_clip):
    scratch = [((2, 3, 4, 4, 16, D), BF), ((4, 4, 16, 128), BF), ((16, D), BF), ((8, 16, 512), BF), ((16, D), F32),
               ((512, 128), F32), ((384, D), BF), ((2, 96, D), BF), ((8, D), F32), ((8, D), F32), ((16, 8, 256), F32),
               ((8, D), F32), ((16, 8, 256), F32), ((1152, D), BF), ((3, 2, 96, D), BF), ((3, 384, 256), BF), ((3, 256, 384), BF), ((3, 192, 128), F32),
               ((384, 768), F32),
               ((192, 768), F32), ((2, 4, 192, 1), F32), ((4, 192, 768), F32), ((192, 768), F32)]
    scratch += [((CHUNKS, 3, 4, 4, 16, WIDE), BF)] * 3
    scratch += [((CHUNKS, 2) + shape, BF) for shape in ((1, 2, 16, WIDE), (2, 1, 16, WIDE), (2, 4, 16, WIDE // 4))]
    scratch += [((CHUNKS, 3) + phase_shape(p, 2), BF) for p in range(3)]
    scratch += [((CHUNKS, 3) + phase_shape(p, 1), BF) for phase in range(2) for p in range(3)]
    outs = (sds((2, 2, 96), F32), sds((2, 2, 96), F32), sds((2, 2, 256), F32))
    made = pl.pallas_call(
        kernel,
        out_shape=outs,
        in_specs=[VM] * 4 + [ANY] * 3 + [VM] * 3,
        out_specs=(VM,) * 3,
        scratch_shapes=[pltpu.VMEM(s, t) for s, t in scratch] + [SEM((5,))] + [SEM((2,))] * 6 + [
            SEM((3,)), SEM((2, 6)), SEM((3,)), SEM((CHUNKS, 9))],
        compiler_params=pltpu.CompilerParams(collective_id=0, has_side_effects=True, vmem_limit_bytes=62 << 20),
    )(x_fp, x_q, expert_ids, route_weight, gate_weight, up_weight, down_weight, gate_clip, up_clip, down_clip)
    return pl.pallas_call(hand_over, out_shape=outs, in_specs=[VM] * 3, out_specs=(VM,) * 3)(*made)


def solution(mesh):
    token = P(("grp", "unit"), None)
    weight = P("grp", "unit", None)
    clip = P(None, "grp", "unit")
    return jax.shard_map(
        on_device,
        mesh=mesh,
        in_specs=(token,) * 4 + (weight,) * 3 + (clip, clip, P(None, "grp", None)),
        out_specs=(clip,) * 3,
        check_vma=False,
    )
```

```python
import jax
import jax.numpy as jnp
from jax import lax
from jax.experimental import pallas as pl
from jax.experimental.pallas import tpu as pltpu
from jax.sharding import PartitionSpec as P

MESH = pl.DeviceIdType.MESH
D = 4096
BF = jnp.bfloat16
F32 = jnp.float32
ORDERS = ("xyz", "yzx", "zxy")
CHUNKS = 4
TWO_WAY = (False, True, True, False)
RING_OUT = (True, True, True, True)
WIDE = 2048 // CHUNKS


def place():
    g, u = lax.axis_index("grp"), lax.axis_index("unit")
    x, z = lax.div(g, 2), lax.rem(g, 2) * 2 + lax.div(u, 8)
    y, c = lax.rem(lax.div(u, 2), 4), lax.rem(u, 2)
    return dict(x=x, y=y, z=z, c=c)


def device(at):
    return (at["x"] * 2 + lax.div(at["z"], 2), lax.rem(at["z"], 2) * 8 + at["y"] * 2 + at["c"])


def moved(at, **by):
    out = dict(at)
    for axis, step in by.items():
        out[axis] = lax.rem(at[axis] + step, 2 if axis == "c" else 4)
    return out


def remote(src, dst, send, recv, to):
    return pltpu.make_async_remote_copy(
        src_ref=src, dst_ref=dst, send_sem=send, recv_sem=recv, device_id=device(to), device_id_type=MESH)


def columns(y, c, full):
    if full:
        return pl.ds(pl.multiple_of(c * 2048, 2048), 2048)
    return pl.ds(pl.multiple_of(c * 2048 + y * 512, 512), 512)


def rows_of(at, done, half=None):
    rows = [slice(None) if a in done else pl.ds(at[a], 1) for a in "zx"]
    if half is not None:
        rows[0 if "z" in done else 1] = pl.ds(2 * half, 2)
    return rows


def ring_pos(at, part, phase, ahead):
    axis = ORDERS[part][phase]
    return dict(at, **{axis: lax.rem(at[axis] + ahead, 4)})


def ring_step(at, part, phase, n):
    return moved(at, **{ORDERS[part][phase]: n})


class Gather:
    def __init__(self, at, buf, mat, send, recv):
        self.at, self.buf, self.mat = at, buf, mat
        self.send, self.recv = send, recv
        self.partner = moved(at, c=1)

    def block(self, part, phase, ahead, half=None, at=None):
        where = ring_pos(at or self.at, part, phase, ahead)
        done = ORDERS[part][:phase]
        width = 2048 if "y" in done else 512
        base = where["c"] * 2048 + (0 if "y" in done else where["y"] * 512)
        if half is not None:
            width = width // 2
            base = base + half * width
        rows = rows_of(where, done)
        return self.buf.at[self.mat, part, rows[0], rows[1], :, pl.ds(pl.multiple_of(base, width), width)]

    def push(self, ref, send, recv, to):
        remote(ref, ref, self.send.at[send], self.recv.at[recv], to).start()

    def landed(self, ref, recv):
        remote(ref, ref, self.send.at[0], self.recv.at[recv], self.partner).wait_recv()

    def spread(self, phase):
        for n in (2, 1, 3):
            for part in range(3):
                self.push(self.block(part, phase, 0), 0, phase, ring_step(self.at, part, phase, n))

    def spread_wait(self, phase):
        self.landed(self.buf.at[self.mat, :, 0:3, 0:1, :, 0:(512, 2048)[phase]], phase)

    def last(self):
        for swap in (0, 1):
            for part in range(3):
                for side, step in ((0, 1), (1, 3)):
                    self.push(self.block(part, 2, 0, side ^ swap), 1, 2 + swap, ring_step(self.at, part, 2, step))
        for part in range(3):
            self.push(self.block(part, 2, 0), 2, 5, self.partner)

    def last_mid(self):
        self.landed(self.buf.at[self.mat, :, 0:2, 0:1], 2)
        for part in range(3):
            for side, step in ((0, 1), (1, 3)):
                self.push(self.block(part, 2, 4 - step, side), 1, 4, ring_step(self.at, part, 2, step))

    def last_near(self):
        self.landed(self.buf.at[self.mat, :, 0:2, 0:1], 3)
        for part in range(3):
            for step in (1, 3):
                self.push(self.block(part, 2, step), 2, 5, self.partner)

    def last_far(self):
        self.landed(self.buf.at[self.mat, :, 0:2, 0:1], 4)
        for part in range(3):
            self.push(self.block(part, 2, 2), 2, 5, self.partner)

    def finish(self):
        self.landed(self.buf.at[self.mat, :, 0:2], 5)


def gathers_sent(buf, send, recv, to):
    for sem, ref in enumerate((buf.at[0, :, 0:3, 0:2, :, 0:2560], buf.at[0, :, 0:3, :], buf.at[0])):
        remote(ref, ref, send.at[sem], recv.at[0], to).wait_send()


def phase_shape(part, phase):
    done = ORDERS[part][:phase]
    return (4 if "z" in done else 1, 4 if "x" in done else 1, 16, WIDE if "y" in done else WIDE // 4)


class Reduce:
    def __init__(self, at, chunk, acc, out, theirs, h_in, a_in, b_in, c_in, buf, send, recv):
        self.two_way, self.ring_out = TWO_WAY[chunk], RING_OUT[chunk]
        self.at, self.chunk, self.acc, self.out, self.theirs = at, chunk, acc, out, theirs
        self.halves, self.ins = h_in, {2: a_in, 1: b_in, 0: c_in}
        self.buf, self.send, self.recv = buf, send, recv
        self.partner = moved(at, c=1)

    def push(self, src, dst, send, recv, to):
        remote(src, dst, self.send.at[send], self.recv.at[self.chunk, recv], to).start()

    def landed(self, ref, recv):
        remote(ref, ref, self.send.at[0], self.recv.at[self.chunk, recv], self.partner).wait_recv()

    def own(self, part, phase, ahead, half=None):
        where = ring_pos(self.at, part, phase, ahead)
        done = ORDERS[part][:phase]
        rows = rows_of(where, done, half)
        width = WIDE if "y" in done else WIDE // 4
        base = 0 if "y" in done else where["y"] * width
        return (self.chunk, part, rows[0], rows[1], slice(None), pl.ds(pl.multiple_of(base, width), width))

    def whole(self, part, phase, ahead=0, half=None):
        where = ring_pos(self.at, part, phase, ahead)
        done = ORDERS[part][:phase]
        rows = rows_of(where, done, half)
        width = WIDE if "y" in done else WIDE // 4
        base = self.chunk * 2 * WIDE + where["c"] * WIDE + (0 if "y" in done else where["y"] * width)
        return (0, part, rows[0], rows[1], slice(None), pl.ds(pl.multiple_of(base, width), width))

    def swap(self):
        self.push(self.out.at[self.chunk], self.theirs.at[self.chunk], 0, 0, self.partner)

    def total(self, part, phase, arrived):
        sums = self.acc[self.own(part, phase, 0)].astype(F32)
        for n in range(2 if arrived == 2 and self.two_way else 3):
            sums = sums + self.ins[arrived][part][self.chunk, n].astype(F32)
        return sums

    def first(self):
        self.landed(self.theirs.at[self.chunk], 0)

        def rows(n, carry):
            part, z = lax.div(n, 4), lax.rem(n, 4)
            mine = self.acc[self.chunk, part, z].astype(F32) + self.theirs[self.chunk, part, z].astype(F32)
            self.acc[self.chunk, part, z] = mine.astype(BF)
            return carry
        lax.fori_loop(0, 12, rows, 0)
        for part in range(3):
            if not self.two_way:
                for n in (2, 1, 3):
                    self.push(self.acc.at[self.own(part, 2, n)], self.ins[2][part].at[self.chunk, n - 1], 1, 2,
                              ring_step(self.at, part, 2, n))
                continue
            for side, step in ((0, 1), (1, 3)):
                self.push(self.acc.at[self.own(part, 2, 2, side)], self.halves[part].at[self.chunk, side], 1, 1,
                          ring_step(self.at, part, 2, step))

    def first_mid(self):
        self.landed(self.acc.at[self.chunk, :, 0:1], 1)
        for part in range(3):
            for side, step in ((0, 1), (1, 3)):
                idx = self.own(part, 2, step, side)
                self.acc[idx] = (self.acc[idx].astype(F32) + self.halves[part][self.chunk, side].astype(F32)).astype(BF)
                self.push(self.acc.at[self.own(part, 2, step)], self.ins[2][part].at[self.chunk, side], 1, 2,
                          ring_step(self.at, part, 2, step))

    def first_end(self):
        self.landed(self.acc.at[self.chunk, :, 0:2 if self.two_way else 3], 2)
        for part in range(3):
            self.acc[self.own(part, 2, 0)] = self.total(part, 2, 2).astype(BF)
            for n in (2, 1, 3):
                self.push(self.acc.at[self.own(part, 1, n)], self.ins[1][part].at[self.chunk, n - 1], 2, 3,
                          ring_step(self.at, part, 1, n))

    def second_end(self):
        self.landed(self.acc.at[self.chunk, :, 0:3, 0:1], 3)
        for part in range(3):
            self.acc[self.own(part, 1, 0)] = self.total(part, 1, 1).astype(BF)
            for n in (2, 1, 3):
                self.push(self.acc.at[self.own(part, 1, 0)], self.ins[0][part].at[self.chunk, n - 1], 2, 4,
                          ring_step(self.at, part, 0, n))

    def third_end(self):
        self.landed(self.acc.at[self.chunk, :, 0:3, 0:1], 4)
        for part in range(3):
            block = self.whole(part, 1)
            self.buf[block] = self.total(part, 1, 0).astype(BF)
            for n in (2, 1, 3):
                self.push(self.buf.at[block], self.buf.at[block], 2, 5, ring_step(self.at, part, 1, n))

    def fourth_end(self):
        self.landed(self.acc.at[self.chunk, :, 0:3, 0:1], 5)
        for part in range(3):
            block = self.buf.at[self.whole(part, 2)]
            for step in (1, 3) if self.ring_out else (2, 1, 3):
                self.push(block, block, 1, 6, ring_step(self.at, part, 2, step))

    def cross(self, aheads):
        for part in range(3):
            for ahead in aheads:
                block = self.buf.at[self.whole(part, 2, ahead)]
                self.push(block, block, 0, 8, self.partner)

    def fifth_mid(self):
        self.landed(self.acc.at[self.chunk, :, 0:2], 6)
        for part in range(3):
            for side, step in ((0, 1), (1, 3)):
                block = self.buf.at[self.whole(part, 2, 4 - step, side)]
                self.push(block, block, 1, 7, ring_step(self.at, part, 2, step))
        self.cross((0, 1, 3))

    def fifth_end(self):
        if self.ring_out:
            self.landed(self.acc.at[self.chunk, :, 0:1], 7)
            self.cross((2,))
        else:
            self.landed(self.acc.at[self.chunk, :, 0:3], 6)
            self.cross((0, 1, 2, 3))

    def done(self):
        self.landed(self.acc.at[self.chunk], 8)


def reduces_sent(buf, send, recv, to):
    for sem, ref in enumerate((buf.at[0], buf.at[0, :, 0:3], buf.at[0, :, 0:3, 0:3, :, 0:2048])):
        remote(ref, ref, send.at[sem], recv.at[0, 0], to).wait_send()


def peer(at, n):
    u = lax.rem(lax.rem(at["z"], 2) * 8 + at["y"] * 2 + at["c"] + n, 16)
    return dict(x=at["x"], z=lax.div(at["z"], 2) * 2 + lax.div(u, 8), y=lax.rem(lax.div(u, 2), 4), c=lax.rem(u, 2)), u


def friends(at):
    out = [peer(at, n)[0] for n in range(1, 16)] + [moved(at, x=n) for n in (1, 2, 3)]
    low = lax.rem(at["z"], 2)
    return out + [dict(at, z=lax.rem(at["z"] - low + n, 4)) for n in (2, 3)]


def greet_signal(others):
    barrier = pltpu.get_barrier_semaphore()
    for to in others:
        pl.semaphore_signal(barrier, inc=1, device_id=device(to), device_id_type=MESH)


def greet_wait(others):
    pl.semaphore_wait(pltpu.get_barrier_semaphore(), len(others))


def pack_rows(xf_ref, xq_ref, ids_ref, route_ref, rows_f, packed):
    lane = lax.broadcasted_iota(jnp.int32, (6, 128), 1)
    base = lax.broadcasted_iota(jnp.int32, (6, 128), 0) * 16
    dense = jnp.zeros((6, 128), F32)
    for k in range(8):
        dense = dense + jnp.where(lane == base + ids_ref[:, k:k + 1], route_ref[:, k:k + 1], 0.0)
    weights = jnp.sum(dense, axis=0, keepdims=True)
    rest = weights - weights.astype(BF).astype(F32)
    rows_f[0:6, :] = xf_ref[...].astype(F32)
    rows_f[8:14, :] = xq_ref[...].astype(F32)
    for n in range(8):
        rows_f[6:7, 512 * n:512 * n + 128] = weights
        rows_f[7:8, 512 * n:512 * n + 128] = rest
    packed[...] = rows_f[...].astype(BF)


def turn_start(at, packed, stage, sems):
    mine = at["c"] * 4 + at["y"]
    for n in (4, 5, 2, 3, 6, 7, 1):
        to = moved(at, y=n // 2, c=n % 2)
        remote(packed.at[:, columns(to["y"], to["c"], False)], stage.at[mine], sems.at[0], sems.at[1], to).start()
    stage[mine] = packed[:, columns(at["y"], at["c"], False)]


def both_wait(ref, sems, to):
    cp = remote(ref, ref, sems.at[0], sems.at[1], to)
    cp.wait_recv()
    cp.wait_send()


def turn_end(at, stage, spread, xb, wb, sems):
    both_wait(stage.at[0:7], sems, moved(at, c=1))
    for j in range(8):
        for q in range(4):
            spread[q * 128 + 16 * j:q * 128 + 16 * j + 16, :] = stage[j, :, 128 * q:128 * q + 128].astype(F32)
    cols = columns(at["y"], at["c"], False)
    for mat in range(2):
        for part in range(3):
            rows = [
                jnp.concatenate(
                    [spread[pl.ds(q * 128 + 8 * mat + 2 * part + r, 8, stride=16), :] for q in range(4)], axis=1)
                for r in range(2)
            ]
            xb[mat, part, at["z"], at["x"], :, cols] = jnp.concatenate(rows, axis=0).astype(BF)
    split = [spread[pl.ds(6 + r, 8, stride=16), :] for r in range(2)]
    wb[at["x"], at["z"]] = jnp.concatenate(split, axis=0).astype(BF)


def route_start(at, wb, axis, sems):
    for n in (2, 1, 3):
        idx = (at["x"], at["z"]) if axis == "z" else (at["x"],)
        remote(wb.at[idx], wb.at[idx], sems.at[0], sems.at[1], moved(at, **{axis: n})).start()


def route_end(at, wb, axis, sems):
    both_wait(wb.at[0, 0:3] if axis == "z" else wb.at[0:3], sems, moved(at, c=1))


def unit_cols(u):
    return pl.ds(pl.multiple_of(u * 256, 256), 256)


def stats_local(down_ref, most):
    for e in range(2):
        w = down_ref[e].astype(F32)
        most[e:e + 1, :] = jnp.max(w, axis=0, keepdims=True)
        most[2 + e:3 + e, :] = -jnp.min(w, axis=0, keepdims=True)
    most[4:8, :] = jnp.zeros((4, D), F32)


def spread_start(at, src, dst, sems):
    for n in range(1, 16):
        to, u = peer(at, n)
        remote(src.at[:, unit_cols(u)], dst.at[n], sems.at[0], sems.at[1], to).start()


def spread_end(at, dst, sems):
    both_wait(dst.at[1:16], sems, moved(at, c=1))


def stats_share(at, most, fin, inbox, sems):
    _, me = peer(at, 0)
    top = most[:, unit_cols(me)]
    for n in range(1, 16):
        top = jnp.maximum(top, inbox[n])
    fin[:, unit_cols(me)] = top
    for n in range(1, 16):
        to, _ = peer(at, n)
        remote(fin.at[:, unit_cols(me)], fin.at[:, unit_cols(me)], sems.at[0], sems.at[1], to).start()


HI = lax.Precision.HIGHEST


def nt(a, b, **kw):
    return lax.dot_general(a, b, (((1,), (1,)), ((), ())), preferred_element_type=F32, **kw)


def tn(a, b, **kw):
    return lax.dot_general(a, b, (((0,), (0,)), ((), ())), preferred_element_type=F32, **kw)


def route_rows(wb, w2):
    g = lax.axis_index("grp")
    both = (wb[:, :, 0:8, :].astype(F32) + wb[:, :, 8:16, :].astype(F32)).reshape(128, 128)
    row8 = lax.broadcasted_iota(jnp.int32, (8, 128), 0)
    lane8 = lax.broadcasted_iota(jnp.int32, (8, 128), 1)
    m = lax.broadcasted_iota(jnp.int32, (128, 256), 0)
    n = lax.broadcasted_iota(jnp.int32, (128, 256), 1)
    home = ((m >> 3) & 3) * 64 + (m >> 5) * 16 + (m & 7)
    for part in range(3):
        total = jnp.zeros((8, 256), F32)
        for r in range(2):
            pick = ((lane8 == (2 * part + r) * 16 + 2 * g + row8) & (row8 < 2)).astype(F32)
            chosen = nt(pick, both, precision=HI)
            move = (n == home + 8 * r).astype(F32)
            total = total + jnp.dot(chosen, move, preferred_element_type=F32, precision=HI)
        w2[0:96, 256 * part:256 * part + 256] = jnp.broadcast_to(total[0:1], (96, 256))
        w2[96:192, 256 * part:256 * part + 256] = jnp.broadcast_to(total[1:2], (96, 256))


def to_column(row):
    n = row.shape[1]
    eye = lax.broadcasted_iota(jnp.int32, (n, n), 0) == lax.broadcasted_iota(jnp.int32, (n, n), 1)
    return jnp.sum(jnp.where(eye, jnp.broadcast_to(row, (n, n)), 0.0), axis=1, keepdims=True)


def to_row(col):
    n = col.shape[0]
    eye = lax.broadcasted_iota(jnp.int32, (n, n), 0) == lax.broadcasted_iota(jnp.int32, (n, n), 1)
    return jnp.sum(jnp.where(eye, jnp.broadcast_to(col, (n, n)), 0.0), axis=0, keepdims=True)


def scales(upper, lower, top, low):
    high_end = jax.nn.sigmoid(upper) * top
    low_end = jax.nn.sigmoid(lower) * low
    step = (high_end - low_end) / 15.0
    zero = jnp.floor(-low_end / step + 0.5)
    return low_end, step, zero


def quantize(w, step, inv, zero):
    v = w * inv
    q = jnp.floor(v + 0.5)
    lev = jnp.clip(q, -zero, 15.0 - zero)
    m = jnp.clip(8.0 - jnp.abs(q + zero - 7.5), 0.0, 1.0)
    return lev * step, lev - m * v, m - 1.0


def quant_rows(w_ref, clip_ref, side, ws, keep, wide):
    base = 192 * side
    for e in range(2):
        keep[side, 0, 96 * e:96 * e + 96, :] = to_column(clip_ref[0, e:e + 1, :])
        keep[side, 1, 96 * e:96 * e + 96, :] = to_column(clip_ref[1, e:e + 1, :])
    for block in range(4):
        lines = pl.ds(base + 48 * block, 48)
        first = w_ref[lines, 0:128].astype(F32)

        def extremes(n, carry):
            top, low = carry
            for k in range(4):
                w = w_ref[lines, pl.ds(pl.multiple_of(n * 512 + 128 * k, 128), 128)].astype(F32)
                top, low = jnp.maximum(top, w), jnp.minimum(low, w)
            return top, low
        top, low = lax.fori_loop(0, 8, extremes, (first, first))
        keep[side, 2, 48 * block:48 * block + 48, :] = jnp.max(top, axis=1, keepdims=True)
        keep[side, 3, 48 * block:48 * block + 48, :] = jnp.min(low, axis=1, keepdims=True)
    _, step, zero = scales(*[keep[side, k] for k in range(4)])
    for k, a in enumerate((step, 1.0 / step, zero)):
        wide[k] = jnp.broadcast_to(a, (192, 128))

    def rows(n, carry):
        here = pl.ds(pl.multiple_of(n * 16, 16), 16)
        step, inv, zero = (jnp.concatenate([wide[k, here, :]] * 4, axis=1) for k in range(3))
        for c in range(8):
            w = w_ref[pl.ds(pl.multiple_of(base + n * 16, 16), 16), 512 * c:512 * c + 512].astype(F32)
            for i, a in enumerate(quantize(w, step, inv, zero)):
                ws[pl.ds(pl.multiple_of(384 * i + base + n * 16, 16), 16), 512 * c:512 * c + 512] = a.astype(BF)
        return carry
    lax.fori_loop(0, 12, rows, 0)


def quant_down(w_ref, clip_ref, most, wd):
    for e in range(2):
        def cols(n, carry):
            c = pl.ds(pl.multiple_of(n * 512, 512), 512)
            _, step, zero = scales(clip_ref[0, e:e + 1, c], clip_ref[1, e:e + 1, c], most[e:e + 1, c], -most[2 + e:3 + e, c])
            inv = 1.0 / step

            def rows(k, carry):
                r = pl.ds(pl.multiple_of(k * 16, 16), 16)
                val, slope, zs = quantize(w_ref[e, r, c].astype(F32), step, inv, zero)
                for i, a in enumerate((val, slope, zs)):
                    wd[i, e, r, c] = a.astype(BF)
                return carry
            return lax.fori_loop(0, 6, rows, carry)
        lax.fori_loop(0, 8, cols, 0)


def silu(v):
    return v * jax.nn.sigmoid(v)


def tokens(xb, mat, part):
    return xb[mat, part].reshape(256, D)


def part_cols(part):
    return pl.ds(256 * part, 256)


def teacher(xb, part, w_ref, w2, hid):
    cols = part_cols(part)
    gu = nt(w_ref[...], tokens(xb, 0, part))
    hid[part, 192:384, :] = (-(silu(gu[0:192]) * gu[192:384] * w2[:, cols])).astype(BF)


def student_half(xb, part, core, ws, sgu, fresh):
    k = pl.ds(pl.multiple_of(core * 2048, 2048), 2048)
    gu = nt(ws[0:384, k], xb[1, part, :, :, :, k].reshape(256, 2048))
    sgu[:, part_cols(part)] = gu if fresh else sgu[:, part_cols(part)] + gu


def student(part, w2, hid, hid_t, sgu):
    cols = part_cols(part)
    hid[part, 0:192, :] = (silu(sgu[0:192, cols]) * sgu[192:384, cols] * w2[:, cols]).astype(BF)
    hid_t[part] = jnp.transpose(hid[part].astype(F32)).astype(BF)


def difference(chunk, core, hid_t, wd, down_ref, dst):
    c = pl.ds(pl.multiple_of(chunk * 2 * WIDE + core * WIDE, WIDE), WIDE)
    w = jnp.concatenate([wd[0, :, :, c].reshape(192, WIDE), down_ref[:, :, c].reshape(192, WIDE)], axis=0)
    made = jnp.dot(hid_t[...].reshape(768, 384), w, preferred_element_type=F32)
    dst[chunk] = made.astype(BF).reshape(3, 4, 4, 16, WIDE)


def factors(xb, part, kind, ws, w2, sgu, fac):
    cols = part_cols(part)
    a = nt(ws[384 + 384 * kind:768 + 384 * kind, :], tokens(xb, 1, part))
    g, u = sgu[0:192, cols], sgu[192:384, cols]
    s = jax.nn.sigmoid(g)
    fac[kind, :, cols] = w2[:, cols] * u * s * (1.0 + g * (1.0 - s)) * a[0:192]
    fac[2 + kind, :, cols] = w2[:, cols] * g * s * a[192:384]


def back(at, chunk, core, xb, hid, wd, clip_ref, most, dh, grad, inbox, sems, fresh):
    c = pl.ds(pl.multiple_of(chunk * 2 * WIDE + core * WIDE, WIDE), WIDE)
    w = wd[0, :, :, c].reshape(192, WIDE)
    dq = jnp.zeros((192, WIDE), F32)
    for part in range(3):
        y = xb[0, part, :, :, :, c].reshape(256, WIDE)
        new = nt(w, y)
        cols = part_cols(part)
        dh[:, cols] = new if fresh else dh[:, cols] + new
        dq = dq + jnp.dot(hid[part, 0:192, :], y, preferred_element_type=F32)
    for e in range(2):
        d = dq[96 * e:96 * e + 96]
        s1 = jnp.sum(d * wd[1, e, :, c].astype(F32), axis=0, keepdims=True)
        s2 = jnp.sum(d * wd[2, e, :, c].astype(F32), axis=0, keepdims=True)
        du, dl = slopes(s1, s2, clip_ref[0, e:e + 1, c], clip_ref[1, e:e + 1, c], most[e:e + 1, c], -most[2 + e:3 + e, c])
        grad[e:e + 1, c] = du
        grad[2 + e:3 + e, c] = dl
    _, me = peer(at, 0)
    for k in range(WIDE // 256):
        u = (chunk * 2 * WIDE + core * WIDE) // 256 + k
        n = lax.rem(u - me + 16, 16)
        to, _ = peer(at, n)

        @pl.when(n != 0)
        def _():
            remote(grad.at[:, unit_cols(u)], inbox.at[n], sems.at[0], sems.at[1], to).start()


def slopes(s1, s2, upper, lower, top, low):
    low_end, step, _ = scales(upper, lower, top, low)
    d_step = s1 + s2 * low_end / step
    d_high = d_step / 15.0
    d_low = -s2 - d_high
    su, sl = jax.nn.sigmoid(upper), jax.nn.sigmoid(lower)
    return d_high * top * su * (1.0 - su), d_low * low * sl * (1.0 - sl)


def row_grads(side, fac, dh, keep, out):
    sums = [jnp.sum(fac[2 * side + k] * dh[...], axis=1, keepdims=True) for k in range(2)]
    du, dl = slopes(sums[0], sums[1], *[keep[side, n] for n in range(4)])
    for e in range(2):
        out[0, e:e + 1, :] = to_row(du[96 * e:96 * e + 96, :])
        out[1, e:e + 1, :] = to_row(dl[96 * e:96 * e + 96, :])


def kernel(xf_ref, xq_ref, ids_ref, route_ref, gate_hbm, up_hbm, down_hbm, gc, uc, dc, g_out, u_out, d_out,
           xb, wb, packed, stage, rows_f, spread, raw, down, most, fin, inbox, grad, d_inbox, ws, wd, hid, hid_t, wide, sgu, w2, keep,
           fac, dh, acc, out, theirs, *rest):
    h_in, a_in, b_in, c_in = (rest[3 * k:3 * k + 3] for k in range(4))
    l_s, t_s, z_s, x_s, m_s, n_s, d_s, ag_s, ag_r, rs_s, rs_r = rest[12:]
    at = place()
    loads = [pltpu.make_async_copy(down_hbm, down, l_s.at[0])]
    for side, src in enumerate((gate_hbm, up_hbm)):
        for e in range(2):
            lines = pl.ds(192 * side + 96 * e, 96)
            loads.append(pltpu.make_async_copy(src.at[e], raw.at[lines], l_s.at[1 + 2 * side + e]))
    others = friends(at)
    greet_signal(others)
    for cp in loads:
        cp.start()
    pack_rows(xf_ref, xq_ref, ids_ref, route_ref, rows_f, packed)
    greet_wait(others)
    turn_start(at, packed, stage, t_s)
    loads[0].wait()
    stats_local(down, most)
    spread_start(at, most, inbox, m_s)
    turn_end(at, stage, spread, xb, wb, t_s)
    fp, q = (Gather(at, xb, mat, ag_s, ag_r.at[mat]) for mat in range(2))
    fp.spread(0)
    q.spread(0)
    route_start(at, wb, "z", z_s)
    for cp in loads[1:3]:
        cp.wait()
    quant_rows(raw, gc, 0, ws, keep, wide)
    fp.spread_wait(0)
    fp.spread(1)
    q.spread_wait(0)
    q.spread(1)
    route_end(at, wb, "z", z_s)
    route_start(at, wb, "x", x_s)
    spread_end(at, inbox, m_s)
    stats_share(at, most, fin, inbox, n_s)
    for cp in loads[3:5]:
        cp.wait()
    quant_rows(raw, uc, 1, ws, keep, wide)
    fp.spread_wait(1)
    fp.last()
    route_end(at, wb, "x", x_s)
    route_rows(wb, w2)
    fp.last_mid()
    q.spread_wait(1)
    q.last()
    both_wait(inbox.at[1:16], n_s, moved(at, c=1))
    quant_down(down, dc, fin, wd)
    fp.last_near()
    q.last_mid()
    fp.last_far()
    fp.finish()
    teacher(xb, 0, raw, w2, hid)
    q.last_near()
    teacher(xb, 1, raw, w2, hid)
    q.last_far()
    teacher(xb, 2, raw, w2, hid)
    for p in range(3):
        student_half(xb, p, at["c"], ws, sgu, True)
    q.finish()
    for p in range(3):
        student_half(xb, p, 1 - at["c"], ws, sgu, False)
        student(p, w2, hid, hid_t, sgu)
    gathers_sent(xb, ag_s, ag_r.at[0], moved(at, c=1))
    red = [Reduce(at, k, acc, out, theirs, h_in, a_in, b_in, c_in, xb, rs_s, rs_r) for k in range(CHUNKS)]
    grad[4:8, :] = jnp.zeros((4, D), F32)
    difference(0, 1 - at["c"], hid_t, wd, down, out)
    red[0].swap()
    difference(0, at["c"], hid_t, wd, down, acc)
    difference(1, 1 - at["c"], hid_t, wd, down, out)
    red[1].swap()
    difference(1, at["c"], hid_t, wd, down, acc)
    difference(2, 1 - at["c"], hid_t, wd, down, out)
    red[2].swap()
    difference(2, at["c"], hid_t, wd, down, acc)
    red[0].first()
    red[1].first()
    red[2].first()
    difference(3, 1 - at["c"], hid_t, wd, down, out)
    red[3].swap()
    difference(3, at["c"], hid_t, wd, down, acc)
    factors(xb, 0, 0, ws, w2, sgu, fac)
    factors(xb, 0, 1, ws, w2, sgu, fac)
    red[3].first()
    factors(xb, 1, 0, ws, w2, sgu, fac)
    red[0].first_end()
    red[1].first_mid()
    red[2].first_mid()
    factors(xb, 1, 1, ws, w2, sgu, fac)
    factors(xb, 2, 0, ws, w2, sgu, fac)
    factors(xb, 2, 1, ws, w2, sgu, fac)
    red[0].second_end()
    red[1].first_end()
    red[3].first_end()
    red[2].first_end()
    red[0].third_end()
    red[1].second_end()
    red[3].second_end()
    red[2].second_end()
    red[0].fourth_end()
    red[1].third_end()
    red[3].third_end()
    red[2].third_end()
    red[0].fifth_mid()
    red[1].fourth_end()
    red[3].fourth_end()
    red[2].fourth_end()
    red[0].fifth_end()
    back(at, 0, at["c"], xb, hid, wd, dc, fin, dh, grad, d_inbox, d_s, True)
    red[1].fifth_mid()
    red[0].done()
    back(at, 0, 1 - at["c"], xb, hid, wd, dc, fin, dh, grad, d_inbox, d_s, False)
    red[3].fifth_mid()
    red[2].fifth_mid()
    red[1].fifth_end()
    back(at, 1, at["c"], xb, hid, wd, dc, fin, dh, grad, d_inbox, d_s, False)
    red[3].fifth_end()
    back(at, 3, at["c"], xb, hid, wd, dc, fin, dh, grad, d_inbox, d_s, False)
    red[1].done()
    back(at, 1, 1 - at["c"], xb, hid, wd, dc, fin, dh, grad, d_inbox, d_s, False)
    red[2].fifth_end()
    back(at, 2, at["c"], xb, hid, wd, dc, fin, dh, grad, d_inbox, d_s, False)
    red[3].done()
    back(at, 3, 1 - at["c"], xb, hid, wd, dc, fin, dh, grad, d_inbox, d_s, False)
    red[2].done()
    back(at, 2, 1 - at["c"], xb, hid, wd, dc, fin, dh, grad, d_inbox, d_s, False)
    row_grads(0, fac, dh, keep, g_out)
    row_grads(1, fac, dh, keep, u_out)
    reduces_sent(xb, rs_s, rs_r, moved(at, c=1))
    spread_end(at, d_inbox, d_s)
    _, me = peer(at, 0)
    total = grad[:, unit_cols(me)]
    for n in range(1, 16):
        total = total + d_inbox[n]
    for k in range(2):
        d_out[k] = total[2 * k:2 * k + 2]


SEM = pltpu.SemaphoreType.DMA
VM = pl.BlockSpec(memory_space=pltpu.VMEM)
ANY = pl.BlockSpec(memory_space=pl.ANY)


def sds(shape, dt):
    return jax.ShapeDtypeStruct(shape, dt)


def hand_over(a, b, c, x, y, z):
    x[...] = a[...]
    y[...] = b[...]
    z[...] = c[...]


def on_device(x_fp, x_q, expert_ids, route_weight, gate_weight, up_weight, down_weight, gate_clip, up_clip, down_clip):
    scratch = [((2, 3, 4, 4, 16, D), BF), ((4, 4, 16, 128), BF), ((16, D), BF), ((8, 16, 512), BF), ((16, D), F32),
               ((512, 128), F32), ((384, D), BF), ((2, 96, D), BF), ((8, D), F32), ((8, D), F32), ((16, 8, 256), F32),
               ((8, D), F32), ((16, 8, 256), F32), ((1152, D), BF), ((3, 2, 96, D), BF), ((3, 384, 256), BF), ((3, 256, 384), BF), ((3, 192, 128), F32),
               ((384, 768), F32),
               ((192, 768), F32), ((2, 4, 192, 1), F32), ((4, 192, 768), F32), ((192, 768), F32)]
    scratch += [((CHUNKS, 3, 4, 4, 16, WIDE), BF)] * 3
    scratch += [((CHUNKS, 2) + shape, BF) for shape in ((1, 2, 16, WIDE), (2, 1, 16, WIDE), (2, 4, 16, WIDE // 4))]
    scratch += [((CHUNKS, 3) + phase_shape(p, 2), BF) for p in range(3)]
    scratch += [((CHUNKS, 3) + phase_shape(p, 1), BF) for phase in range(2) for p in range(3)]
    outs = (sds((2, 2, 96), F32), sds((2, 2, 96), F32), sds((2, 2, 256), F32))
    made = pl.pallas_call(
        kernel,
        out_shape=outs,
        in_specs=[VM] * 4 + [ANY] * 3 + [VM] * 3,
        out_specs=(VM,) * 3,
        scratch_shapes=[pltpu.VMEM(s, t) for s, t in scratch] + [SEM((5,))] + [SEM((2,))] * 6 + [
            SEM((3,)), SEM((2, 6)), SEM((3,)), SEM((CHUNKS, 9))],
        compiler_params=pltpu.CompilerParams(collective_id=0, has_side_effects=True, vmem_limit_bytes=62 << 20),
    )(x_fp, x_q, expert_ids, route_weight, gate_weight, up_weight, down_weight, gate_clip, up_clip, down_clip)
    return pl.pallas_call(hand_over, out_shape=outs, in_specs=[VM] * 3, out_specs=(VM,) * 3)(*made)


def solution(mesh):
    token = P(("grp", "unit"), None)
    weight = P("grp", "unit", None)
    clip = P(None, "grp", "unit")
    return jax.shard_map(
        on_device,
        mesh=mesh,
        in_specs=(token,) * 4 + (weight,) * 3 + (clip, clip, P(None, "grp", None)),
        out_specs=(clip,) * 3,
        check_vma=False,
    )
```
